32 devices in a mesh: groups: 2 (over y), latent: 4 (over z), token: 2 (over x), layer: 2 (over core).
Axes of the slice: x: 2, y: 2, z: 4, core: 2. Of those that a mesh axis runs over, the one named last changes fastest.
Arguments:
- inputs: bfloat16 [2, 1536, 4096], P('layer', ('groups', 'token')), parts along dimension 1, may hold values from -1800 to 1800
- targets: bfloat16 [2, 1536, 4096], P('layer', ('groups', 'token'), 'latent'), parts along dimension 1, may hold values from -90 to 90
- enc_weight: bfloat16 [2, 4096, 16384], P('layer', None, ('latent', 'token')), may hold values from -0.09375 to 0.09375
- encoder_layer_bias: bfloat16 [2, 16384], P('layer', 'latent'), may hold values from -3 to 3
- dec_self: bfloat16 [2, 16384, 4096], P('layer', ('latent', 'token')), may hold values from -3 to 3
- dec_cross: bfloat16 [16384, 4096], P(('latent', 'token')), may hold values from -3 to 3
- dec_bias: bfloat16 [2, 4096], P('layer', 'latent'), may hold values from -3 to 3
Outputs:
- recon: bfloat16 [2, 1536, 4096], P('layer', ('groups', 'token'), 'latent'), parts along dimension 1
- loss: float32 [2], P('groups'), parts along dimension 0
The draws below stay inside these ranges and needn't reach their ends.
There are 2 independent parts, one for each index of `groups`. The reference program is written for one: setup_inputs(seed, part) draws one part's arguments, and reference() takes and returns one part's arrays. A program takes and returns all parts, laid end to end along the dimension named above; an argument that names none is the same for every part. Nothing has to cross between parts.
All inputs are finite; a program needn't handle non-finite values.
Results may differ from the reference program's by a relative error of at most 0.0054.
Values may be sent and summed in bfloat16 or wider, within the bound.
No kernel may reach another device: no remote copies, remote signals or barrier semaphores. Data moves between devices by JAX's collectives and lax.ppermute only.
A program may use at most 320 MiB of HBM per device.

```python
import math
import jax
import jax.numpy as jnp

D = 4096
F = 16384
LAYERS = 2
TOKENS = 768
DEC_BLOCKS = 8
OUT_BLOCKS = 4


def rough_field(key, spread_upper, bound):
    key_rows, key_cols, key_base = jax.random.split(key, 3)
    ramp = jnp.exp(jnp.log(3.0) * jnp.arange(TOKENS, dtype=jnp.float32) / max(TOKENS - 1, 1))
    row_factor_scale = jnp.exp(jax.random.uniform(key_rows, (LAYERS, TOKENS, 1), jnp.float32, 0.0, jnp.log(spread_upper)))
    col_scale = jnp.exp(jax.random.uniform(key_cols, (LAYERS, 1, D), jnp.float32, 0.0, jnp.log(spread_upper)))
    base = jnp.clip(jax.random.normal(key_base, (LAYERS, TOKENS, D), jnp.float32), -bound, bound)
    return base * row_factor_scale * col_scale * ramp[None, :, None]


def decoder_field(key, count, common):
    key_base, key_pair, key_shared = jax.random.split(key, 3)
    base = jnp.clip(jax.random.normal(key_base, (count, F, D), jnp.float32), -6.0, 6.0)
    pairing = jax.random.randint(key_pair, (count, DEC_BLOCKS), 0, OUT_BLOCKS)
    row_block = jnp.arange(F) // (F // DEC_BLOCKS)
    col_block = jnp.arange(D) // (D // OUT_BLOCKS)
    chosen = pairing[:, row_block]
    boosted = jnp.where(chosen[:, :, None] == col_block[None, None, :], 4.0 * base, base)
    shared = jnp.clip(jax.random.normal(key_shared, (count, 1, D), jnp.float32), -6.0, 6.0)
    return (boosted + common / math.sqrt(F) * shared) / math.sqrt(F)


def draw_inputs(key, part):
    key = jax.random.fold_in(key, 11)
    field = rough_field(key, 10.0, 6.0)
    return field.astype(jnp.bfloat16)


def draw_targets(key, part):
    key = jax.random.fold_in(key, 12)
    field = 0.05 * rough_field(key, 10.0, 6.0)
    return field.astype(jnp.bfloat16)


def draw_dec_self(key, part):
    key = jax.random.fold_in(key, 13)
    field = decoder_field(key, LAYERS, 1.5)
    return field.astype(jnp.bfloat16)


def draw_dec_cross(key, part):
    key = jax.random.fold_in(key, 14)
    field = decoder_field(key, 1, 1.5)
    return field[0].astype(jnp.bfloat16)


def levels(own_key, dims, cuts, smallest, largest):
    loudness, own = 1.0, jax.random.fold_in(own_key, 6)
    for axis_at, blocks in cuts:
        draws = jnp.exp(jax.random.uniform(jax.random.fold_in(own, axis_at), (blocks,), jnp.float32, smallest / len(cuts), largest / len(cuts)))
        loudness = loudness * jnp.repeat(draws, dims[axis_at] // blocks).reshape([-1 if axis == axis_at else 1 for axis in range(len(dims))])
    return loudness


def normal_values(stream_key, dims, width, reach, shards=(), kind=jnp.bfloat16):
    gain = levels(stream_key, dims, shards, -0.22, 0.18) if shards else 1.0
    array = jax.random.normal(stream_key, dims, jnp.float32) * width * gain
    return jnp.minimum(jnp.maximum(array, -reach), reach).astype(kind)


def setup_inputs(seed: int = 0, part: int = 0) -> dict:
    splits = jax.random.split(jax.random.key(seed), 8)
    part_keys = jax.random.split(jax.random.fold_in(splits[7], part), 8)
    return {
        "inputs": draw_inputs(jax.random.fold_in(jax.random.fold_in(splits[7], part), 71), part),
        "targets": draw_targets(jax.random.fold_in(jax.random.fold_in(splits[7], part), 71), part),
        "enc_weight": normal_values(splits[2], (LAYERS, D, F), D ** -0.5, 0.09375, ((0, 2), (2, 8))),
        "encoder_layer_bias": normal_values(splits[3], (LAYERS, F), 0.5, 3.0, ((0, 2), (1, 4))),
        "dec_self": draw_dec_self(jax.random.fold_in(splits[7], 71), part),
        "dec_cross": draw_dec_cross(jax.random.fold_in(splits[7], 71), part),
        "dec_bias": normal_values(splits[6], (LAYERS, D), 0.5, 3.0, ((0, 2), (1, 4))),
    }


def encode(inputs, enc_weight, encoder_layer_bias, layer):
    field = inputs[layer].astype(jnp.float32)
    scale = jnp.sqrt(jnp.mean(field * field) + 1e-06)
    normed = (field / scale).astype(jnp.bfloat16)
    pre = jnp.dot(normed, enc_weight[layer], preferred_element_type=jnp.float32) + encoder_layer_bias[layer].astype(jnp.float32)
    return jnp.maximum(pre, 0.0).astype(jnp.bfloat16)

def reference(inputs, targets, enc_weight, encoder_layer_bias, dec_self, dec_cross, dec_bias):
    first = encode(inputs, enc_weight, encoder_layer_bias, 0)
    second = encode(inputs, enc_weight, encoder_layer_bias, 1)
    total_first = jnp.dot(first, dec_self[0], preferred_element_type=jnp.float32) + dec_bias[0].astype(jnp.float32)
    total_second = jnp.dot(second, dec_self[1], preferred_element_type=jnp.float32)
    total_second = total_second + jnp.dot(first, dec_cross, preferred_element_type=jnp.float32) + dec_bias[1].astype(jnp.float32)
    totals = [total_first, total_second]
    ratios = []
    for layer in range(2):
        target = targets[layer].astype(jnp.float32)
        diff = totals[layer] - target
        ratios.append(jnp.sum(diff * diff) / jnp.sum(target * target))
    loss = ((ratios[0] + ratios[1]) / 2.0).reshape(1)
    recon = jnp.stack([total_first, total_second]).astype(jnp.bfloat16)
    return (recon, loss)
```

```python
import functools

import jax
import jax.numpy as jnp
from jax import lax
from jax.experimental import pallas as pl
from jax.experimental.pallas import tpu as pltpu
from jax.sharding import PartitionSpec as P

VMEM_LIMIT = 48 * 1024 * 1024
CHUNKS = 2


def tile_of(size, most):
    tile = min(size, most)
    while size % tile:
        tile //= 2
    return tile


def encode_body(inv_ref, x_ref, w_ref, b_ref, o_ref):
    pre = jnp.dot(x_ref[...], w_ref[...], preferred_element_type=jnp.float32)
    pre = pre * inv_ref[0] + b_ref[...].astype(jnp.float32)
    o_ref[...] = jnp.maximum(pre, 0.0).astype(o_ref.dtype)


def encode(x, inv, weight, bias):
    rows, width = x.shape
    latents = weight.shape[1]
    tile = tile_of(latents, 256)
    return pl.pallas_call(
        encode_body,
        grid=(latents // tile,),
        in_specs=[
            pl.BlockSpec(memory_space=pltpu.SMEM),
            pl.BlockSpec((rows, width), lambda j: (0, 0)),
            pl.BlockSpec((width, tile), lambda j: (0, j)),
            pl.BlockSpec((1, tile), lambda j: (0, j)),
        ],
        out_specs=pl.BlockSpec((rows, tile), lambda j: (0, j)),
        out_shape=jax.ShapeDtypeStruct((rows, latents), jnp.bfloat16),
        compiler_params=pltpu.CompilerParams(vmem_limit_bytes=VMEM_LIMIT),
        cost_estimate=pl.CostEstimate(
            flops=2 * rows * width * latents,
            bytes_accessed=2 * (rows * width + width * latents + rows * latents),
            transcendentals=0,
        ),
        name="encode",
    )(inv.reshape(1), x, weight, bias)


def decode_body(info_ref, c_ref, e_ref, s_ref, x_ref, o_ref):
    own = jnp.dot(c_ref[...], s_ref[...], preferred_element_type=jnp.float32)
    layer = info_ref[0]

    @pl.when(layer == 0)
    def _():
        o_ref[0] = own.astype(o_ref.dtype)

    @pl.when(layer != 0)
    def _():
        cross = jnp.dot(e_ref[...], x_ref[...], preferred_element_type=jnp.float32)
        o_ref[0] = (own + cross).astype(o_ref.dtype)


def decode(codes, earlier, own_w, cross_w, info, blocks, width, dtype):
    rows, latents = codes.shape
    tile = tile_of(width, 512)
    per = width // tile

    def column(b, j, info_ref):
        return (0, info_ref[1 + b] * per + j)

    def cross_column(b, j, info_ref):
        return (0, jnp.where(info_ref[0] == 0, 0, info_ref[1 + b] * per + j))

    return pl.pallas_call(
        decode_body,
        grid_spec=pltpu.PrefetchScalarGridSpec(
            num_scalar_prefetch=1,
            grid=(blocks, per),
            in_specs=[
                pl.BlockSpec((rows, latents), lambda b, j, r: (0, 0)),
                pl.BlockSpec((rows, latents), lambda b, j, r: (0, 0)),
                pl.BlockSpec((latents, tile), column),
                pl.BlockSpec((latents, tile), cross_column),
            ],
            out_specs=pl.BlockSpec((1, rows, tile), lambda b, j, r: (b, 0, j)),
        ),
        out_shape=jax.ShapeDtypeStruct((blocks, rows, width), dtype),
        compiler_params=pltpu.CompilerParams(vmem_limit_bytes=VMEM_LIMIT),
        cost_estimate=pl.CostEstimate(
            flops=4 * rows * latents * blocks * width,
            bytes_accessed=4 * (rows * latents + latents * blocks * width) + 4 * rows * blocks * width,
            transcendentals=0,
        ),
        name="decode",
    )(info, codes, earlier, own_w, cross_w)


def shifted(value, axis, distance):
    n = lax.axis_size(axis)
    return lax.ppermute(value, axis, [(i, (i + distance) % n) for i in range(n)])


def swapped(value, axis, bit):
    n = lax.axis_size(axis)
    return lax.ppermute(value, axis, [(i, i ^ bit) for i in range(n)])


def sum_over(value, axis):
    total = value
    for distance in range(1, lax.axis_size(axis)):
        total = total + shifted(value, axis, distance)
    return total


def local(inputs, targets, enc_weight, encoder_layer_bias, dec_self, dec_cross, dec_bias):
    layer = lax.axis_index("layer")
    lat = lax.axis_index("latent")
    n_lat = lax.axis_size("latent")
    n_tok = lax.axis_size("token")
    x_own = inputs[0]
    rows, model = x_own.shape
    enc_w = enc_weight[0]
    own_w = dec_self[0]
    lat_dev = enc_w.shape[1]
    width = dec_bias.shape[1]
    chunk = rows // CHUNKS

    foreign = []
    for distance in range(1, n_tok):
        for c in range(CHUNKS):
            piece = x_own[c * chunk:(c + 1) * chunk]
            foreign.append((distance, shifted(piece, "token", distance)))

    field = x_own.astype(jnp.float32)
    square = sum_over(jnp.sum(field * field).reshape(1, 1), "token")
    scale = jnp.sqrt(square[0, 0] / (rows * n_tok * model) + 1e-06)
    inv = 1.0 / scale
    bias = lax.dynamic_slice_in_dim(
        encoder_layer_bias, lax.axis_index("token") * lat_dev, lat_dev, axis=1
    )

    half = n_lat // 2
    kept = [2 * i + lat % 2 for i in range(half)]
    sent = [2 * i + 1 - lat % 2 for i in range(half)]
    info_kept = jnp.stack([layer] + kept).astype(jnp.int32)
    info_sent = jnp.stack([layer] + sent).astype(jnp.int32)

    def work(x):
        codes = encode(x, inv, enc_w, bias)
        earlier = lax.ppermute(codes, "layer", [(0, 1)])
        away = decode(codes, earlier, own_w, dec_cross, info_sent, half, width, jnp.bfloat16)
        arrived = swapped(away, "latent", 1)
        total = decode(codes, earlier, own_w, dec_cross, info_kept, half, width, jnp.float32)
        total = total + arrived.astype(jnp.float32)
        bit = 2
        while bit < n_lat:
            mine = (lat // bit) % 2
            pairs = total.reshape(total.shape[0] // 2, 2, x.shape[0], width)
            away = lax.dynamic_index_in_dim(pairs, 1 - mine, 1, keepdims=False).astype(jnp.bfloat16)
            arrived = swapped(away, "latent", bit)
            total = lax.dynamic_index_in_dim(pairs, mine, 1, keepdims=False) + arrived.astype(jnp.float32)
            bit *= 2
        return total[0]

    total = work(x_own)
    returned = []
    for distance, x in foreign:
        part = work(x).astype(jnp.bfloat16)
        returned.append(shifted(part, "token", n_tok - distance))
    for d in range(n_tok - 1):
        total = total + jnp.concatenate(returned[d * CHUNKS:(d + 1) * CHUNKS]).astype(jnp.float32)
    total = total + dec_bias.astype(jnp.float32)
    recon = total.astype(jnp.bfloat16)[None]

    target = targets[0].astype(jnp.float32)
    diff = total - target
    sums = jnp.stack([jnp.sum(diff * diff), jnp.sum(target * target)]).reshape(1, 2)
    sums = sum_over(sum_over(sums, "latent"), "token")
    ratio = sums[:, 0] / sums[:, 1]
    loss = sum_over(ratio, "layer") / 2.0
    return (recon, loss)


def solution(mesh):
    return jax.shard_map(
        local,
        mesh=mesh,
        in_specs=(
            P("layer", ("groups", "token"), None),
            P("layer", ("groups", "token"), "latent"),
            P("layer", None, ("latent", "token")),
            P("layer", "latent"),
            P("layer", ("latent", "token"), None),
            P(("latent", "token"), None),
            P("layer", "latent"),
        ),
        out_specs=(P("layer", ("groups", "token"), "latent"), P("groups")),
        check_vma=False,
    )
```

```python
import jax
import jax.numpy as jnp
from jax import lax
from jax.experimental import pallas as pl
from jax.experimental.pallas import tpu as pltpu
from jax.sharding import PartitionSpec as P

VMEM_LIMIT = 24 * 1024 * 1024
SLOTS = 3


def tile_of(size, most):
    tile = min(size, most)
    while size % tile:
        tile //= 2
    return tile


def square_body(x_ref, o_ref):
    @pl.when(pl.program_id(0) == 0)
    def _():
        o_ref[...] = jnp.zeros_like(o_ref)

    value = x_ref[...].astype(jnp.float32)
    value = value * value
    rows, width = value.shape
    o_ref[...] += jnp.sum(value.reshape(rows // 8, 8, width), axis=0)


def square_sum(x):
    rows, width = x.shape
    tile = tile_of(rows, 96)
    sums = pl.pallas_call(
        square_body,
        grid=(rows // tile,),
        in_specs=[pl.BlockSpec((tile, width), lambda i: (i, 0))],
        out_specs=pl.BlockSpec((8, width), lambda i: (0, 0)),
        out_shape=jax.ShapeDtypeStruct((8, width), jnp.float32),
        cost_estimate=pl.CostEstimate(
            flops=2 * rows * width, bytes_accessed=2 * rows * width, transcendentals=0
        ),
        name="square_sum",
    )(x)
    return jnp.sum(sums)


def ring_loop(count, per, depth, start, wait, lhs, ring, acc, finish):
    slots = ring.shape[0]
    for t in range(slots):
        @pl.when(t < count)
        def _():
            start(t)

    def step(t, carry):
        r = lax.rem(t, per)
        slot = lax.rem(t, slots)
        wait(t, r, slot)
        left = lhs[:, pl.ds(pl.multiple_of(r * depth, depth), depth)]
        part = jnp.dot(left, ring[slot], preferred_element_type=jnp.float32)

        @pl.when(r == 0)
        def _():
            acc[...] = part

        @pl.when(r > 0)
        def _():
            acc[...] += part

        @pl.when(t + slots < count)
        def _():
            start(t + slots)

        @pl.when(r == per - 1)
        def _():
            finish(lax.div(t, per))

        return carry

    lax.fori_loop(0, count, step, 0)


def encode(pieces, places, inv, weight, bias, after):
    sizes = [piece.shape[0] for piece in pieces]
    rows, width = sum(sizes), pieces[0].shape[1]
    latents = weight.shape[1]
    tile = tile_of(latents, 1024)
    depth = tile_of(width, 1024)
    per = width // depth
    count = (latents // tile) * per
    n = len(pieces)

    def body(places_ref, inv_ref, b_ref, *refs):
        x_refs, (w_ref, after_ref, o_ref, lhs, ring, acc, lhs_sem, ring_sem) = refs[:n], refs[n:]

        def lhs_copy(i, r):
            part = pl.ds(r * depth, depth)
            place = pl.ds(pl.multiple_of(places_ref[i], 16), sizes[i])
            return pltpu.make_async_copy(
                x_refs[i].at[:, part], lhs.at[place, part], lhs_sem.at[i, r])

        def tile_copy(t):
            b, r, slot = t // per, t % per, t % SLOTS
            down = pl.ds(pl.multiple_of(r * depth, depth), depth)
            across = pl.ds(pl.multiple_of(b * tile, tile), tile)
            return pltpu.make_async_copy(w_ref.at[down, across], ring.at[slot], ring_sem.at[slot])

        for r in range(per):
            for i in range(n):
                lhs_copy(i, r).start()

        def wait(t, r, slot):
            for s in range(per):
                @pl.when(t == s)
                def _():
                    for i in range(n):
                        lhs_copy(i, s).wait()
            tile_copy(t).wait()

        def finish(b):
            across = pl.ds(pl.multiple_of(b * tile, tile), tile)
            pre = acc[...] * inv_ref[0] + b_ref[:, across].astype(jnp.float32)
            o_ref[:, across] = jnp.maximum(pre, 0.0).astype(o_ref.dtype)

        ring_loop(count, per, depth, lambda t: tile_copy(t).start(), wait, lhs, ring, acc, finish)

    return pl.pallas_call(
        body,
        in_specs=[
            pl.BlockSpec(memory_space=pltpu.SMEM),
            pl.BlockSpec(memory_space=pltpu.SMEM),
            pl.BlockSpec(memory_space=pltpu.VMEM),
        ] + [pl.BlockSpec(memory_space=pl.ANY)] * (n + 2),
        out_specs=pl.BlockSpec(memory_space=pltpu.VMEM),
        out_shape=jax.ShapeDtypeStruct((rows, latents), jnp.bfloat16),
        scratch_shapes=[
            pltpu.VMEM((rows, width), jnp.bfloat16),
            pltpu.VMEM((SLOTS, depth, tile), jnp.bfloat16),
            pltpu.VMEM((rows, tile), jnp.float32),
            pltpu.SemaphoreType.DMA((n, per)),
            pltpu.SemaphoreType.DMA((SLOTS,)),
        ],
        compiler_params=pltpu.CompilerParams(vmem_limit_bytes=VMEM_LIMIT),
        cost_estimate=pl.CostEstimate(
            flops=2 * rows * width * latents,
            bytes_accessed=2 * (rows * width + width * latents + rows * latents),
            transcendentals=0,
        ),
        name="encode",
    )(places, inv.reshape(1), bias, *pieces, weight, after)


def decode(codes, earlier, own_w, cross_w, info, group, width, dtype):
    rows, latents = codes.shape
    depth = tile_of(latents, 1024)
    steps = latents // depth

    def body(info_ref, c_ref, e_ref, s_ref, x_ref, first_ref, second_ref, lhs, ring, acc, lhs_sem, ring_sem):
        later = info_ref[0] != 0
        per = jnp.where(later, 2 * steps, steps)
        count = 2 * group * per

        def lhs_copy(source, i):
            part = pl.ds((i % steps) * depth, depth)
            return pltpu.make_async_copy(
                source.at[:, part], lhs.at[:, pl.ds(i * depth, depth)], lhs_sem.at[i])

        def tile_copy(source, t, k):
            slot = lax.rem(t, SLOTS)
            down = pl.ds(pl.multiple_of(k * depth, depth), depth)
            across = pl.ds(pl.multiple_of(info_ref[1 + lax.div(t, per)] * width, width), width)
            return pltpu.make_async_copy(source.at[down, across], ring.at[slot], ring_sem.at[slot])

        def start(t):
            r = lax.rem(t, per)

            @pl.when(r < steps)
            def _():
                tile_copy(s_ref, t, r).start()

            @pl.when(r >= steps)
            def _():
                tile_copy(x_ref, t, r - steps).start()

        for i in range(steps):
            lhs_copy(c_ref, i).start()

        @pl.when(later)
        def _():
            for i in range(steps, 2 * steps):
                lhs_copy(e_ref, i).start()

        def wait(t, r, slot):
            for i in range(2 * steps):
                @pl.when((t == i) & (t < per))
                def _():
                    lhs_copy(c_ref, i).wait()
            tile_copy(s_ref, t, 0).wait()

        def finish(b):
            @pl.when(b < group)
            def _():
                first_ref[jnp.minimum(b, group - 1)] = acc[...].astype(dtype)

            @pl.when(b >= group)
            def _():
                second_ref[jnp.maximum(b - group, 0)] = acc[...].astype(dtype)

        ring_loop(count, per, depth, start, wait, lhs, ring, acc, finish)

    return pl.pallas_call(
        body,
        in_specs=[pl.BlockSpec(memory_space=pltpu.SMEM)] + [pl.BlockSpec(memory_space=pl.ANY)] * 4,
        out_specs=[pl.BlockSpec(memory_space=pltpu.VMEM)] * 2,
        out_shape=[jax.ShapeDtypeStruct((group, rows, width), dtype)] * 2,
        scratch_shapes=[
            pltpu.VMEM((rows, 2 * latents), jnp.bfloat16),
            pltpu.VMEM((SLOTS, depth, width), jnp.bfloat16),
            pltpu.VMEM((rows, width), jnp.float32),
            pltpu.SemaphoreType.DMA((2 * steps,)),
            pltpu.SemaphoreType.DMA((SLOTS,)),
        ],
        compiler_params=pltpu.CompilerParams(vmem_limit_bytes=VMEM_LIMIT),
        cost_estimate=pl.CostEstimate(
            flops=8 * rows * latents * group * width,
            bytes_accessed=4 * (rows * latents + 2 * latents * group * width) + 8 * rows * group * width,
            transcendentals=0,
        ),
        name="decode",
    )(info, codes, earlier, own_w, cross_w)


def shifted(value, axis, distance):
    n = lax.axis_size(axis)
    return lax.ppermute(value, axis, [(i, (i + distance) % n) for i in range(n)])


def swapped(value, axis, bit):
    n = lax.axis_size(axis)
    return lax.ppermute(value, axis, [(i, i ^ bit) for i in range(n)])


def sum_over(value, axis):
    total = value
    for distance in range(1, lax.axis_size(axis)):
        total = total + shifted(value, axis, distance)
    return total


def wide(value):
    return value.astype(jnp.float32)


def local(inputs, targets, enc_weight, encoder_layer_bias, dec_self, dec_cross, dec_bias):
    layer = lax.axis_index("layer")
    lat = lax.axis_index("latent")
    n_lat = lax.axis_size("latent")
    n_tok = lax.axis_size("token")
    x_own = inputs[0]
    rows, model = x_own.shape
    enc_w = enc_weight[0]
    own_w = dec_self[0]
    lat_dev = enc_w.shape[1]
    width = dec_bias.shape[1]
    quarter = rows // 4
    side = lat % 2

    square = sum_over(square_sum(x_own).reshape(1, 1), "token")
    scale = jnp.sqrt(square[0, 0] / (rows * n_tok * model) + 1e-06)
    inv = 1.0 / scale

    outer = lax.dynamic_slice_in_dim(x_own, side * 3 * quarter, quarter, axis=0)
    middle = x_own[quarter:3 * quarter]
    foreign = []
    for distance in range(1, n_tok):
        mine = shifted(outer, "token", distance)
        centre = shifted(middle, "token", distance)
        theirs = swapped(mine, "latent", 1)
        foreign.append((distance, mine, theirs, centre))

    bias = lax.dynamic_slice_in_dim(
        encoder_layer_bias, lax.axis_index("token") * lat_dev, lat_dev, axis=1
    )

    group = n_lat // 4
    other, mine_bit = 1 - lat % 2, lat % 2
    far, near = 1 - (lat // 2) % 2, (lat // 2) % 2
    info_sent = jnp.stack(
        [layer] + [4 * i + 2 * b + other for b in (far, near) for i in range(group)]
    ).astype(jnp.int32)
    info_kept = jnp.stack(
        [layer] + [4 * i + 2 * b + mine_bit for b in (far, near) for i in range(group)]
    ).astype(jnp.int32)

    def work(pieces, places, after):
        codes = encode(pieces, jnp.stack(places).astype(jnp.int32), inv, enc_w, bias, after)
        height = codes.shape[0]
        earlier = lax.ppermute(codes, "layer", [(0, 1)])
        far_sent, near_sent = decode(
            codes, earlier, own_w, dec_cross, info_sent, group, width, jnp.bfloat16)
        far_in = swapped(far_sent, "latent", 1)
        near_in = swapped(near_sent, "latent", 1)
        far_kept, near_kept = decode(
            codes, earlier, own_w, dec_cross, info_kept, group, width, jnp.float32)
        across = swapped((far_kept + wide(far_in)).astype(jnp.bfloat16), "latent", 2)
        total = near_kept + wide(near_in) + wide(across)
        bit = 4
        while bit < n_lat:
            here = (lat // bit) % 2
            pairs = total.reshape(total.shape[0] // 2, 2, height, width)
            away = lax.dynamic_index_in_dim(pairs, 1 - here, 1, keepdims=False)
            arrived = swapped(away.astype(jnp.bfloat16), "latent", bit)
            total = lax.dynamic_index_in_dim(pairs, here, 1, keepdims=False) + wide(arrived)
            bit *= 2
        return total[0], near_kept

    origin = jnp.int32(0)
    total, after = work([x_own], [origin], x_own)
    for distance, mine, theirs, centre in foreign:
        part, after = work([mine, theirs], [side * quarter, (1 - side) * quarter], after)
        ends = shifted(part.astype(jnp.bfloat16), "token", n_tok - distance)
        part, after = work([centre], [origin], after)
        centre = shifted(part.astype(jnp.bfloat16), "token", n_tok - distance)
        total = total + wide(jnp.concatenate([ends[:quarter], centre, ends[quarter:]]))
    total = total + wide(dec_bias)
    recon = total.astype(jnp.bfloat16)[None]

    target = wide(targets[0])
    diff = total - target
    sums = jnp.stack([jnp.sum(diff * diff), jnp.sum(target * target)]).reshape(1, 2)
    sums = sum_over(sum_over(sums, "latent"), "token")
    ratio = sums[:, 0] / sums[:, 1]
    loss = sum_over(ratio, "layer") / 2.0
    return (recon, loss)


def solution(mesh):
    return jax.shard_map(
        local,
        mesh=mesh,
        in_specs=(
            P("layer", ("groups", "token"), None),
            P("layer", ("groups", "token"), "latent"),
            P("layer", None, ("latent", "token")),
            P("layer", "latent"),
            P("layer", ("latent", "token"), None),
            P(("latent", "token"), None),
            P("layer", "latent"),
        ),
        out_specs=(P("layer", ("groups", "token"), "latent"), P("groups")),
        check_vma=False,
    )
```

```python
import jax
import jax.numpy as jnp
from jax import lax
from jax.experimental import pallas as pl
from jax.experimental.pallas import tpu as pltpu
from jax.sharding import PartitionSpec as P

VMEM_LIMIT = 48 * 1024 * 1024
SLOTS = 3
TILE = 512
COST = pl.CostEstimate(flops=0, bytes_accessed=0, transcendentals=0)


def tile_of(size, most):
    tile = min(size, most)
    while size % tile:
        tile //= 2
    return tile


def prepare(x, side):
    rows, width = x.shape
    quarter = rows // 4
    lanes = tile_of(width, 1024)

    def body(side_ref, x_ref, outer_ref, inner_ref, o_ref, held, sem, out_sem):
        def load(i):
            place = pl.ds(i * quarter, quarter)
            return pltpu.make_async_copy(x_ref.at[place], held.at[place], sem.at[i])

        first = pl.ds(pl.multiple_of(side_ref[0] * (3 * quarter), 16), quarter)
        cuts = [
            pltpu.make_async_copy(x_ref.at[first], outer_ref, out_sem.at[0]),
            pltpu.make_async_copy(x_ref.at[pl.ds(quarter, 2 * quarter)], inner_ref, out_sem.at[1]),
        ]
        for i in range(4):
            load(i).start()
        for copy in cuts:
            copy.start()
        total = jnp.zeros((8, lanes), jnp.float32)
        for i in range(4):
            load(i).wait()
            for c in range(width // lanes):
                def add(r, acc):
                    here = pl.ds(pl.multiple_of(i * quarter + r * 16, 16), 16)
                    value = held[here, c * lanes:(c + 1) * lanes].astype(jnp.float32)
                    value = value * value
                    return acc + value[:8] + value[8:]

                total = lax.fori_loop(0, quarter // 16, add, total)
        o_ref[0] = jnp.sum(total)
        for copy in cuts:
            copy.wait()

    return pl.pallas_call(
        body,
        in_specs=[pl.BlockSpec(memory_space=pltpu.SMEM), pl.BlockSpec(memory_space=pl.ANY)],
        out_specs=[pl.BlockSpec(memory_space=pl.ANY)] * 2 + [pl.BlockSpec(memory_space=pltpu.SMEM)],
        out_shape=[
            jax.ShapeDtypeStruct((quarter, width), x.dtype),
            jax.ShapeDtypeStruct((2 * quarter, width), x.dtype),
            jax.ShapeDtypeStruct((1,), jnp.float32),
        ],
        scratch_shapes=[
            pltpu.VMEM((rows, width), x.dtype),
            pltpu.SemaphoreType.DMA((4,)),
            pltpu.SemaphoreType.DMA((2,)),
        ],
        compiler_params=pltpu.CompilerParams(vmem_limit_bytes=VMEM_LIMIT),
        cost_estimate=COST,
        name="prepare",
    )(side.reshape(1), x)


def ring_loop(count, start, step):
    for t in range(min(SLOTS, count)):
        start(t, t)

    def turn(t, carry):
        slot = lax.rem(t, SLOTS)
        step(t, slot)

        @pl.when(t + SLOTS < count)
        def _():
            start(t + SLOTS, slot)

        return carry

    lax.fori_loop(0, count, turn, 0)


def encode(pieces, places, inv, weight, bias, parts, after):
    rows, width = sum(piece[2] for piece in pieces), pieces[0][0].shape[1]
    latents = weight.shape[1]
    tile = tile_of(latents // parts, TILE)
    per = latents // parts // tile
    n = len(pieces)

    def body(places_ref, inv_ref, b_ref, *refs):
        x_refs, w_ref, o_refs = refs[:n], refs[n], refs[n + 2:n + 2 + parts]
        lhs, ring, lhs_sem, ring_sem = refs[n + 2 + parts:]

        def lhs_copy(i):
            _, first, count = pieces[i]
            place = pl.ds(pl.multiple_of(places_ref[i], 16), count)
            return pltpu.make_async_copy(
                x_refs[i].at[pl.ds(first, count)], lhs.at[place], lhs_sem.at[i])

        def columns(t):
            return pl.ds(pl.multiple_of(t * tile, tile), tile)

        def tile_copy(t, slot):
            return pltpu.make_async_copy(w_ref.at[:, columns(t)], ring.at[slot], ring_sem.at[slot])

        for i in range(n):
            lhs_copy(i).start()

        def step(t, slot):
            @pl.when(t == 0)
            def _():
                for i in range(n):
                    lhs_copy(i).wait()

            tile_copy(t, slot).wait()
            pre = jnp.dot(lhs[...], ring[slot], preferred_element_type=jnp.float32)
            pre = pre * inv_ref[0] + b_ref[:, columns(t)].astype(jnp.float32)
            value = jnp.maximum(pre, 0.0).astype(jnp.bfloat16)
            for p in range(parts):
                @pl.when(lax.div(t, per) == p)
                def _():
                    o_refs[p][:, columns(lax.rem(t, per))] = value

        ring_loop(latents // tile, lambda t, slot: tile_copy(t, slot).start(), step)

    return pl.pallas_call(
        body,
        in_specs=[
            pl.BlockSpec(memory_space=pltpu.SMEM),
            pl.BlockSpec(memory_space=pltpu.SMEM),
            pl.BlockSpec(memory_space=pltpu.VMEM),
        ] + [pl.BlockSpec(memory_space=pl.ANY)] * (n + 2),
        out_specs=[pl.BlockSpec(memory_space=pltpu.VMEM)] * parts,
        out_shape=[jax.ShapeDtypeStruct((rows, latents // parts), jnp.bfloat16)] * parts,
        scratch_shapes=[
            pltpu.VMEM((rows, width), jnp.bfloat16),
            pltpu.VMEM((SLOTS, width, tile), jnp.bfloat16),
            pltpu.SemaphoreType.DMA((n,)),
            pltpu.SemaphoreType.DMA((SLOTS,)),
        ],
        compiler_params=pltpu.CompilerParams(vmem_limit_bytes=VMEM_LIMIT),
        cost_estimate=COST,
        name="encode",
    )(places, inv.reshape(1), bias, *[piece[0] for piece in pieces], weight, after)


def decode(codes, earlier, own_w, cross_w, info, outs, width, after):
    parts = len(codes)
    rows, part = codes[0].shape
    latents = parts * part
    tile = tile_of(width, TILE)
    per = width // tile
    blocks = info.shape[0] - 1

    def body(info_ref, *refs):
        c_refs, e_refs, s_ref, x_ref = refs[:parts], refs[parts:2 * parts], refs[2 * parts], refs[2 * parts + 1]
        o_refs = refs[2 * parts + 3:2 * parts + 3 + len(outs)]
        lhs, ring, lhs_sem, ring_sem = refs[2 * parts + 3 + len(outs):]
        later = info_ref[0] != 0

        def lhs_copy(i):
            source = c_refs[i] if i < parts else e_refs[i - parts]
            return pltpu.make_async_copy(source, lhs.at[:, pl.ds(i * part, part)], lhs_sem.at[i])

        def tile_copy(source, i, t, slot):
            column = info_ref[1 + lax.div(t, per)] * width + lax.rem(t, per) * tile
            across = pl.ds(pl.multiple_of(column, tile), tile)
            return pltpu.make_async_copy(
                source.at[:, across], ring.at[slot, pl.ds(i * latents, latents)], ring_sem.at[slot, i])

        def start(t, slot):
            t = jnp.int32(t)
            tile_copy(s_ref, 0, t, slot).start()

            @pl.when(later)
            def _():
                tile_copy(x_ref, 1, t, slot).start()

        for i in range(parts):
            lhs_copy(i).start()

        @pl.when(later)
        def _():
            for i in range(parts, 2 * parts):
                lhs_copy(i).start()

        def put(t, value):
            b = lax.div(t, per)
            across = pl.ds(pl.multiple_of(lax.rem(t, per) * tile, tile), tile)
            for (block, count, row, height, dtype), o_ref in zip(outs, o_refs):
                @pl.when((b >= block) & (b < block + count))
                def _():
                    here = jnp.clip(b - block, 0, count - 1)
                    o_ref[here, :, across] = value[row:row + height].astype(dtype)

        def step(t, slot):
            @pl.when(t == 0)
            def _():
                for i in range(parts):
                    lhs_copy(i).wait()

            tile_copy(s_ref, 0, t, slot).wait()

            @pl.when(later)
            def _():
                @pl.when(t == 0)
                def _():
                    for i in range(parts, 2 * parts):
                        lhs_copy(i).wait()

                tile_copy(x_ref, 1, t, slot).wait()
                put(t, jnp.dot(lhs[...], ring[slot], preferred_element_type=jnp.float32))

            @pl.when(jnp.logical_not(later))
            def _():
                put(t, jnp.dot(
                    lhs[:, :latents], ring[slot, :latents], preferred_element_type=jnp.float32))

        ring_loop(blocks * per, start, step)

    return pl.pallas_call(
        body,
        in_specs=[pl.BlockSpec(memory_space=pltpu.SMEM)]
        + [pl.BlockSpec(memory_space=pl.ANY)] * (2 * parts + 3),
        out_specs=[pl.BlockSpec(memory_space=pltpu.VMEM)] * len(outs),
        out_shape=[
            jax.ShapeDtypeStruct((count, height, width), dtype)
            for _, count, _, height, dtype in outs
        ],
        scratch_shapes=[
            pltpu.VMEM((rows, 2 * latents), jnp.bfloat16),
            pltpu.VMEM((SLOTS, 2 * latents, tile), jnp.bfloat16),
            pltpu.SemaphoreType.DMA((2 * parts,)),
            pltpu.SemaphoreType.DMA((SLOTS, 2)),
        ],
        compiler_params=pltpu.CompilerParams(vmem_limit_bytes=VMEM_LIMIT),
        cost_estimate=COST,
        name="decode",
    )(info, *codes, *earlier, own_w, cross_w, after)


def shifted(value, axis, distance):
    n = lax.axis_size(axis)
    return lax.ppermute(value, axis, [(i, (i + distance) % n) for i in range(n)])


def swapped(value, axis, bit):
    n = lax.axis_size(axis)
    return lax.ppermute(value, axis, [(i, i ^ bit) for i in range(n)])


def sum_over(value, axis):
    total = value
    for distance in range(1, lax.axis_size(axis)):
        total = total + shifted(value, axis, distance)
    return total


def wide(value):
    return value.astype(jnp.float32)


def local(inputs, targets, enc_weight, encoder_layer_bias, dec_self, dec_cross, dec_bias):
    layer = lax.axis_index("layer")
    lat = lax.axis_index("latent")
    n_lat = lax.axis_size("latent")
    n_tok = lax.axis_size("token")
    x_own = inputs[0]
    rows, model = x_own.shape
    enc_w = enc_weight[0]
    own_w = dec_self[0]
    lat_dev = enc_w.shape[1]
    width = dec_bias.shape[1]
    quarter = rows // 4
    side = lat % 2

    outer, inner, square = prepare(x_own, side.astype(jnp.int32))
    square = sum_over(square, "token")
    scale = jnp.sqrt(square / (rows * n_tok * model) + 1e-06)
    inv = 1.0 / scale
    foreign = []
    for distance in range(1, n_tok):
        mine = shifted(outer, "token", distance)
        theirs = swapped(mine, "latent", 1)
        foreign.append((n_tok - distance, mine, theirs, shifted(inner, "token", distance)))

    bias = lax.dynamic_slice_in_dim(
        encoder_layer_bias, lax.axis_index("token") * lat_dev, lat_dev, axis=1
    )

    group = n_lat // 4
    other, mine_bit = 1 - lat % 2, lat % 2
    far, near = 1 - (lat // 2) % 2, (lat // 2) % 2
    info_sent = jnp.stack(
        [layer] + [4 * i + 2 * b + other for b in (far, near) for i in range(group)]
    ).astype(jnp.int32)
    info_kept = jnp.stack(
        [layer] + [4 * i + 2 * b + mine_bit for b in (far, near) for i in range(group)]
    ).astype(jnp.int32)

    half = 2 * quarter
    both = 2 * group
    narrow = jnp.bfloat16
    origin = jnp.int32(0)

    def codes_of(pieces, places, parts, after):
        codes = encode(
            pieces, jnp.stack(places).astype(jnp.int32), inv, enc_w, bias, parts, after)
        return codes, [lax.ppermute(part, "layer", [(0, 1)]) for part in codes]

    def products(codes, info, outs, after):
        return decode(*codes, own_w, dec_cross, info, outs, width, after)

    def finish(total):
        bit = 4
        while bit < n_lat:
            here = (lat // bit) % 2
            pairs = total.reshape(total.shape[0] // 2, 2, *total.shape[1:])
            away = lax.dynamic_index_in_dim(pairs, 1 - here, 1, keepdims=False)
            arrived = swapped(away.astype(narrow), "latent", bit)
            total = lax.dynamic_index_in_dim(pairs, here, 1, keepdims=False) + wide(arrived)
            bit *= 2
        return total[0]

    codes = codes_of([(x_own, quarter, half), (x_own, 0, quarter), (x_own, 3 * quarter, quarter)],
                     [origin, origin + half, origin + half + quarter], 2, x_own)
    sent_in, sent_out = products(
        codes, info_sent, [(0, both, 0, half, narrow), (0, both, half, half, jnp.float32)], codes[0][0])
    there_in = swapped(sent_in, "latent", 1)
    kept_in, kept_out = products(
        codes, info_kept, [(0, both, 0, half, jnp.float32), (0, both, half, half, jnp.float32)], sent_in)
    after = kept_in
    across_in = (kept_in[:group] + wide(there_in[:group])).astype(narrow)
    total_in = kept_in[group:] + wide(there_in[group:]) + wide(swapped(across_in, "latent", 2))

    sent_back, kept_back = [], []
    for back, mine, theirs, _ in foreign:
        codes = codes_of([(mine, 0, quarter), (theirs, 0, quarter)],
                         [side * quarter, (1 - side) * quarter], 1, after)
        sent, = products(codes, info_sent, [(0, both, 0, half, narrow)], across_in)
        sent_back.append(shifted(sent, "token", back))
        kept, = products(codes, info_kept, [(0, both, 0, half, narrow)], sent)
        kept_back.append(shifted(kept, "token", back))
        after = kept

    sent_out = (sent_out + sum(wide(part) for part in sent_back)).astype(narrow)
    there_out = swapped(sent_out, "latent", 1)
    returned = []
    for back, _, _, rows_in in foreign:
        codes = codes_of([(rows_in, 0, half)], [origin], 1, after)
        far_sent, near_sent = products(
            codes, info_sent, [(0, group, 0, half, narrow), (group, group, 0, half, narrow)], codes[0][0])
        far_in = swapped(far_sent, "latent", 1)
        near_in = swapped(near_sent, "latent", 1)
        after = far_sent if returned else sent_out
        kept, = products(codes, info_kept, [(0, both, 0, half, jnp.float32)], after)
        across = (kept[:group] + wide(far_in)).astype(narrow)
        part = finish(kept[group:] + wide(near_in) + wide(swapped(across, "latent", 2)))
        returned.append(shifted(part.astype(narrow), "token", back))
        after = kept

    kept_out = kept_out + sum(wide(part) for part in kept_back) + wide(there_out)
    across_out = swapped(kept_out[:group].astype(narrow), "latent", 2)
    total_out = finish(kept_out[group:] + wide(across_out))
    total_in = finish(total_in) + sum(wide(part) for part in returned)
    total = jnp.concatenate([total_out[:quarter], total_in, total_out[quarter:]])
    total = total + wide(dec_bias)
    recon = total.astype(jnp.bfloat16)[None]

    target = wide(targets[0])
    diff = total - target
    sums = jnp.stack([jnp.sum(diff * diff), jnp.sum(target * target)]).reshape(1, 2)
    sums = sum_over(sum_over(sums, "latent"), "token")
    ratio = sums[:, 0] / sums[:, 1]
    loss = sum_over(ratio, "layer") / 2.0
    return (recon, loss)


def solution(mesh):
    return jax.shard_map(
        local,
        mesh=mesh,
        in_specs=(
            P("layer", ("groups", "token"), None),
            P("layer", ("groups", "token"), "latent"),
            P("layer", None, ("latent", "token")),
            P("layer", "latent"),
            P("layer", ("latent", "token"), None),
            P(("latent", "token"), None),
            P("layer", "latent"),
        ),
        out_specs=(P("layer", ("groups", "token"), "latent"), P("groups")),
        check_vma=False,
    )
```

```python
import jax
import jax.numpy as jnp
from jax import lax
from jax.experimental import pallas as pl
from jax.experimental.pallas import tpu as pltpu
from jax.sharding import PartitionSpec as P

VMEM_LIMIT = 24 * 1024 * 1024
SLOTS = 3
TILE = 512
COST = pl.CostEstimate(flops=0, bytes_accessed=0, transcendentals=0)


def tile_of(size, most):
    tile = min(size, most)
    while size % tile:
        tile //= 2
    return tile


def square_sum(x):
    rows, width = x.shape
    lanes = tile_of(width, 1024)

    def body(x_ref, o_ref):
        total = jnp.zeros((8, lanes), jnp.float32)
        for c in range(width // lanes):
            def add(r, acc):
                here = pl.ds(pl.multiple_of(r * 16, 16), 16)
                value = x_ref[here, c * lanes:(c + 1) * lanes].astype(jnp.float32)
                value = value * value
                return acc + value[:8] + value[8:]

            total = lax.fori_loop(0, rows // 16, add, total)
        o_ref[0] = jnp.sum(total)

    return pl.pallas_call(
        body,
        in_specs=[pl.BlockSpec(memory_space=pltpu.VMEM)],
        out_specs=pl.BlockSpec(memory_space=pltpu.SMEM),
        out_shape=jax.ShapeDtypeStruct((1,), jnp.float32),
        compiler_params=pltpu.CompilerParams(vmem_limit_bytes=VMEM_LIMIT),
        cost_estimate=COST,
        name="square_sum",
    )(x)


def cut(x, side, after):
    rows, width = x.shape
    quarter = rows // 4

    def body(side_ref, after_ref, x_ref, outer_ref, inner_ref, sem):
        first = pl.ds(pl.multiple_of(side_ref[0] * (3 * quarter), 16), quarter)
        copies = [
            pltpu.make_async_copy(x_ref.at[first], outer_ref, sem.at[0]),
            pltpu.make_async_copy(x_ref.at[pl.ds(quarter, 2 * quarter)], inner_ref, sem.at[1]),
        ]
        for copy in copies:
            copy.start()
        for copy in copies:
            copy.wait()

    return pl.pallas_call(
        body,
        in_specs=[
            pl.BlockSpec(memory_space=pltpu.SMEM),
            pl.BlockSpec(memory_space=pltpu.SMEM),
            pl.BlockSpec(memory_space=pl.ANY),
        ],
        out_specs=[pl.BlockSpec(memory_space=pl.ANY)] * 2,
        out_shape=[
            jax.ShapeDtypeStruct((quarter, width), x.dtype),
            jax.ShapeDtypeStruct((2 * quarter, width), x.dtype),
        ],
        scratch_shapes=[pltpu.SemaphoreType.DMA((2,))],
        compiler_params=pltpu.CompilerParams(vmem_limit_bytes=VMEM_LIMIT),
        cost_estimate=COST,
        name="cut",
    )(side.reshape(1), after, x)


def columns(t, tile):
    return pl.ds(pl.multiple_of(t * tile, tile), tile)


def put_codes(o_ref, t, at, tile, value, inv_ref, b_ref):
    value = value * inv_ref[0] + b_ref[:, t * tile:(t + 1) * tile].astype(jnp.float32)
    o_ref[:, at * tile:(at + 1) * tile] = jnp.maximum(value, 0.0).astype(jnp.bfloat16)


def encode_first(x, inv, weight, bias, parts):
    rows, width = x.shape
    latents = weight.shape[1]
    tile = tile_of(latents // parts, TILE)
    count = latents // tile
    per = count // parts

    def body(inv_ref, b_ref, x_ref, w_ref, *refs):
        o_refs, held, sem = refs[:parts], refs[parts:parts + count], refs[parts + count]

        def copy(t):
            return pltpu.make_async_copy(w_ref.at[:, t * tile:(t + 1) * tile], held[t], sem.at[t])

        for t in range(count):
            copy(t).start()
        for t in range(count):
            copy(t).wait()
            value = jnp.dot(x_ref[...], held[t][...], preferred_element_type=jnp.float32)
            put_codes(o_refs[t // per], t, t % per, tile, value, inv_ref, b_ref)

    outs = pl.pallas_call(
        body,
        in_specs=[pl.BlockSpec(memory_space=pltpu.SMEM)]
        + [pl.BlockSpec(memory_space=pltpu.VMEM)] * 2 + [pl.BlockSpec(memory_space=pl.ANY)],
        out_specs=[pl.BlockSpec(memory_space=pltpu.VMEM)] * (parts + count),
        out_shape=[jax.ShapeDtypeStruct((rows, latents // parts), jnp.bfloat16)] * parts
        + [pltpu.VMEM((width, tile), weight.dtype)] * count,
        scratch_shapes=[pltpu.SemaphoreType.DMA((count,))],
        compiler_params=pltpu.CompilerParams(vmem_limit_bytes=VMEM_LIMIT),
        cost_estimate=COST,
        name="encode_first",
    )(inv.reshape(1), bias, x, weight)
    return outs[:parts], outs[parts:]


def call_with_held(body, held, specs, operands, out_specs, out_shape, scratch, also, name):
    n, m, k = len(held), len(specs), len(also)
    vmem = pl.BlockSpec(memory_space=pltpu.VMEM)

    def inner(*refs):
        body(refs[:n], *refs[n:n + m], *refs[n + m + k:n + m + k + len(out_specs)],
             *refs[n + m + k + len(out_specs) + n:])

    outs = pl.pallas_call(
        inner,
        in_specs=[vmem] * n + list(specs) + [pl.BlockSpec(memory_space=pl.ANY)] * k,
        out_specs=list(out_specs) + [vmem] * n,
        out_shape=list(out_shape) + [pltpu.VMEM(h.shape, h.dtype) for h in held],
        input_output_aliases={i: len(out_specs) + i for i in range(n)},
        scratch_shapes=scratch,
        compiler_params=pltpu.CompilerParams(vmem_limit_bytes=VMEM_LIMIT),
        cost_estimate=COST,
        name=name,
    )(*[pltpu.with_memory_space_constraint(h, pltpu.VMEM) for h in held], *operands, *also)
    return outs[:len(out_specs)], outs[len(out_specs):]


def encode(pieces, places, inv, held, count, bias, also):
    sizes = [piece.shape[0] for piece in pieces]
    rows = sum(sizes)
    width, tile = held[0].shape
    n = len(pieces)

    def body(held_refs, places_ref, inv_ref, b_ref, *refs):
        x_refs, (o_ref, lhs, sem) = refs[:n], refs[n:]
        copies = []
        for i in range(n):
            place = pl.ds(pl.multiple_of(places_ref[i], 16), sizes[i])
            copies.append(pltpu.make_async_copy(x_refs[i], lhs.at[place], sem.at[i]))
        for copy in copies:
            copy.start()
        for copy in copies:
            copy.wait()

        for t in range(count):
            value = jnp.dot(lhs[...], held_refs[t][...], preferred_element_type=jnp.float32)
            put_codes(o_ref, t, t, tile, value, inv_ref, b_ref)

    outs, held = call_with_held(
        body, held,
        [pl.BlockSpec(memory_space=pltpu.SMEM)] * 2 + [pl.BlockSpec(memory_space=pltpu.VMEM)]
        + [pl.BlockSpec(memory_space=pl.ANY)] * n,
        [places, inv.reshape(1), bias, *pieces],
        [pl.BlockSpec(memory_space=pltpu.VMEM)],
        [jax.ShapeDtypeStruct((rows, count * tile), jnp.bfloat16)],
        [pltpu.VMEM((rows, width), jnp.bfloat16), pltpu.SemaphoreType.DMA((n,))],
        also, "encode")
    return outs[0], held


def decode(codes, earlier, weights, info, outs, width, held, also, mode):
    parts = len(codes)
    rows, part = codes[0].shape
    latents = parts * part
    tile = tile_of(width, TILE)
    per = width // tile
    blocks = info.shape[0] - 1
    count = blocks * per
    slots = SLOTS if mode == "ring" else count

    def body(held_refs, info_ref, *refs):
        refs = list(refs)
        c_refs = [refs.pop(0) for _ in range(parts)]
        e_refs = [refs.pop(0) for _ in range(parts)]
        if mode != "held":
            s_ref, x_ref = refs.pop(0), refs.pop(0)
        o_refs = [refs.pop(0) for _ in outs]
        if mode == "held":
            s_tiles, x_tiles = held_refs[-2:]
        else:
            s_tiles, x_tiles, sem = refs
        later = info_ref[0] != 0

        def copy(source, target, i, t, slot):
            column = info_ref[1 + t // per] * width + lax.rem(t, per) * tile
            across = pl.ds(pl.multiple_of(column, tile), tile)
            return pltpu.make_async_copy(source.at[:, across], target.at[slot], sem.at[i, slot])

        def start(t, slot):
            t = jnp.int32(t)
            copy(s_ref, s_tiles, 0, t, slot).start()

            @pl.when(later)
            def _():
                copy(x_ref, x_tiles, 1, t, slot).start()

        def put(t, value):
            b = t // per
            for (block, many, spans, dtype), o_ref in zip(outs, o_refs):
                @pl.when((b >= block) & (b < block + many))
                def _():
                    here = jnp.clip(b - block, 0, many - 1)
                    at = 0
                    for row, height in spans:
                        o_ref[here, at:at + height, columns(lax.rem(t, per), tile)] = (
                            value[row:row + height].astype(dtype))
                        at += height

        def product(refs, tiles, slot):
            total = None
            for i, ref in enumerate(refs):
                one = jnp.dot(
                    ref[...], tiles[slot, i * part:(i + 1) * part], preferred_element_type=jnp.float32)
                total = one if total is None else total + one
            return total

        def step(t, slot):
            if mode != "held":
                copy(s_ref, s_tiles, 0, t, slot).wait()

            @pl.when(later)
            def _():
                if mode != "held":
                    copy(x_ref, x_tiles, 1, t, slot).wait()
                put(t, product(c_refs, s_tiles, slot) + product(e_refs, x_tiles, slot))

            @pl.when(jnp.logical_not(later))
            def _():
                put(t, product(c_refs, s_tiles, slot))

        if mode != "held":
            for t in range(min(slots, count)):
                start(t, t)

        def turn(t, carry):
            slot = lax.rem(t, slots)
            step(t, slot)
            if mode == "ring":
                @pl.when(t + slots < count)
                def _():
                    start(t + slots, slot)
            return carry

        lax.fori_loop(0, count, turn, 0)

    vmem = pl.BlockSpec(memory_space=pltpu.VMEM)
    out_specs = [vmem] * len(outs)
    out_shape = [
        jax.ShapeDtypeStruct((many, sum(height for _, height in spans), width), dtype)
        for _, many, spans, dtype in outs
    ]
    tiles = (slots, latents, tile)
    scratch = []
    if mode == "ring":
        scratch += [pltpu.VMEM(tiles, jnp.bfloat16)] * 2
    if mode == "keep":
        out_specs += [vmem] * 2
        out_shape += [pltpu.VMEM(tiles, jnp.bfloat16)] * 2
    if mode != "held":
        scratch += [pltpu.SemaphoreType.DMA((2, slots))]
    streamed = [] if mode == "held" else list(weights)
    results, held = call_with_held(
        body, held,
        [pl.BlockSpec(memory_space=pltpu.SMEM)] + [vmem] * (2 * parts)
        + [pl.BlockSpec(memory_space=pl.ANY)] * len(streamed),
        [info, *codes, *earlier, *streamed],
        out_specs, out_shape, scratch, also, "decode_" + mode)
    if mode == "keep":
        results, held = results[:-2], list(held) + list(results[-2:])
    return results, held


def shifted(value, axis, distance):
    n = lax.axis_size(axis)
    return lax.ppermute(value, axis, [(i, (i + distance) % n) for i in range(n)])


def swapped(value, axis, bit):
    n = lax.axis_size(axis)
    return lax.ppermute(value, axis, [(i, i ^ bit) for i in range(n)])


def sum_over(value, axis):
    total = value
    for distance in range(1, lax.axis_size(axis)):
        total = total + shifted(value, axis, distance)
    return total


def wide(value):
    return value.astype(jnp.float32)


def local(inputs, targets, enc_weight, encoder_layer_bias, dec_self, dec_cross, dec_bias):
    layer = lax.axis_index("layer")
    lat = lax.axis_index("latent")
    n_lat = lax.axis_size("latent")
    n_tok = lax.axis_size("token")
    x_own = inputs[0]
    rows, model = x_own.shape
    enc_w = pltpu.with_memory_space_constraint(enc_weight[0], pltpu.HBM)
    own_w = pltpu.with_memory_space_constraint(dec_self[0], pltpu.HBM)
    cross_w = pltpu.with_memory_space_constraint(dec_cross, pltpu.HBM)
    lat_dev = enc_w.shape[1]
    width = dec_bias.shape[1]
    quarter = rows // 4
    side = lat % 2

    square = sum_over(square_sum(x_own), "token")
    scale = jnp.sqrt(square / (rows * n_tok * model) + 1e-06)
    inv = 1.0 / scale
    outer, inner = cut(x_own, side.astype(jnp.int32), inv)
    foreign = []
    for distance in range(1, n_tok):
        mine = shifted(outer, "token", distance)
        theirs = swapped(mine, "latent", 1)
        foreign.append((n_tok - distance, mine, theirs, shifted(inner, "token", distance)))

    bias = lax.dynamic_slice_in_dim(
        encoder_layer_bias, lax.axis_index("token") * lat_dev, lat_dev, axis=1
    )

    group = n_lat // 4
    other, mine_bit = 1 - lat % 2, lat % 2
    far, near = 1 - (lat // 2) % 2, (lat // 2) % 2
    info_sent = jnp.stack(
        [layer] + [4 * i + 2 * b + other for b in (far, near) for i in range(group)]
    ).astype(jnp.int32)
    info_kept = jnp.stack(
        [layer] + [4 * i + 2 * b + mine_bit for b in (far, near) for i in range(group)]
    ).astype(jnp.int32)

    half = 2 * quarter
    both = 2 * group
    narrow = jnp.bfloat16

    def handed(codes):
        return codes, [lax.ppermute(part, "layer", [(0, 1)]) for part in codes]

    def finish(total):
        bit = 4
        while bit < n_lat:
            here = (lat // bit) % 2
            pairs = total.reshape(total.shape[0] // 2, 2, *total.shape[1:])
            away = lax.dynamic_index_in_dim(pairs, 1 - here, 1, keepdims=False)
            arrived = swapped(away.astype(narrow), "latent", bit)
            total = lax.dynamic_index_in_dim(pairs, here, 1, keepdims=False) + wide(arrived)
            bit *= 2
        return total[0]

    weights = (own_w, cross_w)
    codes, held = encode_first(x_own, inv, enc_w, bias, 2)
    codes, n_enc = handed(codes), len(held)
    inside = ((quarter, half),)
    outside = ((0, quarter), (3 * quarter, quarter))
    (sent_in, sent_out), held = decode(
        *codes, weights, info_sent,
        [(0, both, inside, narrow), (0, both, outside, jnp.float32)], width, held, [], "keep")
    there_in = swapped(sent_in, "latent", 1)
    (kept_in, kept_out), held = decode(
        *codes, weights, info_kept,
        [(0, both, inside, jnp.float32), (0, both, outside, jnp.float32)], width, held, [], "ring")
    across_in = (kept_in[:group] + wide(there_in[:group])).astype(narrow)
    total_in = kept_in[group:] + wide(there_in[group:]) + wide(swapped(across_in, "latent", 2))
    whole = ((0, half),)

    sent_back, kept_back = [], []
    for back, mine, theirs, _ in foreign:
        places = jnp.stack([side * quarter, (1 - side) * quarter]).astype(jnp.int32)
        codes, held = encode([mine, theirs], places, inv, held, n_enc, bias, [])
        codes = handed([codes])
        (sent,), held = decode(
            *codes, weights, info_sent, [(0, both, whole, narrow)], width, held, [across_in], "held")
        sent_back.append(shifted(sent, "token", back))
        (kept,), held = decode(
            *codes, weights, info_kept, [(0, both, whole, narrow)], width, held, [], "ring")
        kept_back.append(shifted(kept, "token", back))

    sent_out = (sent_out + sum(wide(part) for part in sent_back)).astype(narrow)
    there_out = swapped(sent_out, "latent", 1)
    returned = []
    for back, _, _, rows_in in foreign:
        codes, held = encode([rows_in], jnp.zeros((1,), jnp.int32), inv, held, n_enc, bias, [])
        codes = handed([codes])
        (far_sent, near_sent), held = decode(
            *codes, weights, info_sent,
            [(0, group, whole, narrow), (group, group, whole, narrow)], width, held, [], "held")
        far_in = swapped(far_sent, "latent", 1)
        near_in = swapped(near_sent, "latent", 1)
        (kept,), held = decode(
            *codes, weights, info_kept, [(0, both, whole, jnp.float32)], width, held,
            [sent_out, total_in], "ring")
        across = (kept[:group] + wide(far_in)).astype(narrow)
        part = finish(kept[group:] + wide(near_in) + wide(swapped(across, "latent", 2)))
        returned.append(shifted(part.astype(narrow), "token", back))

    kept_out = kept_out + sum(wide(part) for part in kept_back) + wide(there_out)
    across_out = swapped(kept_out[:group].astype(narrow), "latent", 2)
    total_out = finish(kept_out[group:] + wide(across_out))
    total_in = finish(total_in) + sum(wide(part) for part in returned)
    total = jnp.concatenate([total_out[:quarter], total_in, total_out[quarter:]])
    total = total + wide(dec_bias)
    recon = total.astype(jnp.bfloat16)[None]

    target = wide(targets[0])
    diff = total - target
    sums = jnp.stack([jnp.sum(diff * diff), jnp.sum(target * target)]).reshape(1, 2)
    sums = sum_over(sum_over(sums, "latent"), "token")
    ratio = sums[:, 0] / sums[:, 1]
    loss = sum_over(ratio, "layer") / 2.0
    return (recon, loss)


def solution(mesh):
    return jax.shard_map(
        local,
        mesh=mesh,
        in_specs=(
            P("layer", ("groups", "token"), None),
            P("layer", ("groups", "token"), "latent"),
            P("layer", None, ("latent", "token")),
            P("layer", "latent"),
            P("layer", ("latent", "token"), None),
            P(("latent", "token"), None),
            P("layer", "latent"),
        ),
        out_specs=(P("layer", ("groups", "token"), "latent"), P("groups")),
        check_vma=False,
    )
```

```python
import jax
import jax.numpy as jnp
from jax import lax
from jax.experimental import pallas as pl
from jax.experimental.pallas import tpu as pltpu
from jax.sharding import PartitionSpec as P

VMEM_LIMIT = 40 * 1024 * 1024
SLOTS = 3
TILE = 512
COST = pl.CostEstimate(flops=0, bytes_accessed=0, transcendentals=0)


def tile_of(size, most):
    tile = min(size, most)
    while size % tile:
        tile //= 2
    return tile


def prepare(x, side):
    rows, width = x.shape
    quarter = rows // 4
    lanes = tile_of(width, 1024)

    def body(side_ref, x_ref, outer_ref, inner_ref, o_ref, held, sem, out_sem):
        def load(i):
            place = pl.ds(i * quarter, quarter)
            return pltpu.make_async_copy(x_ref.at[place], held.at[place], sem.at[i])

        first = pl.ds(pl.multiple_of(side_ref[0] * (3 * quarter), 16), quarter)
        cuts = [
            pltpu.make_async_copy(x_ref.at[first], outer_ref, out_sem.at[0]),
            pltpu.make_async_copy(x_ref.at[pl.ds(quarter, 2 * quarter)], inner_ref, out_sem.at[1]),
        ]
        for i in range(4):
            load(i).start()
        for copy in cuts:
            copy.start()
        total = jnp.zeros((8, lanes), jnp.float32)
        for i in range(4):
            load(i).wait()
            for c in range(width // lanes):
                def add(r, acc):
                    here = pl.ds(pl.multiple_of(i * quarter + r * 16, 16), 16)
                    value = held[here, c * lanes:(c + 1) * lanes].astype(jnp.float32)
                    value = value * value
                    return acc + value[:8] + value[8:]

                total = lax.fori_loop(0, quarter // 16, add, total)
        o_ref[0] = jnp.sum(total)
        for copy in cuts:
            copy.wait()

    return pl.pallas_call(
        body,
        in_specs=[pl.BlockSpec(memory_space=pltpu.SMEM), pl.BlockSpec(memory_space=pl.ANY)],
        out_specs=[pl.BlockSpec(memory_space=pl.ANY)] * 2 + [pl.BlockSpec(memory_space=pltpu.SMEM)],
        out_shape=[
            jax.ShapeDtypeStruct((quarter, width), x.dtype),
            jax.ShapeDtypeStruct((2 * quarter, width), x.dtype),
            jax.ShapeDtypeStruct((1,), jnp.float32),
        ],
        scratch_shapes=[
            pltpu.VMEM((rows, width), x.dtype),
            pltpu.SemaphoreType.DMA((4,)),
            pltpu.SemaphoreType.DMA((2,)),
        ],
        compiler_params=pltpu.CompilerParams(vmem_limit_bytes=VMEM_LIMIT),
        cost_estimate=COST,
        name="prepare",
    )(side.reshape(1), x)


def gate(values, after):
    n = len(values)

    def body(after_ref, *refs):
        pass

    return pl.pallas_call(
        body,
        in_specs=[pl.BlockSpec(memory_space=pltpu.SMEM)] + [pl.BlockSpec(memory_space=pl.ANY)] * n,
        out_specs=[pl.BlockSpec(memory_space=pl.ANY)] * n,
        out_shape=[jax.ShapeDtypeStruct(value.shape, value.dtype) for value in values],
        input_output_aliases={1 + i: i for i in range(n)},
        cost_estimate=COST,
        name="gate",
    )(after, *values)


def ring_loop(count, start, step):
    for t in range(min(SLOTS, count)):
        start(t, t)

    def turn(t, carry):
        slot = lax.rem(t, SLOTS)
        step(t, slot)

        @pl.when(t + SLOTS < count)
        def _():
            start(t + SLOTS, slot)

        return carry

    lax.fori_loop(0, count, turn, 0)


def encode(pieces, places, inv, weight, bias, parts, also):
    rows, width = sum(piece[2] for piece in pieces), pieces[0][0].shape[1]
    latents = weight.shape[1]
    part = latents // parts
    tile = tile_of(part, TILE)
    n, m = len(pieces), len(also)

    def body(places_ref, inv_ref, b_ref, *refs):
        x_refs, w_ref = refs[:n], refs[n]
        o_refs = refs[n + 1 + m:n + 1 + m + parts]
        lhs, ring, lhs_sem, ring_sem = refs[n + 1 + m + parts:]

        def lhs_copy(i):
            _, first, count = pieces[i]
            place = pl.ds(pl.multiple_of(places_ref[i], 16), count)
            return pltpu.make_async_copy(
                x_refs[i].at[pl.ds(first, count)], lhs.at[place], lhs_sem.at[i])

        def columns(t):
            return pl.ds(pl.multiple_of(t * tile, tile), tile)

        def tile_copy(t, slot):
            return pltpu.make_async_copy(w_ref.at[:, columns(t)], ring.at[slot], ring_sem.at[slot])

        for i in range(n):
            lhs_copy(i).start()

        def step(t, slot):
            @pl.when(t == 0)
            def _():
                for i in range(n):
                    lhs_copy(i).wait()

            tile_copy(t, slot).wait()
            value = jnp.dot(lhs[...], ring[slot], preferred_element_type=jnp.float32)
            value = value * inv_ref[0] + b_ref[:, columns(t)].astype(jnp.float32)
            value = jnp.maximum(value, 0.0).astype(jnp.bfloat16)
            per = part // tile
            for i, o_ref in enumerate(o_refs):
                @pl.when(lax.div(t, per) == i)
                def _():
                    o_ref[:, columns(lax.rem(t, per))] = value

        ring_loop(latents // tile, lambda t, slot: tile_copy(t, slot).start(), step)

    return pl.pallas_call(
        body,
        in_specs=[
            pl.BlockSpec(memory_space=pltpu.SMEM),
            pl.BlockSpec(memory_space=pltpu.SMEM),
            pl.BlockSpec(memory_space=pltpu.VMEM),
        ] + [pl.BlockSpec(memory_space=pl.ANY)] * (n + 1 + m),
        out_specs=[pl.BlockSpec(memory_space=pltpu.VMEM)] * parts,
        out_shape=[jax.ShapeDtypeStruct((rows, part), jnp.bfloat16)] * parts,
        scratch_shapes=[
            pltpu.VMEM((rows, width), jnp.bfloat16),
            pltpu.VMEM((SLOTS, width, tile), jnp.bfloat16),
            pltpu.SemaphoreType.DMA((n,)),
            pltpu.SemaphoreType.DMA((SLOTS,)),
        ],
        compiler_params=pltpu.CompilerParams(vmem_limit_bytes=VMEM_LIMIT),
        cost_estimate=COST,
        name="encode",
    )(places, inv, bias, *[piece[0] for piece in pieces], weight, *also)


def decode(codes, earlier, own_w, cross_w, info, outs, width, also):
    parts = len(codes)
    rows, part = codes[0].shape
    latents = parts * part
    tile = tile_of(width, TILE)
    per = width // tile
    blocks = info.shape[0] - 1
    m = len(also)

    def body(info_ref, *refs):
        code_refs, (s_ref, x_ref), refs = refs[:2 * parts], refs[2 * parts:2 * parts + 2], refs[2 * parts + 2:]
        o_refs = refs[m:m + len(outs)]
        lhs, ring, lhs_sem, ring_sem = refs[m + len(outs):]
        later = info_ref[0] != 0

        def lhs_copy(i):
            return pltpu.make_async_copy(
                code_refs[i], lhs.at[:, pl.ds(i * part, part)], lhs_sem.at[i])

        def tile_copy(source, i, t, slot):
            column = info_ref[1 + lax.div(t, per)] * width + lax.rem(t, per) * tile
            across = pl.ds(pl.multiple_of(column, tile), tile)
            return pltpu.make_async_copy(
                source.at[:, across], ring.at[slot, pl.ds(i * latents, latents)], ring_sem.at[slot, i])

        def start(t, slot):
            t = jnp.int32(t)
            tile_copy(s_ref, 0, t, slot).start()

            @pl.when(later)
            def _():
                tile_copy(x_ref, 1, t, slot).start()

        for i in range(parts):
            lhs_copy(i).start()

        @pl.when(later)
        def _():
            for i in range(parts, 2 * parts):
                lhs_copy(i).start()

        def put(t, value):
            b = lax.div(t, per)
            across = pl.ds(pl.multiple_of(lax.rem(t, per) * tile, tile), tile)
            for (block, many, spans, dtype), o_ref in zip(outs, o_refs):
                @pl.when((b >= block) & (b < block + many))
                def _():
                    here = jnp.clip(b - block, 0, many - 1)
                    at = 0
                    for row, height in spans:
                        o_ref[here, at:at + height, across] = value[row:row + height].astype(dtype)
                        at += height

        def step(t, slot):
            @pl.when(t == 0)
            def _():
                for i in range(parts):
                    lhs_copy(i).wait()

            tile_copy(s_ref, 0, t, slot).wait()

            @pl.when(later)
            def _():
                @pl.when(t == 0)
                def _():
                    for i in range(parts, 2 * parts):
                        lhs_copy(i).wait()

                tile_copy(x_ref, 1, t, slot).wait()
                put(t, jnp.dot(lhs[...], ring[slot], preferred_element_type=jnp.float32))

            @pl.when(jnp.logical_not(later))
            def _():
                put(t, jnp.dot(
                    lhs[:, :latents], ring[slot, :latents], preferred_element_type=jnp.float32))

        ring_loop(blocks * per, start, step)

    return pl.pallas_call(
        body,
        in_specs=[pl.BlockSpec(memory_space=pltpu.SMEM)]
        + [pl.BlockSpec(memory_space=pl.ANY)] * (2 * parts + 2 + m),
        out_specs=[pl.BlockSpec(memory_space=pltpu.VMEM)] * len(outs),
        out_shape=[
            jax.ShapeDtypeStruct((many, sum(height for _, height in spans), width), dtype)
            for _, many, spans, dtype in outs
        ],
        scratch_shapes=[
            pltpu.VMEM((rows, 2 * latents), jnp.bfloat16),
            pltpu.VMEM((SLOTS, 2 * latents, tile), jnp.bfloat16),
            pltpu.SemaphoreType.DMA((2 * parts,)),
            pltpu.SemaphoreType.DMA((SLOTS, 2)),
        ],
        compiler_params=pltpu.CompilerParams(vmem_limit_bytes=VMEM_LIMIT),
        cost_estimate=COST,
        name="decode",
    )(info, *codes, *earlier, own_w, cross_w, *also)


def shifted(value, axis, distance):
    n = lax.axis_size(axis)
    return lax.ppermute(value, axis, [(i, (i + distance) % n) for i in range(n)])


def swapped(value, axis, bit):
    n = lax.axis_size(axis)
    return lax.ppermute(value, axis, [(i, i ^ bit) for i in range(n)])


def sum_over(value, axis):
    total = value
    for distance in range(1, lax.axis_size(axis)):
        total = total + shifted(value, axis, distance)
    return total


def in_hbm(value):
    return pltpu.with_memory_space_constraint(value, pltpu.HBM)


def wide(value):
    return value.astype(jnp.float32)


def local(inputs, targets, enc_weight, encoder_layer_bias, dec_self, dec_cross, dec_bias):
    layer = lax.axis_index("layer")
    lat = lax.axis_index("latent")
    n_lat = lax.axis_size("latent")
    n_tok = lax.axis_size("token")
    x_own = in_hbm(inputs[0])
    rows, model = x_own.shape
    enc_w = in_hbm(enc_weight[0])
    own_w = in_hbm(dec_self[0])
    cross_w = in_hbm(dec_cross)
    lat_dev = enc_w.shape[1]
    width = dec_bias.shape[1]
    quarter = rows // 4
    side = lat % 2

    outer, inner, square = prepare(x_own, side.astype(jnp.int32))
    square = sum_over(square, "token")
    scale = jnp.sqrt(square / (rows * n_tok * model) + 1e-06)
    inv = 1.0 / scale
    outer, inner = gate([outer, inner], inv)
    foreign = []
    for distance in range(1, n_tok):
        mine = shifted(outer, "token", distance)
        theirs = swapped(mine, "latent", 1)
        foreign.append((n_tok - distance, mine, theirs, shifted(inner, "token", distance)))

    bias = lax.dynamic_slice_in_dim(
        encoder_layer_bias, lax.axis_index("token") * lat_dev, lat_dev, axis=1
    )

    group = n_lat // 4
    other, mine_bit = 1 - lat % 2, lat % 2
    far, near = 1 - (lat // 2) % 2, (lat // 2) % 2
    info_sent = jnp.stack(
        [layer] + [4 * i + 2 * b + other for b in (far, near) for i in range(group)]
    ).astype(jnp.int32)
    info_kept = jnp.stack(
        [layer] + [4 * i + 2 * b + mine_bit for b in (far, near) for i in range(group)]
    ).astype(jnp.int32)

    half = 2 * quarter
    both = 2 * group
    narrow = jnp.bfloat16

    def earlier_of(codes):
        return [lax.ppermute(part, "layer", [(0, 1)]) for part in codes]

    def places(*rows):
        return jnp.stack([jnp.int32(row) for row in rows])

    def products(codes, earlier, info, outs, also):
        return decode(codes, earlier, own_w, cross_w, info, outs, width, also)

    def finish(total):
        bit = 4
        while bit < n_lat:
            here = (lat // bit) % 2
            pairs = total.reshape(total.shape[0] // 2, 2, *total.shape[1:])
            away = lax.dynamic_index_in_dim(pairs, 1 - here, 1, keepdims=False)
            arrived = swapped(away.astype(narrow), "latent", bit)
            total = lax.dynamic_index_in_dim(pairs, here, 1, keepdims=False) + wide(arrived)
            bit *= 2
        return total[0]

    codes = encode([(x_own, 0, rows)], places(0), inv, enc_w, bias, 2, [])
    earlier = earlier_of(codes)
    inside = ((quarter, half),)
    outside = ((0, quarter), (3 * quarter, quarter))
    sent_in, sent_out = products(
        codes, earlier, info_sent, [(0, both, inside, narrow), (0, both, outside, jnp.float32)], [])
    there_in = swapped(sent_in, "latent", 1)
    kept_in, kept_out = products(
        codes, earlier, info_kept,
        [(0, both, inside, jnp.float32), (0, both, outside, jnp.float32)], [sent_in])
    across_in = (kept_in[:group] + wide(there_in[:group])).astype(narrow)
    total_in = kept_in[group:] + wide(there_in[group:]) + wide(swapped(across_in, "latent", 2))

    inside, outside = ((0, half),), ((half, half),)
    after = across_in
    sent_back, kept_back, parts = [], [], []
    for back, mine, theirs, inner_rows in foreign:
        codes = encode(
            [(inner_rows, 0, half), (mine, 0, quarter), (theirs, 0, quarter)],
            places(0, half + side * quarter, half + (1 - side) * quarter),
            inv, enc_w, bias, 1, [after])
        earlier = earlier_of(codes)
        far_sent, near_sent, sent = products(
            codes, earlier, info_sent,
            [(0, group, inside, narrow), (group, group, inside, narrow), (0, both, outside, narrow)],
            [])
        far_in = swapped(far_sent, "latent", 1)
        sent_back.append(shifted(sent, "token", back))
        near_in = swapped(near_sent, "latent", 1)
        kept, kept_outer = products(
            codes, earlier, info_kept,
            [(0, both, inside, jnp.float32), (0, both, outside, narrow)], [sent, total_in])
        kept_back.append(shifted(kept_outer, "token", back))
        after = kept
        parts.append((back, kept, far_in, near_in))

    returned = []
    for back, kept, far_in, near_in in parts:
        across = (kept[:group] + wide(far_in)).astype(narrow)
        part = finish(kept[group:] + wide(near_in) + wide(swapped(across, "latent", 2)))
        returned.append(shifted(part.astype(narrow), "token", back))

    sent_out = (sent_out + sum(wide(part) for part in sent_back)).astype(narrow)
    far_out = swapped(sent_out[:group], "latent", 1)
    near_out = swapped(sent_out[group:], "latent", 1)
    kept_out = kept_out + sum(wide(part) for part in kept_back)
    across_out = swapped((kept_out[:group] + wide(far_out)).astype(narrow), "latent", 2)
    total_out = finish(kept_out[group:] + wide(near_out) + wide(across_out))
    total_in = finish(total_in) + sum(wide(part) for part in returned)
    total = jnp.concatenate([total_out[:quarter], total_in, total_out[quarter:]])
    total = total + wide(dec_bias)
    recon = total.astype(jnp.bfloat16)[None]

    target = wide(targets[0])
    diff = total - target
    sums = jnp.stack([jnp.sum(diff * diff), jnp.sum(target * target)]).reshape(1, 2)
    sums = sum_over(sum_over(sums, "latent"), "token")
    ratio = sums[:, 0] / sums[:, 1]
    loss = sum_over(ratio, "layer") / 2.0
    return (recon, loss)


def solution(mesh):
    return jax.shard_map(
        local,
        mesh=mesh,
        in_specs=(
            P("layer", ("groups", "token"), None),
            P("layer", ("groups", "token"), "latent"),
            P("layer", None, ("latent", "token")),
            P("layer", "latent"),
            P("layer", ("latent", "token"), None),
            P(("latent", "token"), None),
            P("layer", "latent"),
        ),
        out_specs=(P("layer", ("groups", "token"), "latent"), P("groups")),
        check_vma=False,
    )
```

```python
import jax
import jax.numpy as jnp
from jax import lax
from jax.experimental import pallas as pl
from jax.experimental.pallas import tpu as pltpu
from jax.sharding import PartitionSpec as P

VMEM_LIMIT = 40 * 1024 * 1024
SLOTS = 6
TILE = 256
COST = pl.CostEstimate(flops=0, bytes_accessed=0, transcendentals=0)


def tile_of(size, most):
    tile = min(size, most)
    while size % tile:
        tile //= 2
    return tile


def prepare(x, side, edge):
    rows, width = x.shape
    middle = rows - 2 * edge
    lanes = tile_of(width, 1024)
    loads = 4
    piece = rows // loads

    def body(side_ref, x_ref, outer_ref, inner_ref, o_ref, held, sem, out_sem):
        def load(i):
            place = pl.ds(i * piece, piece)
            return pltpu.make_async_copy(x_ref.at[place], held.at[place], sem.at[i])

        first = pl.ds(pl.multiple_of(side_ref[0] * (rows - edge), 16), edge)
        cuts = [
            pltpu.make_async_copy(x_ref.at[first], outer_ref, out_sem.at[0]),
            pltpu.make_async_copy(x_ref.at[pl.ds(edge, middle)], inner_ref, out_sem.at[1]),
        ]
        for i in range(loads):
            load(i).start()
        for copy in cuts:
            copy.start()
        total = jnp.zeros((8, lanes), jnp.float32)
        for i in range(loads):
            load(i).wait()
            for c in range(width // lanes):
                def add(r, acc):
                    here = pl.ds(pl.multiple_of(i * piece + r * 16, 16), 16)
                    value = held[here, c * lanes:(c + 1) * lanes].astype(jnp.float32)
                    value = value * value
                    return acc + value[:8] + value[8:]

                total = lax.fori_loop(0, piece // 16, add, total, unroll=2)
        o_ref[0] = jnp.sum(total)
        for copy in cuts:
            copy.wait()

    return pl.pallas_call(
        body,
        in_specs=[pl.BlockSpec(memory_space=pltpu.SMEM), pl.BlockSpec(memory_space=pl.ANY)],
        out_specs=[pl.BlockSpec(memory_space=pl.ANY)] * 2 + [pl.BlockSpec(memory_space=pltpu.SMEM)],
        out_shape=[
            pltpu.HBM((edge, width), x.dtype),
            pltpu.HBM((middle, width), x.dtype),
            jax.ShapeDtypeStruct((1,), jnp.float32),
        ],
        scratch_shapes=[
            pltpu.VMEM((rows, width), x.dtype),
            pltpu.SemaphoreType.DMA((loads,)),
            pltpu.SemaphoreType.DMA((2,)),
        ],
        compiler_params=pltpu.CompilerParams(vmem_limit_bytes=VMEM_LIMIT),
        cost_estimate=COST,
        name="prepare",
    )(side.reshape(1), x)


def gate(values, after):
    n = len(values)

    def body(after_ref, *refs):
        pass

    return pl.pallas_call(
        body,
        in_specs=[pl.BlockSpec(memory_space=pltpu.SMEM)] + [pl.BlockSpec(memory_space=pl.ANY)] * n,
        out_specs=[pl.BlockSpec(memory_space=pl.ANY)] * n,
        out_shape=[pltpu.HBM(value.shape, value.dtype) for value in values],
        input_output_aliases={1 + i: i for i in range(n)},
        cost_estimate=COST,
        name="gate",
    )(after, *[in_hbm(value) for value in values])


def ring_loop(count, start, step):
    for t in range(min(SLOTS, count)):
        start(t, t)

    def turn(t, carry):
        slot = lax.rem(t, SLOTS)
        step(t, slot)

        @pl.when(t + SLOTS < count)
        def _():
            start(t + SLOTS, slot)

        return carry

    lax.fori_loop(0, count, turn, 0)


def encode(pieces, places, inv, weight, bias, parts, also):
    rows, width = sum(piece[2] for piece in pieces), pieces[0][0].shape[1]
    latents = weight.shape[1]
    part = latents // parts
    tile = tile_of(part, TILE)
    n, m = len(pieces), len(also)

    def body(places_ref, inv_ref, b_ref, *refs):
        x_refs, w_ref = refs[:n], refs[n]
        o_refs = refs[n + 1 + m:n + 1 + m + parts]
        lhs, ring, lhs_sem, ring_sem = refs[n + 1 + m + parts:]

        def lhs_copy(i):
            _, first, count = pieces[i]
            place = pl.ds(pl.multiple_of(places_ref[i], 16), count)
            return pltpu.make_async_copy(
                x_refs[i].at[pl.ds(first, count)], lhs.at[place], lhs_sem.at[i])

        def columns(t):
            return pl.ds(pl.multiple_of(t * tile, tile), tile)

        def tile_copy(t, slot):
            return pltpu.make_async_copy(w_ref.at[:, columns(t)], ring.at[slot], ring_sem.at[slot])

        for i in range(n):
            lhs_copy(i).start()

        def step(t, slot):
            @pl.when(t == 0)
            def _():
                for i in range(n):
                    lhs_copy(i).wait()

            tile_copy(t, slot).wait()
            value = jnp.dot(lhs[...], ring[slot], preferred_element_type=jnp.float32)
            value = value * inv_ref[0] + b_ref[:, columns(t)].astype(jnp.float32)
            value = jnp.maximum(value, 0.0).astype(jnp.bfloat16)
            per = part // tile
            for i, o_ref in enumerate(o_refs):
                @pl.when(lax.div(t, per) == i)
                def _():
                    o_ref[:, columns(lax.rem(t, per))] = value

        ring_loop(latents // tile, lambda t, slot: tile_copy(t, slot).start(), step)

    return pl.pallas_call(
        body,
        in_specs=[
            pl.BlockSpec(memory_space=pltpu.SMEM),
            pl.BlockSpec(memory_space=pltpu.SMEM),
            pl.BlockSpec(memory_space=pltpu.VMEM),
        ] + [pl.BlockSpec(memory_space=pl.ANY)] * (n + 1 + m),
        out_specs=[pl.BlockSpec(memory_space=pltpu.VMEM)] * parts,
        out_shape=[jax.ShapeDtypeStruct((rows, part), jnp.bfloat16)] * parts,
        scratch_shapes=[
            pltpu.VMEM((rows, width), jnp.bfloat16),
            pltpu.VMEM((SLOTS, width, tile), jnp.bfloat16),
            pltpu.SemaphoreType.DMA((n,)),
            pltpu.SemaphoreType.DMA((SLOTS,)),
        ],
        compiler_params=pltpu.CompilerParams(vmem_limit_bytes=VMEM_LIMIT),
        cost_estimate=COST,
        name="encode",
    )(places, inv, bias, *[piece[0] for piece in pieces], weight, *also)


def decode(codes, earlier, own_w, cross_w, info, outs, width, also):
    parts = len(codes)
    rows, part = codes[0].shape
    latents = parts * part
    tile = tile_of(width, TILE)
    per = width // tile
    blocks = info.shape[0] - 1
    m = len(also)

    def body(info_ref, *refs):
        code_refs, (s_ref, x_ref), refs = refs[:2 * parts], refs[2 * parts:2 * parts + 2], refs[2 * parts + 2:]
        o_refs = refs[m:m + len(outs)]
        lhs, ring, lhs_sem, ring_sem = refs[m + len(outs):]
        later = info_ref[0] != 0

        def lhs_copy(i):
            return pltpu.make_async_copy(
                code_refs[i], lhs.at[:, pl.ds(i * part, part)], lhs_sem.at[i])

        def tile_copy(source, i, t, slot):
            column = info_ref[1 + lax.div(t, per)] * width + lax.rem(t, per) * tile
            across = pl.ds(pl.multiple_of(column, tile), tile)
            return pltpu.make_async_copy(
                source.at[:, across], ring.at[slot, pl.ds(i * latents, latents)], ring_sem.at[slot, i])

        def start(t, slot):
            t = jnp.int32(t)
            tile_copy(s_ref, 0, t, slot).start()

            @pl.when(later)
            def _():
                tile_copy(x_ref, 1, t, slot).start()

        for i in range(parts):
            lhs_copy(i).start()

        @pl.when(later)
        def _():
            for i in range(parts, 2 * parts):
                lhs_copy(i).start()

        def put(t, value):
            b = lax.div(t, per)
            across = pl.ds(pl.multiple_of(lax.rem(t, per) * tile, tile), tile)
            for (block, many, spans, dtype), o_ref in zip(outs, o_refs):
                @pl.when((b >= block) & (b < block + many))
                def _():
                    here = jnp.clip(b - block, 0, many - 1)
                    at = 0
                    for row, height in spans:
                        o_ref[here, at:at + height, across] = value[row:row + height].astype(dtype)
                        at += height

        def step(t, slot):
            @pl.when(t == 0)
            def _():
                for i in range(parts):
                    lhs_copy(i).wait()

            tile_copy(s_ref, 0, t, slot).wait()

            @pl.when(later)
            def _():
                @pl.when(t == 0)
                def _():
                    for i in range(parts, 2 * parts):
                        lhs_copy(i).wait()

                tile_copy(x_ref, 1, t, slot).wait()
                put(t, jnp.dot(lhs[...], ring[slot], preferred_element_type=jnp.float32))

            @pl.when(jnp.logical_not(later))
            def _():
                put(t, jnp.dot(
                    lhs[:, :latents], ring[slot, :latents], preferred_element_type=jnp.float32))

        ring_loop(blocks * per, start, step)

    return pl.pallas_call(
        body,
        in_specs=[pl.BlockSpec(memory_space=pltpu.SMEM)]
        + [pl.BlockSpec(memory_space=pl.ANY)] * (2 * parts + 2 + m),
        out_specs=[pl.BlockSpec(memory_space=pltpu.VMEM)] * len(outs),
        out_shape=[
            jax.ShapeDtypeStruct((many, sum(height for _, height in spans), width), dtype)
            for _, many, spans, dtype in outs
        ],
        scratch_shapes=[
            pltpu.VMEM((rows, 2 * latents), jnp.bfloat16),
            pltpu.VMEM((SLOTS, 2 * latents, tile), jnp.bfloat16),
            pltpu.SemaphoreType.DMA((2 * parts,)),
            pltpu.SemaphoreType.DMA((SLOTS, 2)),
        ],
        compiler_params=pltpu.CompilerParams(vmem_limit_bytes=VMEM_LIMIT),
        cost_estimate=COST,
        name="decode",
    )(info, *codes, *earlier, own_w, cross_w, *also)


def finale(outer_terms, inner_terms, bias, target, layer):
    rows, width = target.shape
    half, quarter = rows // 2, rows // 4
    n, m = len(outer_terms), len(inner_terms)

    def body(layer_ref, b_ref, t_ref, *refs):
        terms = {0: refs[:n], 1: refs[n:n + m]}
        r_ref, s_ref = refs[n + m:]
        bias = b_ref[...].astype(jnp.float32)
        spans = [(0, 0, 0, quarter), (1, 0, quarter, half), (0, quarter, 3 * quarter, quarter)]

        def block(which, start, target_start):
            def run(r, sums):
                here = pl.ds(pl.multiple_of(start + r * 16, 16), 16)
                there = pl.ds(pl.multiple_of(target_start + r * 16, 16), 16)
                total = sum(term[here, :].astype(jnp.float32) for term in terms[which]) + bias
                goal = t_ref[there, :].astype(jnp.float32)
                r_ref[there, :] = total.astype(r_ref.dtype)
                diff = total - goal
                diff, goal = diff * diff, goal * goal
                return sums[0] + diff[:8] + diff[8:], sums[1] + goal[:8] + goal[8:]

            return run

        zero = jnp.zeros((8, width), jnp.float32)
        sums = (zero, zero)
        for which, start, target_start, count in spans:
            sums = lax.fori_loop(0, count // 16, block(which, start, target_start), sums)
        lane = lax.broadcasted_iota(jnp.int32, (8, 128), 1)
        value = jnp.where(lane == layer_ref[0], jnp.sum(sums[0]), 0.0)
        s_ref[...] = jnp.where(lane == layer_ref[0] + 2, jnp.sum(sums[1]), value)

    vmem = pl.BlockSpec(memory_space=pltpu.VMEM)
    return pl.pallas_call(
        body,
        in_specs=[pl.BlockSpec(memory_space=pltpu.SMEM)] + [vmem] * (2 + n + m),
        out_specs=[vmem] * 2,
        out_shape=[
            jax.ShapeDtypeStruct((rows, width), jnp.bfloat16),
            jax.ShapeDtypeStruct((8, 128), jnp.float32),
        ],
        compiler_params=pltpu.CompilerParams(vmem_limit_bytes=VMEM_LIMIT),
        cost_estimate=COST,
        name="finale",
    )(layer.astype(jnp.int32).reshape(1), bias, target, *outer_terms, *inner_terms)


def shifted(value, axis, distance):
    n = lax.axis_size(axis)
    return lax.ppermute(value, axis, [(i, (i + distance) % n) for i in range(n)])


def swapped(value, axis, bit):
    n = lax.axis_size(axis)
    return lax.ppermute(value, axis, [(i, i ^ bit) for i in range(n)])


def sum_over(value, axis):
    total = value
    for distance in range(1, lax.axis_size(axis)):
        total = total + shifted(value, axis, distance)
    return total


def in_hbm(value):
    return pltpu.with_memory_space_constraint(value, pltpu.HBM)


def wide(value):
    return value.astype(jnp.float32)


def local(inputs, targets, enc_weight, encoder_layer_bias, dec_self, dec_cross, dec_bias):
    layer = lax.axis_index("layer")
    lat = lax.axis_index("latent")
    n_lat = lax.axis_size("latent")
    n_tok = lax.axis_size("token")
    x_own = in_hbm(inputs[0])
    rows, model = x_own.shape
    enc_w = in_hbm(enc_weight[0])
    own_w = in_hbm(dec_self[0])
    cross_w = in_hbm(dec_cross)
    lat_dev = enc_w.shape[1]
    width = dec_bias.shape[1]
    quarter = rows // 4
    side = lat % 2

    edge = rows * 7 // 24 // 16 * 16
    outer, inner, square = prepare(x_own, side.astype(jnp.int32), edge)
    square = sum_over(square, "token")
    scale = jnp.sqrt(square / (rows * n_tok * model) + 1e-06)
    inv = 1.0 / scale
    outer, inner = gate([outer, inner], inv)
    foreign = []
    for distance in range(1, n_tok):
        mine = shifted(outer, "token", distance)
        theirs = swapped(mine, "latent", 1)
        foreign.append((n_tok - distance, mine, theirs, shifted(inner, "token", distance)))

    bias = lax.dynamic_slice_in_dim(
        encoder_layer_bias, lax.axis_index("token") * lat_dev, lat_dev, axis=1
    )

    group = n_lat // 4
    other, mine_bit = 1 - lat % 2, lat % 2
    far, near = 1 - (lat // 2) % 2, (lat // 2) % 2

    def info(low, highs):
        blocks = [4 * i + 2 * high + low for high in highs for i in range(group)]
        return jnp.stack([layer] + blocks).astype(jnp.int32)


    half = 2 * quarter
    both = 2 * group
    narrow = jnp.bfloat16

    def earlier_of(codes):
        return [lax.ppermute(part, "layer", [(0, 1)]) for part in codes]

    def places(*rows):
        return jnp.stack([jnp.int32(row) for row in rows])

    def products(codes, earlier, info, outs, also):
        return decode(codes, earlier, own_w, cross_w, info, outs, width, also)

    def finish(total):
        bit = 4
        while bit < n_lat:
            here = (lat // bit) % 2
            pairs = total.reshape(total.shape[0] // 2, 2, *total.shape[1:])
            away = lax.dynamic_index_in_dim(pairs, 1 - here, 1, keepdims=False)
            arrived = swapped(away.astype(narrow), "latent", bit)
            total = lax.dynamic_index_in_dim(pairs, here, 1, keepdims=False) + wide(arrived)
            bit *= 2
        return total[0]

    codes = encode([(x_own, 0, rows)], places(0), inv, enc_w, bias, 2, [])
    earlier = earlier_of(codes)
    inside = ((quarter, half),)
    outside = ((0, quarter), (3 * quarter, quarter))
    spans = [(0, group, inside), (group, group, inside), (0, group, outside), (group, group, outside)]
    far_sent, near_sent, far_out_sent, near_out_sent = products(
        codes, earlier, info(other, (far, near)),
        [span + (dtype,) for span, dtype in zip(spans, (narrow, narrow, jnp.float32, jnp.float32))], [])
    far_in = swapped(far_sent, "latent", 1)
    near_in = swapped(near_sent, "latent", 1)
    far_kept, near_kept, far_out_kept, near_out_kept = products(
        codes, earlier, info(mine_bit, (far, near)), [span + (jnp.float32,) for span in spans], [far_sent])
    across_in = (far_kept + wide(far_in)).astype(narrow)
    total_in = near_kept + wide(near_in) + wide(swapped(across_in, "latent", 2))

    after = across_in
    returned = []
    far_out_back, far_out_kept_back, near_out_back, near_out_kept_back = [], [], [], []

    for back, mine, theirs, inner_rows in foreign:
        codes = encode(
            [(mine, 0, edge), (theirs, 0, edge), (inner_rows, 0, rows - 2 * edge)],
            places(side * (rows - edge), (1 - side) * (rows - edge), edge),
            inv, enc_w, bias, 1, [after])
        earlier = earlier_of(codes)

        def quarter_of(low, high, spans, dtype, also):
            *insides, outer = products(
                codes, earlier, info(low, (high,)),
                [(0, group, span, dtype) for span in spans] + [(0, group, outside, narrow)], also)
            return insides, shifted(outer, "token", back)

        (far_sent,), far_back = quarter_of(other, far, [inside], narrow, [])
        far_in = swapped(far_sent, "latent", 1)
        (far_kept,), far_kept_back = quarter_of(mine_bit, far, [inside], jnp.float32, [far_sent, total_in])
        across = (far_kept + wide(far_in)).astype(narrow)
        halves = [((quarter, quarter),), ((2 * quarter, quarter),)]
        near_sent, near_back = quarter_of(other, near, halves, narrow, [across])
        near_in = jnp.concatenate([swapped(part, "latent", 1) for part in near_sent], axis=1)
        (near_kept,), near_kept_back = quarter_of(mine_bit, near, [inside], jnp.float32, near_sent)
        part = finish(near_kept + wide(near_in) + wide(swapped(across, "latent", 2)))
        returned.append(shifted(part.astype(narrow), "token", back))
        far_out_back.append(far_back)
        far_out_kept_back.append(far_kept_back)
        near_out_back.append(near_back)
        near_out_kept_back.append(near_kept_back)
        after = near_kept

    def joined(own, back):
        return own + sum(wide(part) for part in back)

    far_out = swapped(joined(far_out_sent, far_out_back).astype(narrow), "latent", 1)
    near_out = swapped(joined(near_out_sent, near_out_back).astype(narrow), "latent", 1)
    across_out = (joined(far_out_kept, far_out_kept_back) + wide(far_out)).astype(narrow)
    across_out = swapped(across_out, "latent", 2)
    if group == 1:
        outer_terms = [near_out_kept, *near_out_kept_back, near_out, across_out]
        outer_terms = [term[0] for term in outer_terms]
    else:
        outer_terms = [finish(joined(near_out_kept, near_out_kept_back) + wide(near_out) + wide(across_out))]
    recon, sums = finale(outer_terms, [finish(total_in), *returned], dec_bias, targets[0], layer)

    sums = sum_over(sum_over(sums, ("token", "layer")), "latent")
    loss = (sums[:1, 0] / sums[:1, 2] + sums[:1, 1] / sums[:1, 3]) / 2.0
    return (recon[None], loss)


def solution(mesh):
    return jax.shard_map(
        local,
        mesh=mesh,
        in_specs=(
            P("layer", ("groups", "token"), None),
            P("layer", ("groups", "token"), "latent"),
            P("layer", None, ("latent", "token")),
            P("layer", "latent"),
            P("layer", ("latent", "token"), None),
            P(("latent", "token"), None),
            P("layer", "latent"),
        ),
        out_specs=(P("layer", ("groups", "token"), "latent"), P("groups")),
        check_vma=False,
    )
```

```python
import jax
import jax.numpy as jnp
from jax import lax
from jax.experimental import pallas as pl
from jax.experimental.pallas import tpu as pltpu
from jax.sharding import PartitionSpec as P

VMEM_LIMIT = 28 * 1024 * 1024
ENCODE_TILE, ENCODE_SLOTS = 512, 3
DECODE_TILE, DECODE_SLOTS = 256, 6
COST = pl.CostEstimate(flops=0, bytes_accessed=0, transcendentals=0)


def tile_of(size, most):
    tile = min(size, most)
    while size % tile:
        tile //= 2
    return tile


def prepare(x, side, edge):
    rows, width = x.shape
    middle = rows - 2 * edge
    lanes = tile_of(width, 1024)
    loads = 4
    piece = rows // loads

    def body(side_ref, x_ref, outer_ref, inner_ref, o_ref, held, sem, out_sem):
        def load(i):
            place = pl.ds(i * piece, piece)
            return pltpu.make_async_copy(x_ref.at[place], held.at[place], sem.at[i])

        first = pl.ds(pl.multiple_of(side_ref[0] * (rows - edge), 16), edge)
        cuts = [
            pltpu.make_async_copy(held.at[first], outer_ref, out_sem.at[0]),
            pltpu.make_async_copy(held.at[pl.ds(edge, middle)], inner_ref, out_sem.at[1]),
        ]
        for i in range(loads):
            load(i).start()
        total = jnp.zeros((8, lanes), jnp.float32)
        for i in range(loads):
            load(i).wait()
            for c in range(width // lanes):
                def add(r, acc):
                    here = pl.ds(pl.multiple_of(i * piece + r * 16, 16), 16)
                    value = held[here, c * lanes:(c + 1) * lanes].astype(jnp.float32)
                    value = value * value
                    return acc + value[:8] + value[8:]

                total = lax.fori_loop(0, piece // 16, add, total, unroll=2)
        for copy in cuts:
            copy.start()
        o_ref[0] = jnp.sum(total)
        for copy in cuts:
            copy.wait()

    return pl.pallas_call(
        body,
        in_specs=[pl.BlockSpec(memory_space=pltpu.SMEM), pl.BlockSpec(memory_space=pl.ANY)],
        out_specs=[pl.BlockSpec(memory_space=pl.ANY)] * 2 + [pl.BlockSpec(memory_space=pltpu.SMEM)],
        out_shape=[
            pltpu.HBM((edge, width), x.dtype),
            pltpu.HBM((middle, width), x.dtype),
            jax.ShapeDtypeStruct((1,), jnp.float32),
        ],
        scratch_shapes=[
            pltpu.VMEM((rows, width), x.dtype),
            pltpu.SemaphoreType.DMA((loads,)),
            pltpu.SemaphoreType.DMA((2,)),
        ],
        compiler_params=pltpu.CompilerParams(vmem_limit_bytes=VMEM_LIMIT),
        cost_estimate=COST,
        name="prepare",
    )(side.reshape(1), x)


def gate(values, after):
    n = len(values)

    def body(after_ref, *refs):
        pass

    return pl.pallas_call(
        body,
        in_specs=[pl.BlockSpec(memory_space=pltpu.SMEM)] + [pl.BlockSpec(memory_space=pl.ANY)] * n,
        out_specs=[pl.BlockSpec(memory_space=pl.ANY)] * n,
        out_shape=[pltpu.HBM(value.shape, value.dtype) for value in values],
        input_output_aliases={1 + i: i for i in range(n)},
        cost_estimate=COST,
        name="gate",
    )(after, *[in_hbm(value) for value in values])


def ring_loop(count, slots, start, step):
    for t in range(min(slots, count)):
        start(t, t)

    def turn(t, carry):
        slot = lax.rem(t, slots)
        step(t, slot)

        @pl.when(t + slots < count)
        def _():
            start(t + slots, slot)

        return carry

    lax.fori_loop(0, count, turn, 0)


def encode(pieces, places, inv, weight, bias, parts, also):
    rows, width = sum(piece[2] for piece in pieces), pieces[0][0].shape[1]
    latents = weight.shape[1]
    part = latents // parts
    tile = tile_of(part, ENCODE_TILE)
    n, m = len(pieces), len(also)

    def body(places_ref, inv_ref, b_ref, *refs):
        x_refs, w_ref = refs[:n], refs[n]
        o_refs = refs[n + 1 + m:n + 1 + m + parts]
        lhs, ring, lhs_sem, ring_sem = refs[n + 1 + m + parts:]

        def lhs_copy(i):
            _, first, count = pieces[i]
            place = pl.ds(pl.multiple_of(places_ref[i], 16), count)
            return pltpu.make_async_copy(
                x_refs[i].at[pl.ds(first, count)], lhs.at[place], lhs_sem.at[i])

        def columns(t):
            return pl.ds(pl.multiple_of(t * tile, tile), tile)

        def tile_copy(t, slot):
            return pltpu.make_async_copy(w_ref.at[:, columns(t)], ring.at[slot], ring_sem.at[slot])

        for i in range(n):
            lhs_copy(i).start()

        def step(t, slot):
            @pl.when(t == 0)
            def _():
                for i in range(n):
                    lhs_copy(i).wait()

            tile_copy(t, slot).wait()
            value = jnp.dot(lhs[...], ring[slot], preferred_element_type=jnp.float32)
            value = value * inv_ref[0] + b_ref[:, columns(t)].astype(jnp.float32)
            value = jnp.maximum(value, 0.0).astype(jnp.bfloat16)
            per = part // tile
            for i, o_ref in enumerate(o_refs):
                @pl.when(lax.div(t, per) == i)
                def _():
                    o_ref[:, columns(lax.rem(t, per))] = value

        ring_loop(latents // tile, ENCODE_SLOTS, lambda t, slot: tile_copy(t, slot).start(), step)

    return pl.pallas_call(
        body,
        in_specs=[
            pl.BlockSpec(memory_space=pltpu.SMEM),
            pl.BlockSpec(memory_space=pltpu.SMEM),
            pl.BlockSpec(memory_space=pltpu.VMEM),
        ] + [pl.BlockSpec(memory_space=pl.ANY)] * (n + 1 + m),
        out_specs=[pl.BlockSpec(memory_space=pltpu.VMEM)] * parts,
        out_shape=[jax.ShapeDtypeStruct((rows, part), jnp.bfloat16)] * parts,
        scratch_shapes=[
            pltpu.VMEM((rows, width), jnp.bfloat16),
            pltpu.VMEM((ENCODE_SLOTS, width, tile), jnp.bfloat16),
            pltpu.SemaphoreType.DMA((n,)),
            pltpu.SemaphoreType.DMA((ENCODE_SLOTS,)),
        ],
        compiler_params=pltpu.CompilerParams(vmem_limit_bytes=VMEM_LIMIT),
        cost_estimate=COST,
        name="encode",
    )(places, inv, bias, *[piece[0] for piece in pieces], weight, *also)


def decode(codes, earlier, own_w, cross_w, info, outs, width, also):
    parts = len(codes)
    rows, part = codes[0].shape
    latents = parts * part
    tile = tile_of(width, DECODE_TILE)
    per = width // tile
    blocks = info.shape[0] - 1
    m = len(also)

    def body(info_ref, *refs):
        code_refs, (s_ref, x_ref), refs = refs[:2 * parts], refs[2 * parts:2 * parts + 2], refs[2 * parts + 2:]
        o_refs = refs[m:m + len(outs)]
        lhs, ring, lhs_sem, ring_sem = refs[m + len(outs):]
        later = info_ref[0] != 0

        def lhs_copy(i):
            return pltpu.make_async_copy(
                code_refs[i], lhs.at[:, pl.ds(i * part, part)], lhs_sem.at[i])

        def tile_copy(source, i, t, slot):
            column = info_ref[1 + lax.div(t, per)] * width + lax.rem(t, per) * tile
            across = pl.ds(pl.multiple_of(column, tile), tile)
            return pltpu.make_async_copy(
                source.at[:, across], ring.at[slot, pl.ds(i * latents, latents)], ring_sem.at[slot, i])

        def start(t, slot):
            t = jnp.int32(t)
            tile_copy(s_ref, 0, t, slot).start()

            @pl.when(later)
            def _():
                tile_copy(x_ref, 1, t, slot).start()

        for i in range(parts):
            lhs_copy(i).start()

        @pl.when(later)
        def _():
            for i in range(parts, 2 * parts):
                lhs_copy(i).start()

        def put(t, value):
            b = lax.div(t, per)
            across = pl.ds(pl.multiple_of(lax.rem(t, per) * tile, tile), tile)
            for (block, many, spans, dtype), o_ref in zip(outs, o_refs):
                @pl.when((b >= block) & (b < block + many))
                def _():
                    here = jnp.clip(b - block, 0, many - 1)
                    at = 0
                    for row, height in spans:
                        o_ref[here, at:at + height, across] = value[row:row + height].astype(dtype)
                        at += height

        def step(t, slot):
            @pl.when(t == 0)
            def _():
                for i in range(parts):
                    lhs_copy(i).wait()

            tile_copy(s_ref, 0, t, slot).wait()

            @pl.when(later)
            def _():
                @pl.when(t == 0)
                def _():
                    for i in range(parts, 2 * parts):
                        lhs_copy(i).wait()

                tile_copy(x_ref, 1, t, slot).wait()
                put(t, jnp.dot(lhs[...], ring[slot], preferred_element_type=jnp.float32))

            @pl.when(jnp.logical_not(later))
            def _():
                put(t, jnp.dot(
                    lhs[:, :latents], ring[slot, :latents], preferred_element_type=jnp.float32))

        ring_loop(blocks * per, DECODE_SLOTS, start, step)

    return pl.pallas_call(
        body,
        in_specs=[pl.BlockSpec(memory_space=pltpu.SMEM)]
        + [pl.BlockSpec(memory_space=pl.ANY)] * (2 * parts + 2 + m),
        out_specs=[pl.BlockSpec(memory_space=pltpu.VMEM)] * len(outs),
        out_shape=[
            jax.ShapeDtypeStruct((many, sum(height for _, height in spans), width), dtype)
            for _, many, spans, dtype in outs
        ],
        scratch_shapes=[
            pltpu.VMEM((rows, 2 * latents), jnp.bfloat16),
            pltpu.VMEM((DECODE_SLOTS, 2 * latents, tile), jnp.bfloat16),
            pltpu.SemaphoreType.DMA((2 * parts,)),
            pltpu.SemaphoreType.DMA((DECODE_SLOTS, 2)),
        ],
        compiler_params=pltpu.CompilerParams(vmem_limit_bytes=VMEM_LIMIT),
        cost_estimate=COST,
        name="decode",
    )(info, *codes, *earlier, own_w, cross_w, *also)


def finale(outer_terms, inner_terms, bias, target, layer):
    rows, width = target.shape
    half, quarter = rows // 2, rows // 4
    n, m = len(outer_terms), len(inner_terms)

    def body(layer_ref, b_ref, t_ref, *refs):
        terms = {0: refs[:n], 1: refs[n:n + m]}
        r_ref, s_ref = refs[n + m:]
        bias = b_ref[...].astype(jnp.float32)
        spans = [(0, 0, 0, quarter), (1, 0, quarter, half), (0, quarter, 3 * quarter, quarter)]

        def block(which, start, target_start):
            def run(r, sums):
                here = pl.ds(pl.multiple_of(start + r * 16, 16), 16)
                there = pl.ds(pl.multiple_of(target_start + r * 16, 16), 16)
                total = sum(term[here, :].astype(jnp.float32) for term in terms[which]) + bias
                goal = t_ref[there, :].astype(jnp.float32)
                r_ref[there, :] = total.astype(r_ref.dtype)
                diff = total - goal
                diff, goal = diff * diff, goal * goal
                return sums[0] + diff[:8] + diff[8:], sums[1] + goal[:8] + goal[8:]

            return run

        zero = jnp.zeros((8, width), jnp.float32)
        sums = (zero, zero)
        for which, start, target_start, count in spans:
            sums = lax.fori_loop(0, count // 16, block(which, start, target_start), sums)
        lane = lax.broadcasted_iota(jnp.int32, (8, 128), 1)
        value = jnp.where(lane == layer_ref[0], jnp.sum(sums[0]), 0.0)
        s_ref[...] = jnp.where(lane == layer_ref[0] + 2, jnp.sum(sums[1]), value)

    vmem = pl.BlockSpec(memory_space=pltpu.VMEM)
    return pl.pallas_call(
        body,
        in_specs=[pl.BlockSpec(memory_space=pltpu.SMEM)] + [vmem] * (2 + n + m),
        out_specs=[vmem] * 2,
        out_shape=[
            jax.ShapeDtypeStruct((rows, width), jnp.bfloat16),
            jax.ShapeDtypeStruct((8, 128), jnp.float32),
        ],
        compiler_params=pltpu.CompilerParams(vmem_limit_bytes=VMEM_LIMIT),
        cost_estimate=COST,
        name="finale",
    )(layer.astype(jnp.int32).reshape(1), bias, target, *outer_terms, *inner_terms)


def shifted(value, axis, distance):
    n = lax.axis_size(axis)
    return lax.ppermute(value, axis, [(i, (i + distance) % n) for i in range(n)])


def swapped(value, axis, bit):
    n = lax.axis_size(axis)
    return lax.ppermute(value, axis, [(i, i ^ bit) for i in range(n)])


def sum_over(value, axis):
    total = value
    for distance in range(1, lax.axis_size(axis)):
        total = total + shifted(value, axis, distance)
    return total


def in_hbm(value):
    return pltpu.with_memory_space_constraint(value, pltpu.HBM)


def wide(value):
    return value.astype(jnp.float32)


def local(inputs, targets, enc_weight, encoder_layer_bias, dec_self, dec_cross, dec_bias):
    layer = lax.axis_index("layer")
    lat = lax.axis_index("latent")
    n_lat = lax.axis_size("latent")
    n_tok = lax.axis_size("token")
    x_own = in_hbm(inputs[0])
    rows, model = x_own.shape
    enc_w = in_hbm(enc_weight[0])
    own_w = in_hbm(dec_self[0])
    cross_w = in_hbm(dec_cross)
    lat_dev = enc_w.shape[1]
    width = dec_bias.shape[1]
    quarter = rows // 4
    side = lat % 2

    edge = rows * 7 // 24 // 16 * 16
    outer, inner, square = prepare(x_own, side.astype(jnp.int32), edge)
    square = sum_over(square, "token")
    scale = jnp.sqrt(square / (rows * n_tok * model) + 1e-06)
    inv = 1.0 / scale
    outer, inner = gate([outer, inner], inv)
    foreign = []
    for distance in range(1, n_tok):
        mine = shifted(outer, "token", distance)
        theirs = swapped(mine, "latent", 1)
        foreign.append((n_tok - distance, mine, theirs, shifted(inner, "token", distance)))

    bias = lax.dynamic_slice_in_dim(
        encoder_layer_bias, lax.axis_index("token") * lat_dev, lat_dev, axis=1
    )

    group = n_lat // 4
    other, mine_bit = 1 - lat % 2, lat % 2
    far, near = 1 - (lat // 2) % 2, (lat // 2) % 2

    def info(low, highs):
        blocks = [4 * i + 2 * high + low for high in highs for i in range(group)]
        return jnp.stack([layer] + blocks).astype(jnp.int32)


    half = 2 * quarter
    both = 2 * group
    narrow = jnp.bfloat16

    def earlier_of(codes):
        return [lax.ppermute(part, "layer", [(0, 1)]) for part in codes]

    def places(*rows):
        return jnp.stack([jnp.int32(row) for row in rows])

    def products(codes, earlier, info, outs, also):
        return decode(codes, earlier, own_w, cross_w, info, outs, width, also)

    def finish(total):
        bit = 4
        while bit < n_lat:
            here = (lat // bit) % 2
            pairs = total.reshape(total.shape[0] // 2, 2, *total.shape[1:])
            away = lax.dynamic_index_in_dim(pairs, 1 - here, 1, keepdims=False)
            arrived = swapped(away.astype(narrow), "latent", bit)
            total = lax.dynamic_index_in_dim(pairs, here, 1, keepdims=False) + wide(arrived)
            bit *= 2
        return total[0]

    codes = encode([(x_own, 0, rows)], places(0), inv, enc_w, bias, 2, [])
    earlier = earlier_of(codes)
    inside = ((quarter, half),)
    outside = ((0, quarter), (3 * quarter, quarter))
    spans = [(0, group, inside), (group, group, inside), (0, group, outside), (group, group, outside)]
    far_sent, near_sent, far_out_sent, near_out_sent = products(
        codes, earlier, info(other, (far, near)),
        [span + (dtype,) for span, dtype in zip(spans, (narrow, narrow, jnp.float32, jnp.float32))], [])
    far_in = swapped(far_sent, "latent", 1)
    near_in = swapped(near_sent, "latent", 1)
    far_kept, near_kept, far_out_kept, near_out_kept = products(
        codes, earlier, info(mine_bit, (far, near)), [span + (jnp.float32,) for span in spans], [far_sent])
    across_in = (far_kept + wide(far_in)).astype(narrow)
    total_in = near_kept + wide(near_in) + wide(swapped(across_in, "latent", 2))

    after = across_in
    returned = []
    far_out_back, far_out_kept_back, near_out_back, near_out_kept_back = [], [], [], []

    def joined(own, back):
        return own + sum(wide(part) for part in back)

    for back, mine, theirs, inner_rows in foreign:
        codes = encode(
            [(mine, 0, edge), (theirs, 0, edge), (inner_rows, 0, rows - 2 * edge)],
            places(side * (rows - edge), (1 - side) * (rows - edge), edge),
            inv, enc_w, bias, 1, [after])
        earlier = earlier_of(codes)

        def quarter_of(low, high, spans, dtype, also):
            *insides, outer = products(
                codes, earlier, info(low, (high,)),
                [(0, group, span, dtype) for span in spans] + [(0, group, outside, narrow)], also)
            return insides, shifted(outer, "token", back)

        (far_sent,), far_back = quarter_of(other, far, [inside], narrow, [])
        far_in = swapped(far_sent, "latent", 1)
        (far_kept,), far_kept_back = quarter_of(mine_bit, far, [inside], jnp.float32, [far_sent, total_in])
        far_out_back.append(far_back)
        ready = [(far_kept + wide(far_in)).astype(narrow)]
        across = swapped(ready[0], "latent", 2)
        if len(far_out_back) == n_tok - 1:
            ready.append(joined(far_out_sent, far_out_back).astype(narrow))
            far_out = swapped(ready[1], "latent", 1)
        halves = [((quarter, quarter),), ((2 * quarter, quarter),)]
        near_sent, near_back = quarter_of(other, near, halves, narrow, ready)
        near_in = jnp.concatenate([swapped(part, "latent", 1) for part in near_sent], axis=1)
        (near_kept,), near_kept_back = quarter_of(mine_bit, near, [inside], jnp.float32, near_sent)
        part = finish(near_kept + wide(near_in) + wide(across))
        returned.append(shifted(part.astype(narrow), "token", back))
        far_out_kept_back.append(far_kept_back)
        near_out_back.append(near_back)
        near_out_kept_back.append(near_kept_back)
        after = near_kept

    near_out = swapped(joined(near_out_sent, near_out_back).astype(narrow), "latent", 1)
    across_out = (joined(far_out_kept, far_out_kept_back) + wide(far_out)).astype(narrow)
    across_out = swapped(across_out, "latent", 2)
    if group == 1:
        outer_terms = [near_out_kept, *near_out_kept_back, near_out, across_out]
        outer_terms = [term[0] for term in outer_terms]
    else:
        outer_terms = [finish(joined(near_out_kept, near_out_kept_back) + wide(near_out) + wide(across_out))]
    recon, sums = finale(outer_terms, [finish(total_in), *returned], dec_bias, targets[0], layer)

    sums = sum_over(sum_over(sums, ("token", "layer")), "latent")
    loss = (sums[:1, 0] / sums[:1, 2] + sums[:1, 1] / sums[:1, 3]) / 2.0
    return (recon[None], loss)


def solution(mesh):
    return jax.shard_map(
        local,
        mesh=mesh,
        in_specs=(
            P("layer", ("groups", "token"), None),
            P("layer", ("groups", "token"), "latent"),
            P("layer", None, ("latent", "token")),
            P("layer", "latent"),
            P("layer", ("latent", "token"), None),
            P(("latent", "token"), None),
            P("layer", "latent"),
        ),
        out_specs=(P("layer", ("groups", "token"), "latent"), P("groups")),
        check_vma=False,
    )
```

```python
import jax
import jax.numpy as jnp
from jax import lax
from jax.experimental import pallas as pl
from jax.experimental.pallas import tpu as pltpu
from jax.sharding import PartitionSpec as P

VMEM_LIMIT = 28 * 1024 * 1024
ENCODE_TILE, ENCODE_SLOTS = 512, 3
DECODE_TILE, DECODE_SLOTS = 256, 6
COST = pl.CostEstimate(flops=0, bytes_accessed=0, transcendentals=0)


def tile_of(size, most):
    tile = min(size, most)
    while size % tile:
        tile //= 2
    return tile


def square_sum(x):
    rows, width = x.shape
    lanes = tile_of(width, 1024)
    loads = 4
    piece = rows // loads

    def body(x_ref, o_ref, held, sem):
        def load(i):
            place = pl.ds(i * piece, piece)
            return pltpu.make_async_copy(x_ref.at[place], held.at[place], sem.at[i])

        for i in range(loads):
            load(i).start()
        total = jnp.zeros((8, lanes), jnp.float32)
        for i in range(loads):
            load(i).wait()
            for c in range(width // lanes):
                def add(r, acc):
                    here = pl.ds(pl.multiple_of(i * piece + r * 16, 16), 16)
                    value = held[here, c * lanes:(c + 1) * lanes].astype(jnp.float32)
                    value = value * value
                    return acc + value[:8] + value[8:]

                total = lax.fori_loop(0, piece // 16, add, total, unroll=2)
        o_ref[0] = jnp.sum(total)

    return pl.pallas_call(
        body,
        in_specs=[pl.BlockSpec(memory_space=pl.ANY)],
        out_specs=pl.BlockSpec(memory_space=pltpu.SMEM),
        out_shape=jax.ShapeDtypeStruct((1,), jnp.float32),
        scratch_shapes=[pltpu.VMEM((rows, width), x.dtype), pltpu.SemaphoreType.DMA((loads,))],
        compiler_params=pltpu.CompilerParams(vmem_limit_bytes=VMEM_LIMIT),
        cost_estimate=COST,
        name="square_sum",
    )(x)


def cut(x, side, edge, after):
    rows, width = x.shape
    middle = rows - 2 * edge

    def body(side_ref, after_ref, x_ref, outer_ref, inner_ref, first, second, sem, out_sem):
        start = pl.multiple_of(side_ref[0] * (rows - edge), 16)
        loads = [
            pltpu.make_async_copy(x_ref.at[pl.ds(start, edge)], first, sem.at[0]),
            pltpu.make_async_copy(x_ref.at[pl.ds(edge, middle)], second, sem.at[1]),
        ]
        stores = [
            pltpu.make_async_copy(first, outer_ref, out_sem.at[0]),
            pltpu.make_async_copy(second, inner_ref, out_sem.at[1]),
        ]
        for load in loads:
            load.start()
        for load, store in zip(loads, stores):
            load.wait()
            store.start()
        for store in stores:
            store.wait()

    return pl.pallas_call(
        body,
        in_specs=[
            pl.BlockSpec(memory_space=pltpu.SMEM),
            pl.BlockSpec(memory_space=pltpu.SMEM),
            pl.BlockSpec(memory_space=pl.ANY),
        ],
        out_specs=[pl.BlockSpec(memory_space=pl.ANY)] * 2,
        out_shape=[pltpu.HBM((edge, width), x.dtype), pltpu.HBM((middle, width), x.dtype)],
        scratch_shapes=[
            pltpu.VMEM((edge, width), x.dtype),
            pltpu.VMEM((middle, width), x.dtype),
            pltpu.SemaphoreType.DMA((2,)),
            pltpu.SemaphoreType.DMA((2,)),
        ],
        compiler_params=pltpu.CompilerParams(vmem_limit_bytes=VMEM_LIMIT),
        cost_estimate=COST,
        name="cut",
    )(side.reshape(1), after, x)


def gate(values, after):
    n = len(values)

    def body(after_ref, *refs):
        pass

    return pl.pallas_call(
        body,
        in_specs=[pl.BlockSpec(memory_space=pltpu.SMEM)] + [pl.BlockSpec(memory_space=pl.ANY)] * n,
        out_specs=[pl.BlockSpec(memory_space=pl.ANY)] * n,
        out_shape=[pltpu.HBM(value.shape, value.dtype) for value in values],
        input_output_aliases={1 + i: i for i in range(n)},
        cost_estimate=COST,
        name="gate",
    )(after, *[in_hbm(value) for value in values])


def ring_loop(count, slots, start, step):
    for t in range(min(slots, count)):
        start(t, t)

    def turn(t, carry):
        slot = lax.rem(t, slots)
        step(t, slot)

        @pl.when(t + slots < count)
        def _():
            start(t + slots, slot)

        return carry

    lax.fori_loop(0, count, turn, 0)


def encode(pieces, places, inv, weight, bias, parts, also):
    rows, width = sum(piece[2] for piece in pieces), pieces[0][0].shape[1]
    latents = weight.shape[1]
    part = latents // parts
    tile = tile_of(part, ENCODE_TILE)
    n, m = len(pieces), len(also)

    def body(places_ref, inv_ref, b_ref, *refs):
        x_refs, w_ref = refs[:n], refs[n]
        o_refs = refs[n + 1 + m:n + 1 + m + parts]
        lhs, ring, lhs_sem, ring_sem = refs[n + 1 + m + parts:]

        def lhs_copy(i):
            _, first, count = pieces[i]
            place = pl.ds(pl.multiple_of(places_ref[i], 16), count)
            return pltpu.make_async_copy(
                x_refs[i].at[pl.ds(first, count)], lhs.at[place], lhs_sem.at[i])

        def columns(t):
            return pl.ds(pl.multiple_of(t * tile, tile), tile)

        def tile_copy(t, slot):
            return pltpu.make_async_copy(w_ref.at[:, columns(t)], ring.at[slot], ring_sem.at[slot])

        for i in range(n):
            lhs_copy(i).start()

        def step(t, slot):
            @pl.when(t == 0)
            def _():
                for i in range(n):
                    lhs_copy(i).wait()

            tile_copy(t, slot).wait()
            value = jnp.dot(lhs[...], ring[slot], preferred_element_type=jnp.float32)
            value = value * inv_ref[0] + b_ref[:, columns(t)].astype(jnp.float32)
            value = jnp.maximum(value, 0.0).astype(jnp.bfloat16)
            per = part // tile
            for i, o_ref in enumerate(o_refs):
                @pl.when(lax.div(t, per) == i)
                def _():
                    o_ref[:, columns(lax.rem(t, per))] = value

        ring_loop(latents // tile, ENCODE_SLOTS, lambda t, slot: tile_copy(t, slot).start(), step)

    return pl.pallas_call(
        body,
        in_specs=[
            pl.BlockSpec(memory_space=pltpu.SMEM),
            pl.BlockSpec(memory_space=pltpu.SMEM),
            pl.BlockSpec(memory_space=pltpu.VMEM),
        ] + [pl.BlockSpec(memory_space=pl.ANY)] * (n + 1 + m),
        out_specs=[pl.BlockSpec(memory_space=pltpu.VMEM)] * parts,
        out_shape=[jax.ShapeDtypeStruct((rows, part), jnp.bfloat16)] * parts,
        scratch_shapes=[
            pltpu.VMEM((rows, width), jnp.bfloat16),
            pltpu.VMEM((ENCODE_SLOTS, width, tile), jnp.bfloat16),
            pltpu.SemaphoreType.DMA((n,)),
            pltpu.SemaphoreType.DMA((ENCODE_SLOTS,)),
        ],
        compiler_params=pltpu.CompilerParams(vmem_limit_bytes=VMEM_LIMIT),
        cost_estimate=COST,
        name="encode",
    )(places, inv, bias, *[piece[0] for piece in pieces], weight, *also)


def decode(codes, earlier, own_w, cross_w, info, outs, width, also):
    parts = len(codes)
    rows, part = codes[0].shape
    latents = parts * part
    tile = tile_of(width, DECODE_TILE)
    per = width // tile
    blocks = info.shape[0] - 1
    m = len(also)

    def body(info_ref, *refs):
        code_refs, (s_ref, x_ref), refs = refs[:2 * parts], refs[2 * parts:2 * parts + 2], refs[2 * parts + 2:]
        o_refs = refs[m:m + len(outs)]
        lhs, ring, lhs_sem, ring_sem = refs[m + len(outs):]
        later = info_ref[0] != 0

        def lhs_copy(i):
            return pltpu.make_async_copy(
                code_refs[i], lhs.at[:, pl.ds(i * part, part)], lhs_sem.at[i])

        def tile_copy(source, i, t, slot):
            column = info_ref[1 + lax.div(t, per)] * width + lax.rem(t, per) * tile
            across = pl.ds(pl.multiple_of(column, tile), tile)
            return pltpu.make_async_copy(
                source.at[:, across], ring.at[slot, pl.ds(i * latents, latents)], ring_sem.at[slot, i])

        def start(t, slot):
            t = jnp.int32(t)
            tile_copy(s_ref, 0, t, slot).start()

            @pl.when(later)
            def _():
                tile_copy(x_ref, 1, t, slot).start()

        for i in range(parts):
            lhs_copy(i).start()

        @pl.when(later)
        def _():
            for i in range(parts, 2 * parts):
                lhs_copy(i).start()

        def put(t, value):
            b = lax.div(t, per)
            across = pl.ds(pl.multiple_of(lax.rem(t, per) * tile, tile), tile)
            for (block, many, spans, dtype), o_ref in zip(outs, o_refs):
                @pl.when((b >= block) & (b < block + many))
                def _():
                    here = jnp.clip(b - block, 0, many - 1)
                    at = 0
                    for row, height in spans:
                        o_ref[here, at:at + height, across] = value[row:row + height].astype(dtype)
                        at += height

        def step(t, slot):
            @pl.when(t == 0)
            def _():
                for i in range(parts):
                    lhs_copy(i).wait()

            tile_copy(s_ref, 0, t, slot).wait()

            @pl.when(later)
            def _():
                @pl.when(t == 0)
                def _():
                    for i in range(parts, 2 * parts):
                        lhs_copy(i).wait()

                tile_copy(x_ref, 1, t, slot).wait()
                put(t, jnp.dot(lhs[...], ring[slot], preferred_element_type=jnp.float32))

            @pl.when(jnp.logical_not(later))
            def _():
                put(t, jnp.dot(
                    lhs[:, :latents], ring[slot, :latents], preferred_element_type=jnp.float32))

        ring_loop(blocks * per, DECODE_SLOTS, start, step)

    return pl.pallas_call(
        body,
        in_specs=[pl.BlockSpec(memory_space=pltpu.SMEM)]
        + [pl.BlockSpec(memory_space=pl.ANY)] * (2 * parts + 2 + m),
        out_specs=[pl.BlockSpec(memory_space=pltpu.VMEM)] * len(outs),
        out_shape=[
            (pltpu.HBM if dtype == jnp.float32 else jax.ShapeDtypeStruct)(
                (many, sum(height for _, height in spans), width), dtype)
            for _, many, spans, dtype in outs
        ],
        scratch_shapes=[
            pltpu.VMEM((rows, 2 * latents), jnp.bfloat16),
            pltpu.VMEM((DECODE_SLOTS, 2 * latents, tile), jnp.bfloat16),
            pltpu.SemaphoreType.DMA((2 * parts,)),
            pltpu.SemaphoreType.DMA((DECODE_SLOTS, 2)),
        ],
        compiler_params=pltpu.CompilerParams(vmem_limit_bytes=VMEM_LIMIT),
        cost_estimate=COST,
        name="decode",
    )(info, *codes, *earlier, own_w, cross_w, *also)


def finale(outer_terms, inner_terms, bias, target, layer):
    rows, width = target.shape
    half = inner_terms[0].shape[0]
    quarter = (rows - half) // 2
    n, m = len(outer_terms), len(inner_terms)

    def body(layer_ref, b_ref, t_ref, *refs):
        terms = {0: refs[:n], 1: refs[n:n + m]}
        r_ref, s_ref = refs[n + m:]
        bias = b_ref[...].astype(jnp.float32)
        spans = [(0, 0, 0, quarter), (1, 0, quarter, half), (0, quarter, quarter + half, quarter)]

        def block(which, start, target_start):
            def run(r, sums):
                here = pl.ds(pl.multiple_of(start + r * 16, 16), 16)
                there = pl.ds(pl.multiple_of(target_start + r * 16, 16), 16)
                total = sum(term[here, :].astype(jnp.float32) for term in terms[which]) + bias
                goal = t_ref[there, :].astype(jnp.float32)
                r_ref[there, :] = total.astype(r_ref.dtype)
                diff = total - goal
                diff, goal = diff * diff, goal * goal
                return sums[0] + diff[:8] + diff[8:], sums[1] + goal[:8] + goal[8:]

            return run

        zero = jnp.zeros((8, width), jnp.float32)
        sums = (zero, zero)
        for which, start, target_start, count in spans:
            sums = lax.fori_loop(0, count // 16, block(which, start, target_start), sums)
        lane = lax.broadcasted_iota(jnp.int32, (8, 128), 1)
        value = jnp.where(lane == layer_ref[0], jnp.sum(sums[0]), 0.0)
        s_ref[...] = jnp.where(lane == layer_ref[0] + 2, jnp.sum(sums[1]), value)

    vmem = pl.BlockSpec(memory_space=pltpu.VMEM)
    return pl.pallas_call(
        body,
        in_specs=[pl.BlockSpec(memory_space=pltpu.SMEM)] + [vmem] * (2 + n + m),
        out_specs=[vmem] * 2,
        out_shape=[
            jax.ShapeDtypeStruct((rows, width), jnp.bfloat16),
            jax.ShapeDtypeStruct((8, 128), jnp.float32),
        ],
        compiler_params=pltpu.CompilerParams(vmem_limit_bytes=VMEM_LIMIT),
        cost_estimate=COST,
        name="finale",
    )(layer.astype(jnp.int32).reshape(1), bias, target, *outer_terms, *inner_terms)


def shifted(value, axis, distance):
    n = lax.axis_size(axis)
    return lax.ppermute(value, axis, [(i, (i + distance) % n) for i in range(n)])


def swapped(value, axis, bit):
    n = lax.axis_size(axis)
    return lax.ppermute(value, axis, [(i, i ^ bit) for i in range(n)])


def sum_over(value, axis):
    total = value
    for distance in range(1, lax.axis_size(axis)):
        total = total + shifted(value, axis, distance)
    return total


def in_hbm(value):
    return pltpu.with_memory_space_constraint(value, pltpu.HBM)


def wide(value):
    return value.astype(jnp.float32)


def local(inputs, targets, enc_weight, encoder_layer_bias, dec_self, dec_cross, dec_bias):
    layer = lax.axis_index("layer")
    lat = lax.axis_index("latent")
    n_lat = lax.axis_size("latent")
    n_tok = lax.axis_size("token")
    x_own = in_hbm(inputs[0])
    rows, model = x_own.shape
    enc_w = in_hbm(enc_weight[0])
    own_w = in_hbm(dec_self[0])
    cross_w = in_hbm(dec_cross)
    lat_dev = enc_w.shape[1]
    width = dec_bias.shape[1]
    side = lat % 2

    edge = rows * 7 // 24 // 16 * 16
    square = square_sum(x_own)
    outer, inner = cut(x_own, side.astype(jnp.int32), edge, square)
    square = sum_over(square, "token")
    scale = jnp.sqrt(square / (rows * n_tok * model) + 1e-06)
    inv = 1.0 / scale
    outer, inner = gate([outer, inner], inv)
    foreign = []
    for distance in range(1, n_tok):
        mine = shifted(outer, "token", distance)
        theirs = swapped(mine, "latent", 1)
        foreign.append((n_tok - distance, mine, theirs, shifted(inner, "token", distance)))

    bias = lax.dynamic_slice_in_dim(
        encoder_layer_bias, lax.axis_index("token") * lat_dev, lat_dev, axis=1
    )

    group = n_lat // 4
    other, mine_bit = 1 - lat % 2, lat % 2
    far, near = 1 - (lat // 2) % 2, (lat // 2) % 2

    def info(low, highs):
        blocks = [4 * i + 2 * high + low for high in highs for i in range(group)]
        return jnp.stack([layer] + blocks).astype(jnp.int32)

    middle = rows * 7 // 12 // 16 * 16
    first = (rows - middle) // 2
    narrow = jnp.bfloat16

    def earlier_of(codes):
        return [lax.ppermute(part, "layer", [(0, 1)]) for part in codes]

    def places(*rows):
        return jnp.stack([jnp.int32(row) for row in rows])

    def products(codes, earlier, info, outs, also):
        return decode(codes, earlier, own_w, cross_w, info, outs, width, also)

    def finish(total):
        bit = 4
        while bit < n_lat:
            here = (lat // bit) % 2
            pairs = total.reshape(total.shape[0] // 2, 2, *total.shape[1:])
            away = lax.dynamic_index_in_dim(pairs, 1 - here, 1, keepdims=False)
            arrived = swapped(away.astype(narrow), "latent", bit)
            total = lax.dynamic_index_in_dim(pairs, here, 1, keepdims=False) + wide(arrived)
            bit *= 2
        return total[0]

    codes = encode([(x_own, 0, rows)], places(0), inv, enc_w, bias, 2, [])
    earlier = earlier_of(codes)
    inside = ((first, middle),)
    outside = ((0, first), (rows - first, first))
    spans = [(0, group, inside), (group, group, inside), (0, group, outside), (group, group, outside)]
    far_sent, near_sent, far_out_sent, near_out_sent = products(
        codes, earlier, info(other, (far, near)),
        [span + (dtype,) for span, dtype in zip(spans, (narrow, narrow, jnp.float32, jnp.float32))], [])
    far_in = swapped(far_sent, "latent", 1)
    near_in = swapped(near_sent, "latent", 1)
    (far_kept, far_out_kept) = products(
        codes, earlier, info(mine_bit, (far,)),
        [(0, group, inside, jnp.float32), (0, group, outside, jnp.float32)], [far_sent])
    across_in = (far_kept + wide(far_in)).astype(narrow)
    across_in_there = swapped(across_in, "latent", 2)
    own = codes, earlier

    after = across_in
    returned = []
    far_out_back, near_out_back, near_out_kept_back = [], [], []

    def joined(own, back):
        return own + sum(wide(part) for part in back)

    for back, mine, theirs, inner_rows in foreign:
        codes = encode(
            [(mine, 0, edge), (theirs, 0, edge), (inner_rows, 0, rows - 2 * edge)],
            places(side * (rows - edge), (1 - side) * (rows - edge), edge),
            inv, enc_w, bias, 1, [after])
        earlier = earlier_of(codes)

        def quarter_of(low, high, spans, dtype, also):
            *insides, outer = products(
                codes, earlier, info(low, (high,)),
                [(0, group, span, dtype) for span in spans] + [(0, group, outside, narrow)], also)
            return insides, shifted(outer, "token", back)

        before = []
        if not returned:
            near_own, near_out_kept = products(
                *own, info(mine_bit, (near,)),
                [(0, group, inside, jnp.float32), (0, group, outside, jnp.float32)], codes)
            total_in = near_own + wide(near_in) + wide(across_in_there)
            before = [near_own]
        (far_sent,), far_back = quarter_of(other, far, [inside], narrow, before)
        far_in = swapped(far_sent, "latent", 1)
        (far_kept,), far_kept_back = quarter_of(mine_bit, far, [inside], jnp.float32, [far_sent, total_in])
        far_out_back.append(far_back)
        ready = [(far_kept + wide(far_in)).astype(narrow)]
        across = swapped(ready[0], "latent", 2)
        if len(far_out_back) == n_tok - 1:
            ready.append(joined(far_out_sent, far_out_back).astype(narrow))
            far_out = swapped(ready[1], "latent", 1)
        halves = [((first + i * (middle // 2), middle // 2),) for i in range(2)]
        near_sent, near_back = quarter_of(other, near, halves, narrow, ready)
        near_in = jnp.concatenate([swapped(rows_in, "latent", 1) for rows_in in near_sent], axis=1)
        far_out_kept = far_out_kept + wide(far_kept_back)
        pins = list(near_sent)
        if len(far_out_back) == n_tok - 1:
            far_out_kept = (far_out_kept + wide(far_out)).astype(narrow)
            pins.append(far_out_kept)
        (near_kept,), near_kept_back = quarter_of(mine_bit, near, [inside], jnp.float32, pins)
        part = finish(near_kept + wide(near_in) + wide(across))
        returned.append(shifted(part.astype(narrow), "token", back))
        near_out_back.append(near_back)
        near_out_kept_back.append(near_kept_back)
        after = near_kept

    near_out = swapped(joined(near_out_sent, near_out_back).astype(narrow), "latent", 1)
    across_out = swapped(far_out_kept, "latent", 2)
    if group == 1:
        outer_terms = [near_out_kept, *near_out_kept_back, near_out, across_out]
        outer_terms = [term[0] for term in outer_terms]
    else:
        outer_terms = [finish(joined(near_out_kept, near_out_kept_back) + wide(near_out) + wide(across_out))]
    recon, sums = finale(outer_terms, [finish(total_in), *returned], dec_bias, targets[0], layer)

    sums = sum_over(sum_over(sums, ("token", "layer")), "latent")
    loss = (sums[:1, 0] / sums[:1, 2] + sums[:1, 1] / sums[:1, 3]) / 2.0
    return (recon[None], loss)


def solution(mesh):
    return jax.shard_map(
        local,
        mesh=mesh,
        in_specs=(
            P("layer", ("groups", "token"), None),
            P("layer", ("groups", "token"), "latent"),
            P("layer", None, ("latent", "token")),
            P("layer", "latent"),
            P("layer", ("latent", "token"), None),
            P(("latent", "token"), None),
            P("layer", "latent"),
        ),
        out_specs=(P("layer", ("groups", "token"), "latent"), P("groups")),
        check_vma=False,
    )
```

```python
import jax
import jax.numpy as jnp
from jax import lax
from jax.experimental import pallas as pl
from jax.experimental.pallas import tpu as pltpu
from jax.sharding import PartitionSpec as P

VMEM_LIMIT = 28 * 1024 * 1024
ENCODE_TILE, ENCODE_SLOTS = 512, 3
DECODE_TILE, DECODE_SLOTS = 256, 6
COST = pl.CostEstimate(flops=0, bytes_accessed=0, transcendentals=0)


def tile_of(size, most):
    tile = min(size, most)
    while size % tile:
        tile //= 2
    return tile


def square_sum(x):
    rows, width = x.shape
    lanes = tile_of(width, 1024)
    loads = 4
    piece = rows // loads

    def body(x_ref, o_ref, held, sem):
        def load(i):
            place = pl.ds(i * piece, piece)
            return pltpu.make_async_copy(x_ref.at[place], held.at[place], sem.at[i])

        for i in range(loads):
            load(i).start()
        total = jnp.zeros((8, lanes), jnp.float32)
        for i in range(loads):
            load(i).wait()
            for c in range(width // lanes):
                def add(r, acc):
                    here = pl.ds(pl.multiple_of(i * piece + r * 16, 16), 16)
                    value = held[here, c * lanes:(c + 1) * lanes].astype(jnp.float32)
                    value = value * value
                    return acc + value[:8] + value[8:]

                total = lax.fori_loop(0, piece // 16, add, total, unroll=2)
        o_ref[0] = jnp.sum(total)

    return pl.pallas_call(
        body,
        in_specs=[pl.BlockSpec(memory_space=pl.ANY)],
        out_specs=pl.BlockSpec(memory_space=pltpu.SMEM),
        out_shape=jax.ShapeDtypeStruct((1,), jnp.float32),
        scratch_shapes=[pltpu.VMEM((rows, width), x.dtype), pltpu.SemaphoreType.DMA((loads,))],
        compiler_params=pltpu.CompilerParams(vmem_limit_bytes=VMEM_LIMIT),
        cost_estimate=COST,
        name="square_sum",
    )(x)


def cut(x, side, edge, after):
    rows, width = x.shape
    middle = rows - 2 * edge

    def body(side_ref, after_ref, x_ref, outer_ref, inner_ref, first, second, sem, out_sem):
        start = pl.multiple_of(side_ref[0] * (rows - edge), 16)
        loads = [
            pltpu.make_async_copy(x_ref.at[pl.ds(start, edge)], first, sem.at[0]),
            pltpu.make_async_copy(x_ref.at[pl.ds(edge, middle)], second, sem.at[1]),
        ]
        stores = [
            pltpu.make_async_copy(first, outer_ref, out_sem.at[0]),
            pltpu.make_async_copy(second, inner_ref, out_sem.at[1]),
        ]
        for load in loads:
            load.start()
        for load, store in zip(loads, stores):
            load.wait()
            store.start()
        for store in stores:
            store.wait()

    return pl.pallas_call(
        body,
        in_specs=[
            pl.BlockSpec(memory_space=pltpu.SMEM),
            pl.BlockSpec(memory_space=pltpu.SMEM),
            pl.BlockSpec(memory_space=pl.ANY),
        ],
        out_specs=[pl.BlockSpec(memory_space=pl.ANY)] * 2,
        out_shape=[pltpu.HBM((edge, width), x.dtype), pltpu.HBM((middle, width), x.dtype)],
        scratch_shapes=[
            pltpu.VMEM((edge, width), x.dtype),
            pltpu.VMEM((middle, width), x.dtype),
            pltpu.SemaphoreType.DMA((2,)),
            pltpu.SemaphoreType.DMA((2,)),
        ],
        compiler_params=pltpu.CompilerParams(vmem_limit_bytes=VMEM_LIMIT),
        cost_estimate=COST,
        name="cut",
    )(side.reshape(1), after, x)


def gate(values, after):
    n = len(values)

    def body(after_ref, *refs):
        pass

    return pl.pallas_call(
        body,
        in_specs=[pl.BlockSpec(memory_space=pltpu.SMEM)] + [pl.BlockSpec(memory_space=pl.ANY)] * n,
        out_specs=[pl.BlockSpec(memory_space=pl.ANY)] * n,
        out_shape=[pltpu.HBM(value.shape, value.dtype) for value in values],
        input_output_aliases={1 + i: i for i in range(n)},
        cost_estimate=COST,
        name="gate",
    )(after, *[in_hbm(value) for value in values])


def ring_loop(count, slots, start, step):
    for t in range(min(slots, count)):
        start(t, t)

    def turn(t, carry):
        slot = lax.rem(t, slots)
        step(t, slot)

        @pl.when(t + slots < count)
        def _():
            start(t + slots, slot)

        return carry

    lax.fori_loop(0, count, turn, 0)


def encode(pieces, places, inv, weight, bias, parts, also):
    rows, width = sum(piece[2] for piece in pieces), pieces[0][0].shape[1]
    latents = weight.shape[1]
    part = latents // parts
    tile = tile_of(part, ENCODE_TILE)
    n, m = len(pieces), len(also)

    def body(places_ref, inv_ref, b_ref, *refs):
        x_refs, w_ref = refs[:n], refs[n]
        o_refs = refs[n + 1 + m:n + 1 + m + parts]
        lhs, ring, lhs_sem, ring_sem = refs[n + 1 + m + parts:]

        def lhs_copy(i):
            _, first, count = pieces[i]
            place = pl.ds(pl.multiple_of(places_ref[i], 16), count)
            return pltpu.make_async_copy(
                x_refs[i].at[pl.ds(first, count)], lhs.at[place], lhs_sem.at[i])

        def columns(t):
            return pl.ds(pl.multiple_of(t * tile, tile), tile)

        def tile_copy(t, slot):
            return pltpu.make_async_copy(w_ref.at[:, columns(t)], ring.at[slot], ring_sem.at[slot])

        for i in range(n):
            lhs_copy(i).start()

        def step(t, slot):
            @pl.when(t == 0)
            def _():
                for i in range(n):
                    lhs_copy(i).wait()

            tile_copy(t, slot).wait()
            value = jnp.dot(lhs[...], ring[slot], preferred_element_type=jnp.float32)
            value = value * inv_ref[0] + b_ref[:, columns(t)].astype(jnp.float32)
            value = jnp.maximum(value, 0.0).astype(jnp.bfloat16)
            per = part // tile
            for i, o_ref in enumerate(o_refs):
                @pl.when(lax.div(t, per) == i)
                def _():
                    o_ref[:, columns(lax.rem(t, per))] = value

        ring_loop(latents // tile, ENCODE_SLOTS, lambda t, slot: tile_copy(t, slot).start(), step)

    return pl.pallas_call(
        body,
        in_specs=[
            pl.BlockSpec(memory_space=pltpu.SMEM),
            pl.BlockSpec(memory_space=pltpu.SMEM),
            pl.BlockSpec(memory_space=pltpu.VMEM),
        ] + [pl.BlockSpec(memory_space=pl.ANY)] * (n + 1 + m),
        out_specs=[pl.BlockSpec(memory_space=pltpu.VMEM)] * parts,
        out_shape=[jax.ShapeDtypeStruct((rows, part), jnp.bfloat16)] * parts,
        scratch_shapes=[
            pltpu.VMEM((rows, width), jnp.bfloat16),
            pltpu.VMEM((ENCODE_SLOTS, width, tile), jnp.bfloat16),
            pltpu.SemaphoreType.DMA((n,)),
            pltpu.SemaphoreType.DMA((ENCODE_SLOTS,)),
        ],
        compiler_params=pltpu.CompilerParams(vmem_limit_bytes=VMEM_LIMIT),
        cost_estimate=COST,
        name="encode",
    )(places, inv, bias, *[piece[0] for piece in pieces], weight, *also)


def decode(codes, earlier, own_w, cross_w, info, outs, width, also):
    parts = len(codes)
    rows, part = codes[0].shape
    latents = parts * part
    tile = tile_of(width, DECODE_TILE)
    per = width // tile
    blocks = info.shape[0] - 1
    m = len(also)

    def body(info_ref, *refs):
        code_refs, (s_ref, x_ref), refs = refs[:2 * parts], refs[2 * parts:2 * parts + 2], refs[2 * parts + 2:]
        o_refs = refs[m:m + len(outs)]
        lhs, ring, lhs_sem, ring_sem = refs[m + len(outs):]
        later = info_ref[0] != 0

        def lhs_copy(i):
            return pltpu.make_async_copy(
                code_refs[i], lhs.at[:, pl.ds(i * part, part)], lhs_sem.at[i])

        def tile_copy(source, i, t, slot):
            column = info_ref[1 + lax.div(t, per)] * width + lax.rem(t, per) * tile
            across = pl.ds(pl.multiple_of(column, tile), tile)
            return pltpu.make_async_copy(
                source.at[:, across], ring.at[slot, pl.ds(i * latents, latents)], ring_sem.at[slot, i])

        def start(t, slot):
            t = jnp.int32(t)
            tile_copy(s_ref, 0, t, slot).start()

            @pl.when(later)
            def _():
                tile_copy(x_ref, 1, t, slot).start()

        for i in range(parts):
            lhs_copy(i).start()

        @pl.when(later)
        def _():
            for i in range(parts, 2 * parts):
                lhs_copy(i).start()

        def put(t, value):
            b = lax.div(t, per)
            across = pl.ds(pl.multiple_of(lax.rem(t, per) * tile, tile), tile)
            for (block, many, spans, dtype), o_ref in zip(outs, o_refs):
                @pl.when((b >= block) & (b < block + many))
                def _():
                    here = jnp.clip(b - block, 0, many - 1)
                    at = 0
                    for row, height in spans:
                        o_ref[here, at:at + height, across] = value[row:row + height].astype(dtype)
                        at += height

        def step(t, slot):
            @pl.when(t == 0)
            def _():
                for i in range(parts):
                    lhs_copy(i).wait()

            tile_copy(s_ref, 0, t, slot).wait()

            @pl.when(later)
            def _():
                @pl.when(t == 0)
                def _():
                    for i in range(parts, 2 * parts):
                        lhs_copy(i).wait()

                tile_copy(x_ref, 1, t, slot).wait()
                put(t, jnp.dot(lhs[...], ring[slot], preferred_element_type=jnp.float32))

            @pl.when(jnp.logical_not(later))
            def _():
                put(t, jnp.dot(
                    lhs[:, :latents], ring[slot, :latents], preferred_element_type=jnp.float32))

        ring_loop(blocks * per, DECODE_SLOTS, start, step)

    return pl.pallas_call(
        body,
        in_specs=[pl.BlockSpec(memory_space=pltpu.SMEM)]
        + [pl.BlockSpec(memory_space=pl.ANY)] * (2 * parts + 2 + m),
        out_specs=[pl.BlockSpec(memory_space=pltpu.VMEM)] * len(outs),
        out_shape=[
            jax.ShapeDtypeStruct((many, sum(height for _, height in spans), width), dtype)
            for _, many, spans, dtype in outs
        ],
        scratch_shapes=[
            pltpu.VMEM((rows, 2 * latents), jnp.bfloat16),
            pltpu.VMEM((DECODE_SLOTS, 2 * latents, tile), jnp.bfloat16),
            pltpu.SemaphoreType.DMA((2 * parts,)),
            pltpu.SemaphoreType.DMA((DECODE_SLOTS, 2)),
        ],
        compiler_params=pltpu.CompilerParams(vmem_limit_bytes=VMEM_LIMIT),
        cost_estimate=COST,
        name="decode",
    )(info, *codes, *earlier, own_w, cross_w, *also)


def finale(outer_terms, inner_terms, bias, target, layer):
    rows, width = target.shape
    half = inner_terms[0].shape[0]
    quarter = (rows - half) // 2
    n, m = len(outer_terms), len(inner_terms)

    def body(layer_ref, b_ref, t_ref, *refs):
        terms = {0: refs[:n], 1: refs[n:n + m]}
        r_ref, s_ref = refs[n + m:]
        bias = b_ref[...].astype(jnp.float32)
        spans = [(0, 0, 0, quarter), (1, 0, quarter, half), (0, quarter, quarter + half, quarter)]

        def block(which, start, target_start):
            def run(r, sums):
                here = pl.ds(pl.multiple_of(start + r * 16, 16), 16)
                there = pl.ds(pl.multiple_of(target_start + r * 16, 16), 16)
                total = sum(term[here, :].astype(jnp.float32) for term in terms[which]) + bias
                goal = t_ref[there, :].astype(jnp.float32)
                r_ref[there, :] = total.astype(r_ref.dtype)
                diff = total - goal
                diff, goal = diff * diff, goal * goal
                return sums[0] + diff[:8] + diff[8:], sums[1] + goal[:8] + goal[8:]

            return run

        zero = jnp.zeros((8, width), jnp.float32)
        sums = (zero, zero)
        for which, start, target_start, count in spans:
            sums = lax.fori_loop(0, count // 16, block(which, start, target_start), sums)
        row = lax.broadcasted_iota(jnp.int32, (8, 128), 0)
        value = jnp.where(row == layer_ref[0], jnp.sum(sums[0]), 0.0)
        s_ref[...] = jnp.where(row == layer_ref[0] + 2, jnp.sum(sums[1]), value)

    vmem = pl.BlockSpec(memory_space=pltpu.VMEM)
    return pl.pallas_call(
        body,
        in_specs=[pl.BlockSpec(memory_space=pltpu.SMEM)] + [vmem] * (2 + n + m),
        out_specs=[vmem] * 2,
        out_shape=[
            jax.ShapeDtypeStruct((rows, width), jnp.bfloat16),
            jax.ShapeDtypeStruct((8, 128), jnp.float32),
        ],
        compiler_params=pltpu.CompilerParams(vmem_limit_bytes=VMEM_LIMIT),
        cost_estimate=COST,
        name="finale",
    )(layer.astype(jnp.int32).reshape(1), bias, target, *outer_terms, *inner_terms)


def mean_ratio(terms):
    n = len(terms)

    def body(*refs):
        total = sum(ref[...] for ref in refs[:n])
        ratio = total[0:2] / total[2:4]
        refs[n][...] = (ratio[0:1, 0:1] + ratio[1:2, 0:1]) / 2.0

    vmem = pl.BlockSpec(memory_space=pltpu.VMEM)
    return pl.pallas_call(
        body,
        in_specs=[vmem] * n,
        out_specs=vmem,
        out_shape=jax.ShapeDtypeStruct((1, 1), jnp.float32),
        cost_estimate=COST,
        name="mean_ratio",
    )(*terms).reshape(1)


def shifted(value, axis, distance):
    n = lax.axis_size(axis)
    return lax.ppermute(value, axis, [(i, (i + distance) % n) for i in range(n)])


def swapped(value, axis, bit):
    n = lax.axis_size(axis)
    return lax.ppermute(value, axis, [(i, i ^ bit) for i in range(n)])


def sum_over(value, axis):
    total = value
    for distance in range(1, lax.axis_size(axis)):
        total = total + shifted(value, axis, distance)
    return total


def in_hbm(value):
    return pltpu.with_memory_space_constraint(value, pltpu.HBM)


def wide(value):
    return value.astype(jnp.float32)


def local(inputs, targets, enc_weight, encoder_layer_bias, dec_self, dec_cross, dec_bias):
    layer = lax.axis_index("layer")
    lat = lax.axis_index("latent")
    n_lat = lax.axis_size("latent")
    n_tok = lax.axis_size("token")
    x_own = in_hbm(inputs[0])
    rows, model = x_own.shape
    enc_w = in_hbm(enc_weight[0])
    own_w = in_hbm(dec_self[0])
    cross_w = in_hbm(dec_cross)
    lat_dev = enc_w.shape[1]
    width = dec_bias.shape[1]
    side = lat % 2

    edge = rows * 7 // 24 // 16 * 16
    square = square_sum(x_own)
    outer, inner = cut(x_own, side.astype(jnp.int32), edge, square)
    square = sum_over(square, "token")
    scale = jnp.sqrt(square / (rows * n_tok * model) + 1e-06)
    inv = 1.0 / scale
    outer, inner = gate([outer, inner], inv)
    foreign = []
    for distance in range(1, n_tok):
        mine = shifted(outer, "token", distance)
        theirs = swapped(mine, "latent", 1)
        foreign.append((n_tok - distance, mine, theirs, shifted(inner, "token", distance)))

    bias = lax.dynamic_slice_in_dim(
        encoder_layer_bias, lax.axis_index("token") * lat_dev, lat_dev, axis=1
    )

    group = n_lat // 4
    other, mine_bit = 1 - lat % 2, lat % 2
    far, near = 1 - (lat // 2) % 2, (lat // 2) % 2

    def info(low, highs):
        blocks = [4 * i + 2 * high + low for high in highs for i in range(group)]
        return jnp.stack([layer] + blocks).astype(jnp.int32)

    middle = rows * 7 // 12 // 16 * 16
    first = (rows - middle) // 2
    narrow = jnp.bfloat16

    def earlier_of(codes):
        return [lax.ppermute(part, "layer", [(0, 1)]) for part in codes]

    def places(*rows):
        return jnp.stack([jnp.int32(row) for row in rows])

    def products(codes, earlier, info, outs, also):
        return decode(codes, earlier, own_w, cross_w, info, outs, width, also)

    def finish(total):
        bit = 4
        while bit < n_lat:
            here = (lat // bit) % 2
            pairs = total.reshape(total.shape[0] // 2, 2, *total.shape[1:])
            away = lax.dynamic_index_in_dim(pairs, 1 - here, 1, keepdims=False)
            arrived = swapped(away.astype(narrow), "latent", bit)
            total = lax.dynamic_index_in_dim(pairs, here, 1, keepdims=False) + wide(arrived)
            bit *= 2
        return total[0]

    codes = encode([(x_own, 0, rows)], places(0), inv, enc_w, bias, 2, [])
    earlier = earlier_of(codes)
    inside = ((first, middle),)
    outside = ((0, first), (rows - first, first))
    spans = [(0, group, inside), (group, group, inside), (0, group, outside), (group, group, outside)]
    far_sent, near_sent, far_out_sent, near_out_sent = products(
        codes, earlier, info(other, (far, near)),
        [span + (dtype,) for span, dtype in zip(spans, (narrow, narrow, jnp.float32, jnp.float32))], [])
    far_in = swapped(far_sent, "latent", 1)
    near_in = swapped(near_sent, "latent", 1)
    far_kept, near_kept, far_out_kept, near_out_kept = products(
        codes, earlier, info(mine_bit, (far, near)), [span + (jnp.float32,) for span in spans], [far_sent])
    across_in = (far_kept + wide(far_in)).astype(narrow)
    total_in = near_kept + wide(near_in) + wide(swapped(across_in, "latent", 2))

    after = across_in
    returned = []
    far_out_back, near_out_back, near_out_kept_back = [], [], []

    def joined(own, back):
        return own + sum(wide(part) for part in back)

    for back, mine, theirs, inner_rows in foreign:
        codes = encode(
            [(mine, 0, edge), (theirs, 0, edge), (inner_rows, 0, rows - 2 * edge)],
            places(side * (rows - edge), (1 - side) * (rows - edge), edge),
            inv, enc_w, bias, 1, [after])
        earlier = earlier_of(codes)

        def quarter_of(low, high, spans, dtype, also):
            *insides, outer = products(
                codes, earlier, info(low, (high,)),
                [(0, group, span, dtype) for span in spans] + [(0, group, outside, narrow)], also)
            return insides, shifted(outer, "token", back)

        (far_sent,), far_back = quarter_of(other, far, [inside], narrow, [])
        far_in = swapped(far_sent, "latent", 1)
        (far_kept,), far_kept_back = quarter_of(mine_bit, far, [inside], jnp.float32, [far_sent, total_in])
        far_out_back.append(far_back)
        ready = [(far_kept + wide(far_in)).astype(narrow)]
        across = swapped(ready[0], "latent", 2)
        if len(far_out_back) == n_tok - 1:
            ready.append(joined(far_out_sent, far_out_back).astype(narrow))
            far_out = swapped(ready[1], "latent", 1)
        halves = [((first + i * (middle // 2), middle // 2),) for i in range(2)]
        near_sent, near_back = quarter_of(other, near, halves, narrow, ready)
        near_in = jnp.concatenate([swapped(rows_in, "latent", 1) for rows_in in near_sent], axis=1)
        far_out_kept = far_out_kept + wide(far_kept_back)
        pins = list(near_sent)
        if len(far_out_back) == n_tok - 1:
            far_out_kept = (far_out_kept + wide(far_out)).astype(narrow)
            pins.append(far_out_kept)
        (near_kept,), near_kept_back = quarter_of(mine_bit, near, [inside], jnp.float32, pins)
        part = finish(near_kept + wide(near_in) + wide(across))
        returned.append(shifted(part.astype(narrow), "token", back))
        near_out_back.append(near_back)
        near_out_kept_back.append(near_kept_back)
        after = near_kept

    near_out = swapped(joined(near_out_sent, near_out_back).astype(narrow), "latent", 1)
    across_out = swapped(far_out_kept, "latent", 2)
    if group == 1:
        outer_terms = [near_out_kept, *near_out_kept_back, near_out, across_out]
        outer_terms = [term[0] for term in outer_terms]
    else:
        outer_terms = [finish(joined(near_out_kept, near_out_kept_back) + wide(near_out) + wide(across_out))]
    recon, sums = finale(outer_terms, [finish(total_in), *returned], dec_bias, targets[0], layer)

    sums = sum_over(sums, ("token", "layer"))
    loss = mean_ratio([sums] + [shifted(sums, "latent", d) for d in range(1, n_lat)])
    return (recon[None], loss)


def solution(mesh):
    return jax.shard_map(
        local,
        mesh=mesh,
        in_specs=(
            P("layer", ("groups", "token"), None),
            P("layer", ("groups", "token"), "latent"),
            P("layer", None, ("latent", "token")),
            P("layer", "latent"),
            P("layer", ("latent", "token"), None),
            P(("latent", "token"), None),
            P("layer", "latent"),
        ),
        out_specs=(P("layer", ("groups", "token"), "latent"), P("groups")),
        check_vma=False,
    )
```

```python
import jax
import jax.numpy as jnp
from jax import lax
from jax.experimental import pallas as pl
from jax.experimental.pallas import tpu as pltpu
from jax.sharding import PartitionSpec as P

VMEM_LIMIT = 28 * 1024 * 1024
ENCODE_TILE, ENCODE_SLOTS = 512, 3
DECODE_TILE, DECODE_SLOTS = 256, 6
COST = pl.CostEstimate(flops=0, bytes_accessed=0, transcendentals=0)


def tile_of(size, most):
    tile = min(size, most)
    while size % tile:
        tile //= 2
    return tile


def square_sum(x):
    rows, width = x.shape
    lanes = tile_of(width, 1024)
    loads = 4
    piece = rows // loads

    def body(x_ref, o_ref, held, sem):
        def load(i):
            place = pl.ds(i * piece, piece)
            return pltpu.make_async_copy(x_ref.at[place], held.at[place], sem.at[i])

        for i in range(loads):
            load(i).start()
        total = jnp.zeros((8, lanes), jnp.float32)
        for i in range(loads):
            load(i).wait()
            for c in range(width // lanes):
                def add(r, acc):
                    here = pl.ds(pl.multiple_of(i * piece + r * 16, 16), 16)
                    value = held[here, c * lanes:(c + 1) * lanes].astype(jnp.float32)
                    value = value * value
                    return acc + value[:8] + value[8:]

                total = lax.fori_loop(0, piece // 16, add, total, unroll=2)
        o_ref[0] = jnp.sum(total)

    return pl.pallas_call(
        body,
        in_specs=[pl.BlockSpec(memory_space=pl.ANY)],
        out_specs=pl.BlockSpec(memory_space=pltpu.SMEM),
        out_shape=jax.ShapeDtypeStruct((1,), jnp.float32),
        scratch_shapes=[pltpu.VMEM((rows, width), x.dtype), pltpu.SemaphoreType.DMA((loads,))],
        compiler_params=pltpu.CompilerParams(vmem_limit_bytes=VMEM_LIMIT),
        cost_estimate=COST,
        name="square_sum",
    )(x)


def cut(x, side, edge, after):
    rows, width = x.shape
    middle = rows - 2 * edge

    def body(side_ref, after_ref, x_ref, outer_ref, inner_ref, first, second, sem, out_sem):
        start = pl.multiple_of(side_ref[0] * (rows - edge), 16)
        loads = [
            pltpu.make_async_copy(x_ref.at[pl.ds(start, edge)], first, sem.at[0]),
            pltpu.make_async_copy(x_ref.at[pl.ds(edge, middle)], second, sem.at[1]),
        ]
        stores = [
            pltpu.make_async_copy(first, outer_ref, out_sem.at[0]),
            pltpu.make_async_copy(second, inner_ref, out_sem.at[1]),
        ]
        for load in loads:
            load.start()
        for load, store in zip(loads, stores):
            load.wait()
            store.start()
        for store in stores:
            store.wait()

    return pl.pallas_call(
        body,
        in_specs=[
            pl.BlockSpec(memory_space=pltpu.SMEM),
            pl.BlockSpec(memory_space=pltpu.SMEM),
            pl.BlockSpec(memory_space=pl.ANY),
        ],
        out_specs=[pl.BlockSpec(memory_space=pl.ANY)] * 2,
        out_shape=[pltpu.HBM((edge, width), x.dtype), pltpu.HBM((middle, width), x.dtype)],
        scratch_shapes=[
            pltpu.VMEM((edge, width), x.dtype),
            pltpu.VMEM((middle, width), x.dtype),
            pltpu.SemaphoreType.DMA((2,)),
            pltpu.SemaphoreType.DMA((2,)),
        ],
        compiler_params=pltpu.CompilerParams(vmem_limit_bytes=VMEM_LIMIT),
        cost_estimate=COST,
        name="cut",
    )(side.reshape(1), after, x)


def gate(values, after):
    n = len(values)

    def body(after_ref, *refs):
        pass

    return pl.pallas_call(
        body,
        in_specs=[pl.BlockSpec(memory_space=pltpu.SMEM)] + [pl.BlockSpec(memory_space=pl.ANY)] * n,
        out_specs=[pl.BlockSpec(memory_space=pl.ANY)] * n,
        out_shape=[pltpu.HBM(value.shape, value.dtype) for value in values],
        input_output_aliases={1 + i: i for i in range(n)},
        cost_estimate=COST,
        name="gate",
    )(after, *[in_hbm(value) for value in values])


def ring_loop(count, slots, start, step):
    for t in range(min(slots, count)):
        start(t, t)

    def turn(t, carry):
        slot = lax.rem(t, slots)
        step(t, slot)

        @pl.when(t + slots < count)
        def _():
            start(t + slots, slot)

        return carry

    lax.fori_loop(0, count, turn, 0)


def encode(pieces, places, inv, weight, bias, parts, also):
    rows, width = sum(piece[2] for piece in pieces), pieces[0][0].shape[1]
    latents = weight.shape[1]
    part = latents // parts
    tile = tile_of(part, ENCODE_TILE)
    n, m = len(pieces), len(also)

    def body(places_ref, inv_ref, b_ref, *refs):
        x_refs, w_ref = refs[:n], refs[n]
        o_refs = refs[n + 1 + m:n + 1 + m + parts]
        lhs, ring, lhs_sem, ring_sem = refs[n + 1 + m + parts:]

        def lhs_copy(i):
            _, first, count = pieces[i]
            place = pl.ds(pl.multiple_of(places_ref[i], 16), count)
            return pltpu.make_async_copy(
                x_refs[i].at[pl.ds(first, count)], lhs.at[place], lhs_sem.at[i])

        def columns(t):
            return pl.ds(pl.multiple_of(t * tile, tile), tile)

        def tile_copy(t, slot):
            return pltpu.make_async_copy(w_ref.at[:, columns(t)], ring.at[slot], ring_sem.at[slot])

        for i in range(n):
            lhs_copy(i).start()

        def step(t, slot):
            @pl.when(t == 0)
            def _():
                for i in range(n):
                    lhs_copy(i).wait()

            tile_copy(t, slot).wait()
            value = jnp.dot(lhs[...], ring[slot], preferred_element_type=jnp.float32)
            value = value * inv_ref[0] + b_ref[:, columns(t)].astype(jnp.float32)
            value = jnp.maximum(value, 0.0).astype(jnp.bfloat16)
            per = part // tile
            for i, o_ref in enumerate(o_refs):
                @pl.when(lax.div(t, per) == i)
                def _():
                    o_ref[:, columns(lax.rem(t, per))] = value

        ring_loop(latents // tile, ENCODE_SLOTS, lambda t, slot: tile_copy(t, slot).start(), step)

    return pl.pallas_call(
        body,
        in_specs=[
            pl.BlockSpec(memory_space=pltpu.SMEM),
            pl.BlockSpec(memory_space=pltpu.SMEM),
            pl.BlockSpec(memory_space=pltpu.VMEM),
        ] + [pl.BlockSpec(memory_space=pl.ANY)] * (n + 1 + m),
        out_specs=[pl.BlockSpec(memory_space=pltpu.VMEM)] * parts,
        out_shape=[jax.ShapeDtypeStruct((rows, part), jnp.bfloat16)] * parts,
        scratch_shapes=[
            pltpu.VMEM((rows, width), jnp.bfloat16),
            pltpu.VMEM((ENCODE_SLOTS, width, tile), jnp.bfloat16),
            pltpu.SemaphoreType.DMA((n,)),
            pltpu.SemaphoreType.DMA((ENCODE_SLOTS,)),
        ],
        compiler_params=pltpu.CompilerParams(vmem_limit_bytes=VMEM_LIMIT),
        cost_estimate=COST,
        name="encode",
    )(places, inv, bias, *[piece[0] for piece in pieces], weight, *also)


def decode(codes, earlier, own_w, cross_w, info, outs, width, also):
    parts = len(codes)
    rows, part = codes[0].shape
    latents = parts * part
    tile = tile_of(width, DECODE_TILE)
    per = width // tile
    blocks = info.shape[0] - 1
    m = len(also)

    def body(info_ref, *refs):
        code_refs, (s_ref, x_ref), refs = refs[:2 * parts], refs[2 * parts:2 * parts + 2], refs[2 * parts + 2:]
        o_refs = refs[m:m + len(outs)]
        lhs, ring, lhs_sem, ring_sem = refs[m + len(outs):]
        later = info_ref[0] != 0

        def lhs_copy(i):
            return pltpu.make_async_copy(
                code_refs[i], lhs.at[:, pl.ds(i * part, part)], lhs_sem.at[i])

        def tile_copy(source, i, t, slot):
            column = info_ref[1 + lax.div(t, per)] * width + lax.rem(t, per) * tile
            across = pl.ds(pl.multiple_of(column, tile), tile)
            return pltpu.make_async_copy(
                source.at[:, across], ring.at[slot, pl.ds(i * latents, latents)], ring_sem.at[slot, i])

        def start(t, slot):
            t = jnp.int32(t)
            tile_copy(s_ref, 0, t, slot).start()

            @pl.when(later)
            def _():
                tile_copy(x_ref, 1, t, slot).start()

        for i in range(parts):
            lhs_copy(i).start()

        @pl.when(later)
        def _():
            for i in range(parts, 2 * parts):
                lhs_copy(i).start()

        def put(t, value):
            b = lax.div(t, per)
            across = pl.ds(pl.multiple_of(lax.rem(t, per) * tile, tile), tile)
            for (block, many, spans, dtype), o_ref in zip(outs, o_refs):
                @pl.when((b >= block) & (b < block + many))
                def _():
                    here = jnp.clip(b - block, 0, many - 1)
                    at = 0
                    for row, height in spans:
                        o_ref[here, at:at + height, across] = value[row:row + height].astype(dtype)
                        at += height

        def step(t, slot):
            @pl.when(t == 0)
            def _():
                for i in range(parts):
                    lhs_copy(i).wait()

            tile_copy(s_ref, 0, t, slot).wait()

            @pl.when(later)
            def _():
                @pl.when(t == 0)
                def _():
                    for i in range(parts, 2 * parts):
                        lhs_copy(i).wait()

                tile_copy(x_ref, 1, t, slot).wait()
                put(t, jnp.dot(lhs[...], ring[slot], preferred_element_type=jnp.float32))

            @pl.when(jnp.logical_not(later))
            def _():
                put(t, jnp.dot(
                    lhs[:, :latents], ring[slot, :latents], preferred_element_type=jnp.float32))

        ring_loop(blocks * per, DECODE_SLOTS, start, step)

    return pl.pallas_call(
        body,
        in_specs=[pl.BlockSpec(memory_space=pltpu.SMEM)]
        + [pl.BlockSpec(memory_space=pl.ANY)] * (2 * parts + 2 + m),
        out_specs=[pl.BlockSpec(memory_space=pltpu.VMEM)] * len(outs),
        out_shape=[
            jax.ShapeDtypeStruct((many, sum(height for _, height in spans), width), dtype)
            for _, many, spans, dtype in outs
        ],
        scratch_shapes=[
            pltpu.VMEM((rows, 2 * latents), jnp.bfloat16),
            pltpu.VMEM((DECODE_SLOTS, 2 * latents, tile), jnp.bfloat16),
            pltpu.SemaphoreType.DMA((2 * parts,)),
            pltpu.SemaphoreType.DMA((DECODE_SLOTS, 2)),
        ],
        compiler_params=pltpu.CompilerParams(vmem_limit_bytes=VMEM_LIMIT),
        cost_estimate=COST,
        name="decode",
    )(info, *codes, *earlier, own_w, cross_w, *also)


def finale(outer_terms, inner_terms, bias, target, layer):
    rows, width = target.shape
    half = inner_terms[0].shape[0]
    quarter = (rows - half) // 2
    n, m = len(outer_terms), len(inner_terms)

    def body(layer_ref, b_ref, t_ref, *refs):
        terms = {0: refs[:n], 1: refs[n:n + m]}
        r_ref, s_ref = refs[n + m:]
        bias = b_ref[...].astype(jnp.float32)
        spans = [(0, 0, 0, quarter), (1, 0, quarter, half), (0, quarter, quarter + half, quarter)]

        def block(which, start, target_start):
            def run(r, sums):
                here = pl.ds(pl.multiple_of(start + r * 16, 16), 16)
                there = pl.ds(pl.multiple_of(target_start + r * 16, 16), 16)
                total = sum(term[here, :].astype(jnp.float32) for term in terms[which]) + bias
                goal = t_ref[there, :].astype(jnp.float32)
                r_ref[there, :] = total.astype(r_ref.dtype)
                diff = total - goal
                diff, goal = diff * diff, goal * goal
                return sums[0] + diff[:8] + diff[8:], sums[1] + goal[:8] + goal[8:]

            return run

        zero = jnp.zeros((8, width), jnp.float32)
        sums = (zero, zero)
        for which, start, target_start, count in spans:
            sums = lax.fori_loop(0, count // 16, block(which, start, target_start), sums)
        row = lax.broadcasted_iota(jnp.int32, (8, 128), 0)
        value = jnp.where(row == layer_ref[0], jnp.sum(sums[0]), 0.0)
        s_ref[...] = jnp.where(row == layer_ref[0] + 2, jnp.sum(sums[1]), value)

    vmem = pl.BlockSpec(memory_space=pltpu.VMEM)
    return pl.pallas_call(
        body,
        in_specs=[pl.BlockSpec(memory_space=pltpu.SMEM)] + [vmem] * (2 + n + m),
        out_specs=[vmem] * 2,
        out_shape=[
            jax.ShapeDtypeStruct((rows, width), jnp.bfloat16),
            jax.ShapeDtypeStruct((8, 128), jnp.float32),
        ],
        compiler_params=pltpu.CompilerParams(vmem_limit_bytes=VMEM_LIMIT),
        cost_estimate=COST,
        name="finale",
    )(layer.astype(jnp.int32).reshape(1), bias, target, *outer_terms, *inner_terms)


def mean_ratio(terms):
    n = len(terms)

    def body(*refs):
        total = sum(ref[...] for ref in refs[:n])
        ratio = total[0:2] / total[2:4]
        refs[n][...] = (ratio[0:1, 0:1] + ratio[1:2, 0:1]) / 2.0

    vmem = pl.BlockSpec(memory_space=pltpu.VMEM)
    return pl.pallas_call(
        body,
        in_specs=[vmem] * n,
        out_specs=vmem,
        out_shape=jax.ShapeDtypeStruct((1, 1), jnp.float32),
        cost_estimate=COST,
        name="mean_ratio",
    )(*terms).reshape(1)


def shifted(value, axis, distance):
    n = lax.axis_size(axis)
    return lax.ppermute(value, axis, [(i, (i + distance) % n) for i in range(n)])


def swapped(value, axis, bit):
    n = lax.axis_size(axis)
    return lax.ppermute(value, axis, [(i, i ^ bit) for i in range(n)])


def sum_over(value, axis):
    total = value
    for distance in range(1, lax.axis_size(axis)):
        total = total + shifted(value, axis, distance)
    return total


def in_hbm(value):
    return pltpu.with_memory_space_constraint(value, pltpu.HBM)


def wide(value):
    return value.astype(jnp.float32)


def local(inputs, targets, enc_weight, encoder_layer_bias, dec_self, dec_cross, dec_bias):
    layer = lax.axis_index("layer")
    lat = lax.axis_index("latent")
    n_lat = lax.axis_size("latent")
    n_tok = lax.axis_size("token")
    x_own = in_hbm(inputs[0])
    rows, model = x_own.shape
    enc_w = in_hbm(enc_weight[0])
    own_w = in_hbm(dec_self[0])
    cross_w = in_hbm(dec_cross)
    lat_dev = enc_w.shape[1]
    width = dec_bias.shape[1]
    side = lat % 2

    edge = rows * 7 // 24 // 16 * 16
    square = square_sum(x_own)
    outer, inner = cut(x_own, side.astype(jnp.int32), edge, square)
    square = sum_over(square, "token")
    scale = jnp.sqrt(square / (rows * n_tok * model) + 1e-06)
    inv = 1.0 / scale
    outer, inner = gate([outer, inner], inv)
    foreign = []
    for distance in range(1, n_tok):
        mine = shifted(outer, "token", distance)
        theirs = swapped(mine, "latent", 1)
        foreign.append((n_tok - distance, mine, theirs, shifted(inner, "token", distance)))

    bias = lax.dynamic_slice_in_dim(
        encoder_layer_bias, lax.axis_index("token") * lat_dev, lat_dev, axis=1
    )

    group = n_lat // 4
    other, mine_bit = 1 - lat % 2, lat % 2
    far, near = 1 - (lat // 2) % 2, (lat // 2) % 2

    def info(low, highs):
        blocks = [4 * i + 2 * high + low for high in highs for i in range(group)]
        return jnp.stack([layer] + blocks).astype(jnp.int32)

    middle = rows * 7 // 12 // 16 * 16
    first = (rows - middle) // 2
    narrow = jnp.bfloat16

    def earlier_of(codes):
        return [lax.ppermute(part, "layer", [(0, 1)]) for part in codes]

    def places(*rows):
        return jnp.stack([jnp.int32(row) for row in rows])

    def products(codes, earlier, info, outs, also):
        return decode(codes, earlier, own_w, cross_w, info, outs, width, also)

    def finish(total):
        bit = 4
        while bit < n_lat:
            here = (lat // bit) % 2
            pairs = total.reshape(total.shape[0] // 2, 2, *total.shape[1:])
            away = lax.dynamic_index_in_dim(pairs, 1 - here, 1, keepdims=False)
            arrived = swapped(away.astype(narrow), "latent", bit)
            total = lax.dynamic_index_in_dim(pairs, here, 1, keepdims=False) + wide(arrived)
            bit *= 2
        return total[0]

    codes = encode([(x_own, 0, rows)], places(0), inv, enc_w, bias, 2, [])
    earlier = earlier_of(codes)
    inside = ((first, middle),)
    outside = ((0, first), (rows - first, first))
    spans = [(0, group, inside), (group, group, inside), (0, group, outside), (group, group, outside)]
    sent_in, far_out_sent, near_out_sent = products(
        codes, earlier, info(other, (far, near)),
        [(0, 2 * group, inside, narrow)] + [span + (jnp.float32,) for span in spans[2:]], [])
    there_in = swapped(sent_in, "latent", 1)
    far_kept, near_kept, far_out_kept, near_out_kept = products(
        codes, earlier, info(mine_bit, (far, near)), [span + (jnp.float32,) for span in spans], [sent_in])
    across_in = (far_kept + wide(there_in[:group])).astype(narrow)
    total_in = near_kept + wide(there_in[group:]) + wide(swapped(across_in, "latent", 2))

    after, before = near_kept, [across_in]
    returned = []
    far_out_back, near_out_back, near_out_kept_back = [], [], []

    def joined(own, back):
        return own + sum(wide(part) for part in back)

    for back, mine, theirs, inner_rows in foreign:
        codes = encode(
            [(mine, 0, edge), (theirs, 0, edge), (inner_rows, 0, rows - 2 * edge)],
            places(side * (rows - edge), (1 - side) * (rows - edge), edge),
            inv, enc_w, bias, min(2, lat_dev // 256), [after])
        earlier = earlier_of(codes)

        def quarter_of(low, high, spans, dtype, also):
            *insides, outer = products(
                codes, earlier, info(low, (high,)),
                [(0, group, span, dtype) for span in spans] + [(0, group, outside, narrow)], also)
            return insides, shifted(outer, "token", back)

        (far_sent,), far_back = quarter_of(other, far, [inside], narrow, before)
        far_in = swapped(far_sent, "latent", 1)
        (far_kept,), far_kept_back = quarter_of(mine_bit, far, [inside], jnp.float32, [far_sent, total_in])
        far_out_back.append(far_back)
        ready = [(far_kept + wide(far_in)).astype(narrow)]
        across = swapped(ready[0], "latent", 2)
        if len(far_out_back) == n_tok - 1:
            ready.append(joined(far_out_sent, far_out_back).astype(narrow))
            far_out = swapped(ready[1], "latent", 1)
        halves = [((first + i * (middle // 2), middle // 2),) for i in range(2)]
        near_sent, near_back = quarter_of(other, near, halves, narrow, ready)
        near_in = jnp.concatenate([swapped(rows_in, "latent", 1) for rows_in in near_sent], axis=1)
        far_out_kept = far_out_kept + wide(far_kept_back)
        pins = list(near_sent)
        if len(far_out_back) == n_tok - 1:
            far_out_kept = (far_out_kept + wide(far_out)).astype(narrow)
            pins.append(far_out_kept)
        (near_kept,), near_kept_back = quarter_of(mine_bit, near, [inside], jnp.float32, pins)
        part = finish(near_kept + wide(near_in) + wide(across))
        returned.append(shifted(part.astype(narrow), "token", back))
        near_out_back.append(near_back)
        near_out_kept_back.append(near_kept_back)
        after, before = near_kept, []

    near_out = swapped(joined(near_out_sent, near_out_back).astype(narrow), "latent", 1)
    across_out = swapped(far_out_kept, "latent", 2)
    if group == 1:
        outer_terms = [near_out_kept, *near_out_kept_back, near_out, across_out]
        outer_terms = [term[0] for term in outer_terms]
    else:
        outer_terms = [finish(joined(near_out_kept, near_out_kept_back) + wide(near_out) + wide(across_out))]
    recon, sums = finale(outer_terms, [finish(total_in), *returned], dec_bias, targets[0], layer)

    sums = sum_over(sums, ("token", "layer"))
    loss = mean_ratio([sums] + [shifted(sums, "latent", d) for d in range(1, n_lat)])
    return (recon[None], loss)


def solution(mesh):
    return jax.shard_map(
        local,
        mesh=mesh,
        in_specs=(
            P("layer", ("groups", "token"), None),
            P("layer", ("groups", "token"), "latent"),
            P("layer", None, ("latent", "token")),
            P("layer", "latent"),
            P("layer", ("latent", "token"), None),
            P(("latent", "token"), None),
            P("layer", "latent"),
        ),
        out_specs=(P("layer", ("groups", "token"), "latent"), P("groups")),
        check_vma=False,
    )
```

```python
import jax
import jax.numpy as jnp
from jax import lax
from jax.experimental import pallas as pl
from jax.experimental.pallas import tpu as pltpu
from jax.sharding import PartitionSpec as P

VMEM_LIMIT = 28 * 1024 * 1024
ENCODE_TILE, ENCODE_SLOTS = 512, 3
DECODE_TILE, DECODE_SLOTS = 256, 6
COST = pl.CostEstimate(flops=0, bytes_accessed=0, transcendentals=0)


def tile_of(size, most):
    tile = min(size, most)
    while size % tile:
        tile //= 2
    return tile


def square_sum(x):
    rows, width = x.shape
    lanes = tile_of(width, 1024)
    loads = 4
    piece = rows // loads

    def body(x_ref, o_ref, held, sem):
        def load(i):
            place = pl.ds(i * piece, piece)
            return pltpu.make_async_copy(x_ref.at[place], held.at[place], sem.at[i])

        for i in range(loads):
            load(i).start()
        total = jnp.zeros((8, lanes), jnp.float32)
        for i in range(loads):
            load(i).wait()
            for c in range(width // lanes):
                def add(r, acc):
                    here = pl.ds(pl.multiple_of(i * piece + r * 16, 16), 16)
                    value = held[here, c * lanes:(c + 1) * lanes].astype(jnp.float32)
                    value = value * value
                    return acc + value[:8] + value[8:]

                total = lax.fori_loop(0, piece // 16, add, total, unroll=2)
        o_ref[0] = jnp.sum(total)

    return pl.pallas_call(
        body,
        in_specs=[pl.BlockSpec(memory_space=pl.ANY)],
        out_specs=[pl.BlockSpec(memory_space=pltpu.SMEM), pl.BlockSpec(memory_space=pltpu.VMEM)],
        out_shape=[jax.ShapeDtypeStruct((1,), jnp.float32), pltpu.VMEM((rows, width), x.dtype)],
        scratch_shapes=[pltpu.SemaphoreType.DMA((loads,))],
        compiler_params=pltpu.CompilerParams(vmem_limit_bytes=VMEM_LIMIT),
        cost_estimate=COST,
        name="square_sum",
    )(x)


def cut(x, side, edge, after):
    rows, width = x.shape
    middle = rows - 2 * edge

    def body(side_ref, after_ref, x_ref, outer_ref, inner_ref, sem):
        start = pl.multiple_of(side_ref[0] * (rows - edge), 16)
        copies = [
            pltpu.make_async_copy(x_ref.at[pl.ds(start, edge)], outer_ref, sem.at[0]),
            pltpu.make_async_copy(x_ref.at[pl.ds(edge, middle)], inner_ref, sem.at[1]),
        ]
        for copy in copies:
            copy.start()
        for copy in copies:
            copy.wait()

    return pl.pallas_call(
        body,
        in_specs=[
            pl.BlockSpec(memory_space=pltpu.SMEM),
            pl.BlockSpec(memory_space=pltpu.SMEM),
            pl.BlockSpec(memory_space=pltpu.VMEM),
        ],
        out_specs=[pl.BlockSpec(memory_space=pl.ANY)] * 2,
        out_shape=[pltpu.HBM((edge, width), x.dtype), pltpu.HBM((middle, width), x.dtype)],
        scratch_shapes=[pltpu.SemaphoreType.DMA((2,))],
        compiler_params=pltpu.CompilerParams(vmem_limit_bytes=VMEM_LIMIT),
        cost_estimate=COST,
        name="cut",
    )(side.reshape(1), after, pltpu.with_memory_space_constraint(x, pltpu.VMEM))


def ring_loop(count, slots, start, step):
    for t in range(min(slots, count)):
        start(t, t)

    def turn(t, carry):
        slot = lax.rem(t, slots)
        step(t, slot)

        @pl.when(t + slots < count)
        def _():
            start(t + slots, slot)

        return carry

    lax.fori_loop(0, count, turn, 0)


def encode(pieces, places, inv, weight, bias, parts, also):
    rows, width = sum(piece[2] for piece in pieces), pieces[0][0].shape[1]
    latents = weight.shape[1]
    part = latents // parts
    tile = tile_of(part, ENCODE_TILE)
    n, m = len(pieces), len(also)

    def body(places_ref, inv_ref, b_ref, *refs):
        x_refs, w_ref = refs[:n], refs[n]
        o_refs = refs[n + 1 + m:n + 1 + m + parts]
        lhs, ring, lhs_sem, ring_sem = refs[n + 1 + m + parts:]

        def lhs_copy(i):
            _, first, count = pieces[i]
            place = pl.ds(pl.multiple_of(places_ref[i], 16), count)
            return pltpu.make_async_copy(
                x_refs[i].at[pl.ds(first, count)], lhs.at[place], lhs_sem.at[i])

        def columns(t):
            return pl.ds(pl.multiple_of(t * tile, tile), tile)

        def tile_copy(t, slot):
            return pltpu.make_async_copy(w_ref.at[:, columns(t)], ring.at[slot], ring_sem.at[slot])

        for i in range(n):
            lhs_copy(i).start()

        def step(t, slot):
            @pl.when(t == 0)
            def _():
                for i in range(n):
                    lhs_copy(i).wait()

            tile_copy(t, slot).wait()
            value = jnp.dot(lhs[...], ring[slot], preferred_element_type=jnp.float32)
            value = value * inv_ref[0] + b_ref[:, columns(t)].astype(jnp.float32)
            value = jnp.maximum(value, 0.0).astype(jnp.bfloat16)
            per = part // tile
            for i, o_ref in enumerate(o_refs):
                @pl.when(lax.div(t, per) == i)
                def _():
                    o_ref[:, columns(lax.rem(t, per))] = value

        ring_loop(latents // tile, ENCODE_SLOTS, lambda t, slot: tile_copy(t, slot).start(), step)

    return pl.pallas_call(
        body,
        in_specs=[
            pl.BlockSpec(memory_space=pltpu.SMEM),
            pl.BlockSpec(memory_space=pltpu.SMEM),
            pl.BlockSpec(memory_space=pltpu.VMEM),
        ] + [pl.BlockSpec(memory_space=pl.ANY)] * (n + 1 + m),
        out_specs=[pl.BlockSpec(memory_space=pltpu.VMEM)] * parts,
        out_shape=[jax.ShapeDtypeStruct((rows, part), jnp.bfloat16)] * parts,
        scratch_shapes=[
            pltpu.VMEM((rows, width), jnp.bfloat16),
            pltpu.VMEM((ENCODE_SLOTS, width, tile), jnp.bfloat16),
            pltpu.SemaphoreType.DMA((n,)),
            pltpu.SemaphoreType.DMA((ENCODE_SLOTS,)),
        ],
        compiler_params=pltpu.CompilerParams(vmem_limit_bytes=VMEM_LIMIT),
        cost_estimate=COST,
        name="encode",
    )(places, inv, bias, *[piece[0] for piece in pieces], weight, *also)


def decode(codes, earlier, own_w, cross_w, info, outs, width, also):
    parts = len(codes)
    rows, part = codes[0].shape
    latents = parts * part
    tile = tile_of(width, DECODE_TILE)
    per = width // tile
    blocks = info.shape[0] - 1
    m = len(also)

    def body(info_ref, *refs):
        code_refs, (s_ref, x_ref), refs = refs[:2 * parts], refs[2 * parts:2 * parts + 2], refs[2 * parts + 2:]
        o_refs = refs[m:m + len(outs)]
        lhs, ring, lhs_sem, ring_sem = refs[m + len(outs):]
        later = info_ref[0] != 0

        def lhs_copy(i):
            return pltpu.make_async_copy(
                code_refs[i], lhs.at[:, pl.ds(i * part, part)], lhs_sem.at[i])

        def tile_copy(source, i, t, slot):
            column = info_ref[1 + lax.div(t, per)] * width + lax.rem(t, per) * tile
            across = pl.ds(pl.multiple_of(column, tile), tile)
            return pltpu.make_async_copy(
                source.at[:, across], ring.at[slot, pl.ds(i * latents, latents)], ring_sem.at[slot, i])

        def start(t, slot):
            t = jnp.int32(t)
            tile_copy(s_ref, 0, t, slot).start()

            @pl.when(later)
            def _():
                tile_copy(x_ref, 1, t, slot).start()

        for i in range(parts):
            lhs_copy(i).start()

        @pl.when(later)
        def _():
            for i in range(parts, 2 * parts):
                lhs_copy(i).start()

        def put(t, value):
            b = lax.div(t, per)
            across = pl.ds(pl.multiple_of(lax.rem(t, per) * tile, tile), tile)
            for (block, many, spans, dtype), o_ref in zip(outs, o_refs):
                @pl.when((b >= block) & (b < block + many))
                def _():
                    here = jnp.clip(b - block, 0, many - 1)
                    at = 0
                    for row, height in spans:
                        o_ref[here, at:at + height, across] = value[row:row + height].astype(dtype)
                        at += height

        def step(t, slot):
            @pl.when(t == 0)
            def _():
                for i in range(parts):
                    lhs_copy(i).wait()

            tile_copy(s_ref, 0, t, slot).wait()

            @pl.when(later)
            def _():
                @pl.when(t == 0)
                def _():
                    for i in range(parts, 2 * parts):
                        lhs_copy(i).wait()

                tile_copy(x_ref, 1, t, slot).wait()
                put(t, jnp.dot(lhs[...], ring[slot], preferred_element_type=jnp.float32))

            @pl.when(jnp.logical_not(later))
            def _():
                put(t, jnp.dot(
                    lhs[:, :latents], ring[slot, :latents], preferred_element_type=jnp.float32))

        ring_loop(blocks * per, DECODE_SLOTS, start, step)

    return pl.pallas_call(
        body,
        in_specs=[pl.BlockSpec(memory_space=pltpu.SMEM)]
        + [pl.BlockSpec(memory_space=pl.ANY)] * (2 * parts + 2 + m),
        out_specs=[pl.BlockSpec(memory_space=pltpu.VMEM)] * len(outs),
        out_shape=[
            jax.ShapeDtypeStruct((many, sum(height for _, height in spans), width), dtype)
            for _, many, spans, dtype in outs
        ],
        scratch_shapes=[
            pltpu.VMEM((rows, 2 * latents), jnp.bfloat16),
            pltpu.VMEM((DECODE_SLOTS, 2 * latents, tile), jnp.bfloat16),
            pltpu.SemaphoreType.DMA((2 * parts,)),
            pltpu.SemaphoreType.DMA((DECODE_SLOTS, 2)),
        ],
        compiler_params=pltpu.CompilerParams(vmem_limit_bytes=VMEM_LIMIT),
        cost_estimate=COST,
        name="decode",
    )(info, *codes, *earlier, own_w, cross_w, *also)


def finale(outer_terms, inner_terms, first, bias, target, layer):
    rows, width = target.shape
    middle = inner_terms[0].shape[0]
    last = first + middle
    n, m = len(outer_terms), len(inner_terms)

    def body(layer_ref, b_ref, t_ref, *refs):
        terms = {0: refs[:n], 1: refs[n:n + m]}
        r_ref, s_ref = refs[n + m:]
        bias = b_ref[...].astype(jnp.float32)
        spans = [(0, 0, 0, first), (1, 0, first, middle), (0, first, last, rows - last)]

        def block(which, start, target_start):
            def run(r, sums):
                here = pl.ds(pl.multiple_of(start + r * 16, 16), 16)
                there = pl.ds(pl.multiple_of(target_start + r * 16, 16), 16)
                total = sum(term[here, :].astype(jnp.float32) for term in terms[which]) + bias
                goal = t_ref[there, :].astype(jnp.float32)
                r_ref[there, :] = total.astype(r_ref.dtype)
                diff = total - goal
                diff, goal = diff * diff, goal * goal
                return sums[0] + diff[:8] + diff[8:], sums[1] + goal[:8] + goal[8:]

            return run

        zero = jnp.zeros((8, width), jnp.float32)
        sums = (zero, zero)
        for which, start, target_start, count in spans:
            sums = lax.fori_loop(0, count // 16, block(which, start, target_start), sums)
        row = lax.broadcasted_iota(jnp.int32, (8, 128), 0)
        value = jnp.where(row == layer_ref[0], jnp.sum(sums[0]), 0.0)
        s_ref[...] = jnp.where(row == layer_ref[0] + 2, jnp.sum(sums[1]), value)

    vmem = pl.BlockSpec(memory_space=pltpu.VMEM)
    return pl.pallas_call(
        body,
        in_specs=[pl.BlockSpec(memory_space=pltpu.SMEM)] + [vmem] * (2 + n + m),
        out_specs=[vmem] * 2,
        out_shape=[
            jax.ShapeDtypeStruct((rows, width), jnp.bfloat16),
            jax.ShapeDtypeStruct((8, 128), jnp.float32),
        ],
        compiler_params=pltpu.CompilerParams(vmem_limit_bytes=VMEM_LIMIT),
        cost_estimate=COST,
        name="finale",
    )(layer.astype(jnp.int32).reshape(1), bias, target, *outer_terms, *inner_terms)


def mean_ratio(terms):
    n = len(terms)

    def body(*refs):
        total = sum(ref[...] for ref in refs[:n])
        ratio = total[0:2] / total[2:4]
        refs[n][...] = (ratio[0:1, 0:1] + ratio[1:2, 0:1]) / 2.0

    vmem = pl.BlockSpec(memory_space=pltpu.VMEM)
    return pl.pallas_call(
        body,
        in_specs=[vmem] * n,
        out_specs=vmem,
        out_shape=jax.ShapeDtypeStruct((1, 1), jnp.float32),
        cost_estimate=COST,
        name="mean_ratio",
    )(*terms).reshape(1)


def shifted(value, axis, distance):
    n = lax.axis_size(axis)
    return lax.ppermute(value, axis, [(i, (i + distance) % n) for i in range(n)])


def swapped(value, axis, bit):
    n = lax.axis_size(axis)
    return lax.ppermute(value, axis, [(i, i ^ bit) for i in range(n)])


def sum_over(value, axis):
    total = value
    for distance in range(1, lax.axis_size(axis)):
        total = total + shifted(value, axis, distance)
    return total


def in_hbm(value):
    return pltpu.with_memory_space_constraint(value, pltpu.HBM)


def wide(value):
    return value.astype(jnp.float32)


def local(inputs, targets, enc_weight, encoder_layer_bias, dec_self, dec_cross, dec_bias):
    layer = lax.axis_index("layer")
    lat = lax.axis_index("latent")
    n_lat = lax.axis_size("latent")
    n_tok = lax.axis_size("token")
    x_own = in_hbm(inputs[0])
    rows, model = x_own.shape
    enc_w = in_hbm(enc_weight[0])
    own_w = in_hbm(dec_self[0])
    cross_w = in_hbm(dec_cross)
    lat_dev = enc_w.shape[1]
    width = dec_bias.shape[1]
    side = lat % 2

    edge = rows * 7 // 24 // 16 * 16
    square, x_held = square_sum(x_own)
    square = sum_over(square, "token")
    scale = jnp.sqrt(square / (rows * n_tok * model) + 1e-06)
    inv = 1.0 / scale
    outer, inner = cut(x_held, side.astype(jnp.int32), edge, inv)
    foreign = []
    for distance in range(1, n_tok):
        mine = shifted(outer, "token", distance)
        theirs = swapped(mine, "latent", 1)
        foreign.append((n_tok - distance, mine, theirs, shifted(inner, "token", distance)))

    bias = lax.dynamic_slice_in_dim(
        encoder_layer_bias, lax.axis_index("token") * lat_dev, lat_dev, axis=1
    )

    group = n_lat // 4
    other, mine_bit = 1 - lat % 2, lat % 2
    far, near = 1 - (lat // 2) % 2, (lat // 2) % 2

    def info(low, highs):
        blocks = [4 * i + 2 * high + low for high in highs for i in range(group)]
        return jnp.stack([layer] + blocks).astype(jnp.int32)

    middle = rows * 13 // 24 // 16 * 16
    first = (rows - middle) // 2 // 16 * 16
    last = first + middle
    narrow = jnp.bfloat16

    def earlier_of(codes):
        return [lax.ppermute(part, "layer", [(0, 1)]) for part in codes]

    def places(*rows):
        return jnp.stack([jnp.int32(row) for row in rows])

    def products(codes, earlier, info, outs, also):
        return decode(codes, earlier, own_w, cross_w, info, outs, width, also)

    def finish(total):
        bit = 4
        while bit < n_lat:
            here = (lat // bit) % 2
            pairs = total.reshape(total.shape[0] // 2, 2, *total.shape[1:])
            away = lax.dynamic_index_in_dim(pairs, 1 - here, 1, keepdims=False)
            arrived = swapped(away.astype(narrow), "latent", bit)
            total = lax.dynamic_index_in_dim(pairs, here, 1, keepdims=False) + wide(arrived)
            bit *= 2
        return total[0]

    codes = encode([(x_held, 0, rows)], places(0), inv, enc_w, bias, 2, [])
    earlier = earlier_of(codes)
    inside = ((first, middle),)
    outside = ((0, first), (last, rows - last))
    spans = [(0, group, inside), (group, group, inside), (0, group, outside), (group, group, outside)]
    far_sent, near_sent, far_out_sent, near_out_sent = products(
        codes, earlier, info(other, (far, near)),
        [span + (dtype,) for span, dtype in zip(spans, (narrow, narrow, jnp.float32, jnp.float32))], [])
    far_in = swapped(far_sent, "latent", 1)
    near_in = swapped(near_sent, "latent", 1)
    far_kept, near_kept, far_out_kept, near_out_kept = products(
        codes, earlier, info(mine_bit, (far, near)), [span + (jnp.float32,) for span in spans], [far_sent])
    across_in = (far_kept + wide(far_in)).astype(narrow)
    total_in = near_kept + wide(near_in) + wide(swapped(across_in, "latent", 2))

    after = across_in
    returned = []
    far_out_back, near_out_back, near_out_kept_back = [], [], []

    def joined(own, back):
        return own + sum(wide(part) for part in back)

    for back, mine, theirs, inner_rows in foreign:
        codes = encode(
            [(mine, 0, edge), (theirs, 0, edge), (inner_rows, 0, rows - 2 * edge)],
            places(side * (rows - edge), (1 - side) * (rows - edge), edge),
            inv, enc_w, bias, 1, [after])
        earlier = earlier_of(codes)

        def quarter_of(low, high, spans, dtype, also):
            *insides, outer = products(
                codes, earlier, info(low, (high,)),
                [(0, group, span, dtype) for span in spans] + [(0, group, outside, narrow)], also)
            return insides, shifted(outer, "token", back)

        (far_sent,), far_back = quarter_of(other, far, [inside], narrow, [])
        far_in = swapped(far_sent, "latent", 1)
        (far_kept,), far_kept_back = quarter_of(mine_bit, far, [inside], jnp.float32, [far_sent, total_in])
        far_out_back.append(far_back)
        ready = [(far_kept + wide(far_in)).astype(narrow)]
        across = swapped(ready[0], "latent", 2)
        if len(far_out_back) == n_tok - 1:
            ready.append(joined(far_out_sent, far_out_back).astype(narrow))
            far_out = swapped(ready[1], "latent", 1)
        cut_at = (middle // 2 + 15) // 16 * 16
        halves = [((first, cut_at),), ((first + cut_at, middle - cut_at),)]
        near_sent, near_back = quarter_of(other, near, halves, narrow, ready)
        near_in = jnp.concatenate([swapped(rows_in, "latent", 1) for rows_in in near_sent], axis=1)
        far_out_kept = far_out_kept + wide(far_kept_back)
        pins = list(near_sent)
        if len(far_out_back) == n_tok - 1:
            far_out_kept = (far_out_kept + wide(far_out)).astype(narrow)
            pins.append(far_out_kept)
        (near_kept,), near_kept_back = quarter_of(mine_bit, near, [inside], jnp.float32, pins)
        part = finish(near_kept + wide(near_in) + wide(across))
        returned.append(shifted(part.astype(narrow), "token", back))
        near_out_back.append(near_back)
        near_out_kept_back.append(near_kept_back)
        after = near_kept

    near_out = swapped(joined(near_out_sent, near_out_back).astype(narrow), "latent", 1)
    across_out = swapped(far_out_kept, "latent", 2)
    if group == 1:
        outer_terms = [near_out_kept, *near_out_kept_back, near_out, across_out]
        outer_terms = [term[0] for term in outer_terms]
    else:
        outer_terms = [finish(joined(near_out_kept, near_out_kept_back) + wide(near_out) + wide(across_out))]
    recon, sums = finale(outer_terms, [finish(total_in), *returned], first, dec_bias, targets[0], layer)

    sums = sum_over(sums, ("token", "layer"))
    loss = mean_ratio([sums] + [shifted(sums, "latent", d) for d in range(1, n_lat)])
    return (recon[None], loss)


def solution(mesh):
    return jax.shard_map(
        local,
        mesh=mesh,
        in_specs=(
            P("layer", ("groups", "token"), None),
            P("layer", ("groups", "token"), "latent"),
            P("layer", None, ("latent", "token")),
            P("layer", "latent"),
            P("layer", ("latent", "token"), None),
            P(("latent", "token"), None),
            P("layer", "latent"),
        ),
        out_specs=(P("layer", ("groups", "token"), "latent"), P("groups")),
        check_vma=False,
    )
```

```python
import jax
import jax.numpy as jnp
from jax import lax
from jax.experimental import pallas as pl
from jax.experimental.pallas import tpu as pltpu
from jax.sharding import PartitionSpec as P

VMEM_LIMIT = 28 * 1024 * 1024
ENCODE_TILE, ENCODE_SLOTS = 512, 3
DECODE_TILE, DECODE_SLOTS = 256, 6
COST = pl.CostEstimate(flops=0, bytes_accessed=0, transcendentals=0)


def tile_of(size, most):
    tile = min(size, most)
    while size % tile:
        tile //= 2
    return tile


def square_sum(x):
    rows, width = x.shape
    lanes = tile_of(width, 1024)
    loads = 4
    piece = rows // loads

    def body(x_ref, o_ref, held, sem):
        def load(i):
            place = pl.ds(i * piece, piece)
            return pltpu.make_async_copy(x_ref.at[place], held.at[place], sem.at[i])

        for i in range(loads):
            load(i).start()
        total = jnp.zeros((8, lanes), jnp.float32)
        for i in range(loads):
            load(i).wait()
            for c in range(width // lanes):
                def add(r, acc):
                    here = pl.ds(pl.multiple_of(i * piece + r * 16, 16), 16)
                    value = held[here, c * lanes:(c + 1) * lanes].astype(jnp.float32)
                    value = value * value
                    return acc + value[:8] + value[8:]

                total = lax.fori_loop(0, piece // 16, add, total, unroll=2)
        o_ref[0] = jnp.sum(total)

    return pl.pallas_call(
        body,
        in_specs=[pl.BlockSpec(memory_space=pl.ANY)],
        out_specs=[pl.BlockSpec(memory_space=pltpu.SMEM), pl.BlockSpec(memory_space=pltpu.VMEM)],
        out_shape=[jax.ShapeDtypeStruct((1,), jnp.float32), pltpu.VMEM((rows, width), x.dtype)],
        scratch_shapes=[pltpu.SemaphoreType.DMA((loads,))],
        compiler_params=pltpu.CompilerParams(vmem_limit_bytes=VMEM_LIMIT),
        cost_estimate=COST,
        name="square_sum",
    )(x)


def cut(x, side, edge, after):
    rows, width = x.shape
    middle = rows - 2 * edge

    def body(side_ref, after_ref, x_ref, outer_ref, inner_ref, sem):
        start = pl.multiple_of(side_ref[0] * (rows - edge), 16)
        copies = [
            pltpu.make_async_copy(x_ref.at[pl.ds(start, edge)], outer_ref, sem.at[0]),
            pltpu.make_async_copy(x_ref.at[pl.ds(edge, middle)], inner_ref, sem.at[1]),
        ]
        for copy in copies:
            copy.start()
        for copy in copies:
            copy.wait()

    return pl.pallas_call(
        body,
        in_specs=[
            pl.BlockSpec(memory_space=pltpu.SMEM),
            pl.BlockSpec(memory_space=pltpu.SMEM),
            pl.BlockSpec(memory_space=pltpu.VMEM),
        ],
        out_specs=[pl.BlockSpec(memory_space=pl.ANY)] * 2,
        out_shape=[pltpu.HBM((edge, width), x.dtype), pltpu.HBM((middle, width), x.dtype)],
        scratch_shapes=[pltpu.SemaphoreType.DMA((2,))],
        compiler_params=pltpu.CompilerParams(vmem_limit_bytes=VMEM_LIMIT),
        cost_estimate=COST,
        name="cut",
    )(side.reshape(1), after, pltpu.with_memory_space_constraint(x, pltpu.VMEM))


def ring_loop(count, slots, start, step):
    for t in range(min(slots, count)):
        start(t, t)

    def turn(t, carry):
        slot = lax.rem(t, slots)
        step(t, slot)

        @pl.when(t + slots < count)
        def _():
            start(t + slots, slot)

        return carry

    lax.fori_loop(0, count, turn, 0)


def encode(pieces, places, inv, weight, bias, parts, also):
    rows, width = sum(piece[2] for piece in pieces), pieces[0][0].shape[1]
    latents = weight.shape[1]
    part = latents // parts
    tile = tile_of(part, ENCODE_TILE)
    n, m = len(pieces), len(also)

    def body(places_ref, inv_ref, b_ref, *refs):
        x_refs, w_ref = refs[:n], refs[n]
        o_refs = refs[n + 1 + m:n + 1 + m + parts]
        lhs, ring, lhs_sem, ring_sem = refs[n + 1 + m + parts:]

        def lhs_copy(i):
            _, first, count = pieces[i]
            place = pl.ds(pl.multiple_of(places_ref[i], 16), count)
            return pltpu.make_async_copy(
                x_refs[i].at[pl.ds(first, count)], lhs.at[place], lhs_sem.at[i])

        def columns(t):
            return pl.ds(pl.multiple_of(t * tile, tile), tile)

        def tile_copy(t, slot):
            return pltpu.make_async_copy(w_ref.at[:, columns(t)], ring.at[slot], ring_sem.at[slot])

        for i in range(n):
            lhs_copy(i).start()

        def step(t, slot):
            @pl.when(t == 0)
            def _():
                for i in range(n):
                    lhs_copy(i).wait()

            tile_copy(t, slot).wait()
            value = jnp.dot(lhs[...], ring[slot], preferred_element_type=jnp.float32)
            value = value * inv_ref[0] + b_ref[:, columns(t)].astype(jnp.float32)
            value = jnp.maximum(value, 0.0).astype(jnp.bfloat16)
            per = part // tile
            for i, o_ref in enumerate(o_refs):
                @pl.when(lax.div(t, per) == i)
                def _():
                    o_ref[:, columns(lax.rem(t, per))] = value

        ring_loop(latents // tile, ENCODE_SLOTS, lambda t, slot: tile_copy(t, slot).start(), step)

    return pl.pallas_call(
        body,
        in_specs=[
            pl.BlockSpec(memory_space=pltpu.SMEM),
            pl.BlockSpec(memory_space=pltpu.SMEM),
            pl.BlockSpec(memory_space=pltpu.VMEM),
        ] + [pl.BlockSpec(memory_space=pl.ANY)] * (n + 1 + m),
        out_specs=[pl.BlockSpec(memory_space=pltpu.VMEM)] * parts,
        out_shape=[jax.ShapeDtypeStruct((rows, part), jnp.bfloat16)] * parts,
        scratch_shapes=[
            pltpu.VMEM((rows, width), jnp.bfloat16),
            pltpu.VMEM((ENCODE_SLOTS, width, tile), jnp.bfloat16),
            pltpu.SemaphoreType.DMA((n,)),
            pltpu.SemaphoreType.DMA((ENCODE_SLOTS,)),
        ],
        compiler_params=pltpu.CompilerParams(vmem_limit_bytes=VMEM_LIMIT),
        cost_estimate=COST,
        name="encode",
    )(places, inv, bias, *[piece[0] for piece in pieces], weight, *also)


def decode(codes, earlier, own_w, cross_w, info, outs, width, also):
    parts = len(codes)
    rows, part = codes[0].shape
    latents = parts * part
    tile = tile_of(width, DECODE_TILE)
    per = width // tile
    blocks = info.shape[0] - 1
    m = len(also)

    def body(info_ref, *refs):
        code_refs, (s_ref, x_ref), refs = refs[:2 * parts], refs[2 * parts:2 * parts + 2], refs[2 * parts + 2:]
        o_refs = refs[m:m + len(outs)]
        lhs, ring, lhs_sem, ring_sem = refs[m + len(outs):]
        later = info_ref[0] != 0

        def lhs_copy(i):
            return pltpu.make_async_copy(
                code_refs[i], lhs.at[:, pl.ds(i * part, part)], lhs_sem.at[i])

        def tile_copy(source, i, t, slot):
            column = info_ref[1 + lax.div(t, per)] * width + lax.rem(t, per) * tile
            across = pl.ds(pl.multiple_of(column, tile), tile)
            return pltpu.make_async_copy(
                source.at[:, across], ring.at[slot, pl.ds(i * latents, latents)], ring_sem.at[slot, i])

        def start(t, slot):
            t = jnp.int32(t)
            tile_copy(s_ref, 0, t, slot).start()

            @pl.when(later)
            def _():
                tile_copy(x_ref, 1, t, slot).start()

        for i in range(parts):
            lhs_copy(i).start()

        @pl.when(later)
        def _():
            for i in range(parts, 2 * parts):
                lhs_copy(i).start()

        def put(t, value):
            b = lax.div(t, per)
            across = pl.ds(pl.multiple_of(lax.rem(t, per) * tile, tile), tile)
            for (block, many, spans, dtype), o_ref in zip(outs, o_refs):
                @pl.when((b >= block) & (b < block + many))
                def _():
                    here = jnp.clip(b - block, 0, many - 1)
                    at = 0
                    for row, height in spans:
                        o_ref[here, at:at + height, across] = value[row:row + height].astype(dtype)
                        at += height

        def step(t, slot):
            @pl.when(t == 0)
            def _():
                for i in range(parts):
                    lhs_copy(i).wait()

            tile_copy(s_ref, 0, t, slot).wait()

            @pl.when(later)
            def _():
                @pl.when(t == 0)
                def _():
                    for i in range(parts, 2 * parts):
                        lhs_copy(i).wait()

                tile_copy(x_ref, 1, t, slot).wait()
                put(t, jnp.dot(lhs[...], ring[slot], preferred_element_type=jnp.float32))

            @pl.when(jnp.logical_not(later))
            def _():
                put(t, jnp.dot(
                    lhs[:, :latents], ring[slot, :latents], preferred_element_type=jnp.float32))

        ring_loop(blocks * per, DECODE_SLOTS, start, step)

    return pl.pallas_call(
        body,
        in_specs=[pl.BlockSpec(memory_space=pltpu.SMEM)]
        + [pl.BlockSpec(memory_space=pl.ANY)] * (2 * parts + 2 + m),
        out_specs=[pl.BlockSpec(memory_space=pltpu.VMEM)] * len(outs),
        out_shape=[
            jax.ShapeDtypeStruct((many, sum(height for _, height in spans), width), dtype)
            for _, many, spans, dtype in outs
        ],
        scratch_shapes=[
            pltpu.VMEM((rows, 2 * latents), jnp.bfloat16),
            pltpu.VMEM((DECODE_SLOTS, 2 * latents, tile), jnp.bfloat16),
            pltpu.SemaphoreType.DMA((2 * parts,)),
            pltpu.SemaphoreType.DMA((DECODE_SLOTS, 2)),
        ],
        compiler_params=pltpu.CompilerParams(vmem_limit_bytes=VMEM_LIMIT),
        cost_estimate=COST,
        name="decode",
    )(info, *codes, *earlier, own_w, cross_w, *also)


def finale(outer_terms, inner_terms, first, bias, target, layer):
    rows, width = target.shape
    middle = inner_terms[0].shape[0]
    last = first + middle
    n, m = len(outer_terms), len(inner_terms)

    def body(layer_ref, b_ref, t_ref, *refs):
        terms = {0: refs[:n], 1: refs[n:n + m]}
        r_ref, s_ref = refs[n + m:]
        bias = b_ref[...].astype(jnp.float32)
        spans = [(0, 0, 0, first), (1, 0, first, middle), (0, first, last, rows - last)]

        def block(which, start, target_start):
            def run(r, sums):
                here = pl.ds(pl.multiple_of(start + r * 16, 16), 16)
                there = pl.ds(pl.multiple_of(target_start + r * 16, 16), 16)
                total = sum(term[here, :].astype(jnp.float32) for term in terms[which]) + bias
                goal = t_ref[there, :].astype(jnp.float32)
                r_ref[there, :] = total.astype(r_ref.dtype)
                diff = total - goal
                diff, goal = diff * diff, goal * goal
                return sums[0] + diff[:8] + diff[8:], sums[1] + goal[:8] + goal[8:]

            return run

        zero = jnp.zeros((8, width), jnp.float32)
        sums = (zero, zero)
        for which, start, target_start, count in spans:
            sums = lax.fori_loop(0, count // 16, block(which, start, target_start), sums)
        row = lax.broadcasted_iota(jnp.int32, (8, 128), 0)
        value = jnp.where(row == layer_ref[0], jnp.sum(sums[0]), 0.0)
        s_ref[...] = jnp.where(row == layer_ref[0] + 2, jnp.sum(sums[1]), value)

    vmem = pl.BlockSpec(memory_space=pltpu.VMEM)
    return pl.pallas_call(
        body,
        in_specs=[pl.BlockSpec(memory_space=pltpu.SMEM)] + [vmem] * (2 + n + m),
        out_specs=[vmem] * 2,
        out_shape=[
            jax.ShapeDtypeStruct((rows, width), jnp.bfloat16),
            jax.ShapeDtypeStruct((8, 128), jnp.float32),
        ],
        compiler_params=pltpu.CompilerParams(vmem_limit_bytes=VMEM_LIMIT),
        cost_estimate=COST,
        name="finale",
    )(layer.astype(jnp.int32).reshape(1), bias, target, *outer_terms, *inner_terms)


def mean_ratio(terms):
    n = len(terms)

    def body(*refs):
        total = sum(ref[...] for ref in refs[:n])
        ratio = total[0:2] / total[2:4]
        refs[n][...] = (ratio[0:1, 0:1] + ratio[1:2, 0:1]) / 2.0

    vmem = pl.BlockSpec(memory_space=pltpu.VMEM)
    return pl.pallas_call(
        body,
        in_specs=[vmem] * n,
        out_specs=vmem,
        out_shape=jax.ShapeDtypeStruct((1, 1), jnp.float32),
        cost_estimate=COST,
        name="mean_ratio",
    )(*terms).reshape(1)


def shifted(value, axis, distance):
    n = lax.axis_size(axis)
    return lax.ppermute(value, axis, [(i, (i + distance) % n) for i in range(n)])


def swapped(value, axis, bit):
    n = lax.axis_size(axis)
    return lax.ppermute(value, axis, [(i, i ^ bit) for i in range(n)])


def sum_over(value, axis):
    total = value
    for distance in range(1, lax.axis_size(axis)):
        total = total + shifted(value, axis, distance)
    return total


def in_hbm(value):
    return pltpu.with_memory_space_constraint(value, pltpu.HBM)


def wide(value):
    return value.astype(jnp.float32)


def local(inputs, targets, enc_weight, encoder_layer_bias, dec_self, dec_cross, dec_bias):
    layer = lax.axis_index("layer")
    lat = lax.axis_index("latent")
    n_lat = lax.axis_size("latent")
    n_tok = lax.axis_size("token")
    x_own = in_hbm(inputs[0])
    rows, model = x_own.shape
    enc_w = in_hbm(enc_weight[0])
    own_w = in_hbm(dec_self[0])
    cross_w = in_hbm(dec_cross)
    lat_dev = enc_w.shape[1]
    width = dec_bias.shape[1]
    side = lat % 2

    edge = rows * 7 // 24 // 16 * 16
    square, x_held = square_sum(x_own)
    square = sum_over(square, "token")
    scale = jnp.sqrt(square / (rows * n_tok * model) + 1e-06)
    inv = 1.0 / scale
    outer, inner = cut(x_held, side.astype(jnp.int32), edge, square)
    foreign = []
    for distance in range(1, n_tok):
        mine = shifted(outer, "token", distance)
        theirs = swapped(mine, "latent", 1)
        foreign.append((n_tok - distance, mine, theirs, shifted(inner, "token", distance)))

    bias = lax.dynamic_slice_in_dim(
        encoder_layer_bias, lax.axis_index("token") * lat_dev, lat_dev, axis=1
    )

    group = n_lat // 4
    other, mine_bit = 1 - lat % 2, lat % 2
    far, near = 1 - (lat // 2) % 2, (lat // 2) % 2

    def info(low, highs):
        blocks = [4 * i + 2 * high + low for high in highs for i in range(group)]
        return jnp.stack([layer] + blocks).astype(jnp.int32)

    middle = rows * 13 // 24 // 16 * 16
    first = (rows - middle) // 2 // 16 * 16
    last = first + middle
    narrow = jnp.bfloat16

    def earlier_of(codes):
        return [lax.ppermute(part, "layer", [(0, 1)]) for part in codes]

    def places(*rows):
        return jnp.stack([jnp.int32(row) for row in rows])

    def products(codes, earlier, info, outs, also):
        return decode(codes, earlier, own_w, cross_w, info, outs, width, also)

    def finish(total):
        bit = 4
        while bit < n_lat:
            here = (lat // bit) % 2
            pairs = total.reshape(total.shape[0] // 2, 2, *total.shape[1:])
            away = lax.dynamic_index_in_dim(pairs, 1 - here, 1, keepdims=False)
            arrived = swapped(away.astype(narrow), "latent", bit)
            total = lax.dynamic_index_in_dim(pairs, here, 1, keepdims=False) + wide(arrived)
            bit *= 2
        return total[0]

    codes = encode([(x_held, 0, rows)], places(0), inv, enc_w, bias, 2, [])
    earlier = earlier_of(codes)
    inside = ((first, middle),)
    outside = ((0, first), (last, rows - last))
    spans = [(0, group, inside), (group, group, inside), (0, group, outside), (group, group, outside)]
    far_sent, near_sent, far_out_sent, near_out_sent = products(
        codes, earlier, info(other, (far, near)),
        [span + (dtype,) for span, dtype in zip(spans, (narrow, narrow, jnp.float32, jnp.float32))], [])
    far_in = swapped(far_sent, "latent", 1)
    near_in = swapped(near_sent, "latent", 1)
    far_kept, near_kept, far_out_kept, near_out_kept = products(
        codes, earlier, info(mine_bit, (far, near)), [span + (jnp.float32,) for span in spans], [far_sent])
    across_in = (far_kept + wide(far_in)).astype(narrow)
    total_in = near_kept + wide(near_in) + wide(swapped(across_in, "latent", 2))

    after = across_in
    returned = []
    far_out_back, near_out_back, near_out_kept_back = [], [], []

    def joined(own, back):
        return own + sum(wide(part) for part in back)

    for back, mine, theirs, inner_rows in foreign:
        codes = encode(
            [(mine, 0, edge), (theirs, 0, edge), (inner_rows, 0, rows - 2 * edge)],
            places(side * (rows - edge), (1 - side) * (rows - edge), edge),
            inv, enc_w, bias, min(2, lat_dev // 256), [after])
        earlier = earlier_of(codes)

        def quarter_of(low, high, spans, dtype, also):
            *insides, outer = products(
                codes, earlier, info(low, (high,)),
                [(0, group, span, dtype) for span in spans] + [(0, group, outside, narrow)], also)
            return insides, shifted(outer, "token", back)

        (far_sent,), far_back = quarter_of(other, far, [inside], narrow, [])
        far_in = swapped(far_sent, "latent", 1)
        (far_kept,), far_kept_back = quarter_of(mine_bit, far, [inside], jnp.float32, [far_sent, total_in])
        far_out_back.append(far_back)
        ready = [(far_kept + wide(far_in)).astype(narrow)]
        across = swapped(ready[0], "latent", 2)
        if len(far_out_back) == n_tok - 1:
            ready.append(joined(far_out_sent, far_out_back).astype(narrow))
            far_out = swapped(ready[1], "latent", 1)
        cut_at = (middle // 2 + 15) // 16 * 16
        halves = [((first, cut_at),), ((first + cut_at, middle - cut_at),)]
        near_sent, near_back = quarter_of(other, near, halves, narrow, ready)
        near_in = jnp.concatenate([swapped(rows_in, "latent", 1) for rows_in in near_sent], axis=1)
        far_out_kept = far_out_kept + wide(far_kept_back)
        pins = list(near_sent)
        if len(far_out_back) == n_tok - 1:
            far_out_kept = (far_out_kept + wide(far_out)).astype(narrow)
            pins.append(far_out_kept)
        (near_kept,), near_kept_back = quarter_of(mine_bit, near, [inside], jnp.float32, pins)
        part = finish(near_kept + wide(near_in) + wide(across))
        returned.append(shifted(part.astype(narrow), "token", back))
        near_out_back.append(near_back)
        near_out_kept_back.append(near_kept_back)
        after = near_kept

    near_out = swapped(joined(near_out_sent, near_out_back).astype(narrow), "latent", 1)
    across_out = swapped(far_out_kept, "latent", 2)
    if group == 1:
        outer_terms = [near_out_kept, *near_out_kept_back, near_out, across_out]
        outer_terms = [term[0] for term in outer_terms]
    else:
        outer_terms = [finish(joined(near_out_kept, near_out_kept_back) + wide(near_out) + wide(across_out))]
    recon, sums = finale(outer_terms, [finish(total_in), *returned], first, dec_bias, targets[0], layer)

    sums = sum_over(sums, ("token", "layer"))
    loss = mean_ratio([sums] + [shifted(sums, "latent", d) for d in range(1, n_lat)])
    return (recon[None], loss)


def solution(mesh):
    return jax.shard_map(
        local,
        mesh=mesh,
        in_specs=(
            P("layer", ("groups", "token"), None),
            P("layer", ("groups", "token"), "latent"),
            P("layer", None, ("latent", "token")),
            P("layer", "latent"),
            P("layer", ("latent", "token"), None),
            P(("latent", "token"), None),
            P("layer", "latent"),
        ),
        out_specs=(P("layer", ("groups", "token"), "latent"), P("groups")),
        check_vma=False,
    )
```

```python
import jax
import jax.numpy as jnp
from jax import lax
from jax.experimental import pallas as pl
from jax.experimental.pallas import tpu as pltpu
from jax.sharding import PartitionSpec as P

VMEM_LIMIT = 28 * 1024 * 1024
ENCODE_TILE, ENCODE_SLOTS = 512, 3
DECODE_TILE, DECODE_SLOTS = 256, 6
COST = pl.CostEstimate(flops=0, bytes_accessed=0, transcendentals=0)


def tile_of(size, most):
    tile = min(size, most)
    while size % tile:
        tile //= 2
    return tile


def square_sum(x, side, edge):
    rows, width = x.shape
    lanes = tile_of(width, 1024)
    loads = 4
    piece = rows // loads

    def body(side_ref, x_ref, o_ref, held, outer_ref, sem, out_sem):
        start = pl.multiple_of(side_ref[0] * (rows - edge), 16)
        store = pltpu.make_async_copy(held.at[pl.ds(start, edge)], outer_ref, out_sem)

        def load(i):
            place = pl.ds(i * piece, piece)
            return pltpu.make_async_copy(x_ref.at[place], held.at[place], sem.at[i])

        for i in range(loads):
            load(i).start()
        total = jnp.zeros((8, lanes), jnp.float32)
        for i in range(loads):
            load(i).wait()
            for c in range(width // lanes):
                def add(r, acc):
                    here = pl.ds(pl.multiple_of(i * piece + r * 16, 16), 16)
                    value = held[here, c * lanes:(c + 1) * lanes].astype(jnp.float32)
                    value = value * value
                    return acc + value[:8] + value[8:]

                total = lax.fori_loop(0, piece // 16, add, total, unroll=2)
        store.start()
        o_ref[0] = jnp.sum(total)
        store.wait()

    return pl.pallas_call(
        body,
        in_specs=[pl.BlockSpec(memory_space=pltpu.SMEM), pl.BlockSpec(memory_space=pl.ANY)],
        out_specs=[
            pl.BlockSpec(memory_space=pltpu.SMEM),
            pl.BlockSpec(memory_space=pltpu.VMEM),
            pl.BlockSpec(memory_space=pl.ANY),
        ],
        out_shape=[
            jax.ShapeDtypeStruct((1,), jnp.float32),
            pltpu.VMEM((rows, width), x.dtype),
            pltpu.HBM((edge, width), x.dtype),
        ],
        scratch_shapes=[pltpu.SemaphoreType.DMA((loads,)), pltpu.SemaphoreType.DMA],
        compiler_params=pltpu.CompilerParams(vmem_limit_bytes=VMEM_LIMIT),
        cost_estimate=COST,
        name="square_sum",
    )(side.reshape(1), x)


def cut(x, edge, after):
    rows, width = x.shape
    middle = rows - 2 * edge

    def body(x_ref, after_ref, inner_ref, sem):
        copy = pltpu.make_async_copy(x_ref.at[pl.ds(edge, middle)], inner_ref, sem)
        copy.start()
        copy.wait()

    return pl.pallas_call(
        body,
        in_specs=[pl.BlockSpec(memory_space=pltpu.VMEM), pl.BlockSpec(memory_space=pl.ANY)],
        out_specs=pl.BlockSpec(memory_space=pl.ANY),
        out_shape=pltpu.HBM((middle, width), x.dtype),
        scratch_shapes=[pltpu.SemaphoreType.DMA],
        compiler_params=pltpu.CompilerParams(vmem_limit_bytes=VMEM_LIMIT),
        cost_estimate=COST,
        name="cut",
    )(pltpu.with_memory_space_constraint(x, pltpu.VMEM), after)


def ring_loop(count, slots, start, step):
    for t in range(min(slots, count)):
        start(t, t)

    def turn(t, carry):
        slot = lax.rem(t, slots)
        step(t, slot)

        @pl.when(t + slots < count)
        def _():
            start(t + slots, slot)

        return carry

    lax.fori_loop(0, count, turn, 0)


def encode(pieces, places, inv, weight, bias, parts, also):
    rows, width = sum(piece[2] for piece in pieces), pieces[0][0].shape[1]
    latents = weight.shape[1]
    part = latents // parts
    tile = tile_of(part, ENCODE_TILE)
    n, m = len(pieces), len(also)
    raw = inv is None
    inv = jnp.ones((1,), jnp.float32) if raw else inv

    def body(places_ref, inv_ref, b_ref, *refs):
        x_refs, w_ref = refs[:n], refs[n]
        o_refs = refs[n + 1 + m:n + 1 + m + parts]
        lhs, ring, lhs_sem, ring_sem = refs[n + 1 + m + parts:]

        def lhs_copy(i):
            _, first, count = pieces[i]
            place = pl.ds(pl.multiple_of(places_ref[i], 16), count)
            return pltpu.make_async_copy(
                x_refs[i].at[pl.ds(first, count)], lhs.at[place], lhs_sem.at[i])

        def columns(t):
            return pl.ds(pl.multiple_of(t * tile, tile), tile)

        def tile_copy(t, slot):
            return pltpu.make_async_copy(w_ref.at[:, columns(t)], ring.at[slot], ring_sem.at[slot])

        for i in range(n):
            lhs_copy(i).start()

        def step(t, slot):
            @pl.when(t == 0)
            def _():
                for i in range(n):
                    lhs_copy(i).wait()

            tile_copy(t, slot).wait()
            value = jnp.dot(lhs[...], ring[slot], preferred_element_type=jnp.float32)
            if not raw:
                value = value * inv_ref[0] + b_ref[:, columns(t)].astype(jnp.float32)
                value = jnp.maximum(value, 0.0).astype(jnp.bfloat16)
            per = part // tile
            for i, o_ref in enumerate(o_refs):
                @pl.when(lax.div(t, per) == i)
                def _():
                    o_ref[:, columns(lax.rem(t, per))] = value

        ring_loop(latents // tile, ENCODE_SLOTS, lambda t, slot: tile_copy(t, slot).start(), step)

    return pl.pallas_call(
        body,
        in_specs=[
            pl.BlockSpec(memory_space=pltpu.SMEM),
            pl.BlockSpec(memory_space=pltpu.SMEM),
            pl.BlockSpec(memory_space=pltpu.VMEM),
        ] + [pl.BlockSpec(memory_space=pl.ANY)] * (n + 1 + m),
        out_specs=[pl.BlockSpec(memory_space=pltpu.VMEM)] * parts,
        out_shape=[jax.ShapeDtypeStruct((rows, part), jnp.float32 if raw else jnp.bfloat16)] * parts,
        scratch_shapes=[
            pltpu.VMEM((rows, width), jnp.bfloat16),
            pltpu.VMEM((ENCODE_SLOTS, width, tile), jnp.bfloat16),
            pltpu.SemaphoreType.DMA((n,)),
            pltpu.SemaphoreType.DMA((ENCODE_SLOTS,)),
        ],
        compiler_params=pltpu.CompilerParams(vmem_limit_bytes=VMEM_LIMIT),
        cost_estimate=COST,
        name="encode",
    )(places, inv, bias, *[piece[0] for piece in pieces], weight, *also)


def activate(products, inv, bias):
    n = len(products)
    rows, part = products[0].shape

    def body(inv_ref, b_ref, *refs):
        for i in range(n):
            p_ref, o_ref = refs[i], refs[n + i]
            bias = b_ref[:, i * part:(i + 1) * part].astype(jnp.float32)

            def block(r, carry):
                here = pl.ds(pl.multiple_of(r * 16, 16), 16)
                value = p_ref[here, :] * inv_ref[0] + bias
                o_ref[here, :] = jnp.maximum(value, 0.0).astype(o_ref.dtype)
                return carry

            lax.fori_loop(0, rows // 16, block, 0, unroll=2)

    vmem = pl.BlockSpec(memory_space=pltpu.VMEM)
    return pl.pallas_call(
        body,
        in_specs=[pl.BlockSpec(memory_space=pltpu.SMEM)] + [vmem] * (1 + n),
        out_specs=[vmem] * n,
        out_shape=[jax.ShapeDtypeStruct((rows, part), jnp.bfloat16)] * n,
        compiler_params=pltpu.CompilerParams(vmem_limit_bytes=VMEM_LIMIT),
        cost_estimate=COST,
        name="activate",
    )(inv, bias, *products)


def decode(codes, earlier, own_w, cross_w, info, outs, width, also):
    parts = len(codes)
    rows, part = codes[0].shape
    latents = parts * part
    tile = tile_of(width, DECODE_TILE)
    per = width // tile
    blocks = info.shape[0] - 1
    m = len(also)

    def body(info_ref, *refs):
        code_refs, (s_ref, x_ref), refs = refs[:2 * parts], refs[2 * parts:2 * parts + 2], refs[2 * parts + 2:]
        o_refs = refs[m:m + len(outs)]
        lhs, ring, lhs_sem, ring_sem = refs[m + len(outs):]
        later = info_ref[0] != 0

        def lhs_copy(i):
            return pltpu.make_async_copy(
                code_refs[i], lhs.at[:, pl.ds(i * part, part)], lhs_sem.at[i])

        def tile_copy(source, i, t, slot):
            column = info_ref[1 + lax.div(t, per)] * width + lax.rem(t, per) * tile
            across = pl.ds(pl.multiple_of(column, tile), tile)
            return pltpu.make_async_copy(
                source.at[:, across], ring.at[slot, pl.ds(i * latents, latents)], ring_sem.at[slot, i])

        def start(t, slot):
            t = jnp.int32(t)
            tile_copy(s_ref, 0, t, slot).start()

            @pl.when(later)
            def _():
                tile_copy(x_ref, 1, t, slot).start()

        for i in range(parts):
            lhs_copy(i).start()

        @pl.when(later)
        def _():
            for i in range(parts, 2 * parts):
                lhs_copy(i).start()

        def put(t, value):
            b = lax.div(t, per)
            across = pl.ds(pl.multiple_of(lax.rem(t, per) * tile, tile), tile)
            for (block, many, spans, dtype), o_ref in zip(outs, o_refs):
                @pl.when((b >= block) & (b < block + many))
                def _():
                    here = jnp.clip(b - block, 0, many - 1)
                    at = 0
                    for row, height in spans:
                        o_ref[here, at:at + height, across] = value[row:row + height].astype(dtype)
                        at += height

        def step(t, slot):
            @pl.when(t == 0)
            def _():
                for i in range(parts):
                    lhs_copy(i).wait()

            tile_copy(s_ref, 0, t, slot).wait()

            @pl.when(later)
            def _():
                @pl.when(t == 0)
                def _():
                    for i in range(parts, 2 * parts):
                        lhs_copy(i).wait()

                tile_copy(x_ref, 1, t, slot).wait()
                put(t, jnp.dot(lhs[...], ring[slot], preferred_element_type=jnp.float32))

            @pl.when(jnp.logical_not(later))
            def _():
                put(t, jnp.dot(
                    lhs[:, :latents], ring[slot, :latents], preferred_element_type=jnp.float32))

        ring_loop(blocks * per, DECODE_SLOTS, start, step)

    return pl.pallas_call(
        body,
        in_specs=[pl.BlockSpec(memory_space=pltpu.SMEM)]
        + [pl.BlockSpec(memory_space=pl.ANY)] * (2 * parts + 2 + m),
        out_specs=[pl.BlockSpec(memory_space=pltpu.VMEM)] * len(outs),
        out_shape=[
            jax.ShapeDtypeStruct((many, sum(height for _, height in spans), width), dtype)
            for _, many, spans, dtype in outs
        ],
        scratch_shapes=[
            pltpu.VMEM((rows, 2 * latents), jnp.bfloat16),
            pltpu.VMEM((DECODE_SLOTS, 2 * latents, tile), jnp.bfloat16),
            pltpu.SemaphoreType.DMA((2 * parts,)),
            pltpu.SemaphoreType.DMA((DECODE_SLOTS, 2)),
        ],
        compiler_params=pltpu.CompilerParams(vmem_limit_bytes=VMEM_LIMIT),
        cost_estimate=COST,
        name="decode",
    )(info, *codes, *earlier, own_w, cross_w, *also)


def finale(outer_terms, inner_terms, first, bias, target, layer):
    rows, width = target.shape
    middle = inner_terms[0].shape[0]
    last = first + middle
    n, m = len(outer_terms), len(inner_terms)

    def body(layer_ref, b_ref, t_ref, *refs):
        terms = {0: refs[:n], 1: refs[n:n + m]}
        r_ref, s_ref = refs[n + m:]
        bias = b_ref[...].astype(jnp.float32)
        spans = [(0, 0, 0, first), (1, 0, first, middle), (0, first, last, rows - last)]

        def block(which, start, target_start):
            def run(r, sums):
                here = pl.ds(pl.multiple_of(start + r * 16, 16), 16)
                there = pl.ds(pl.multiple_of(target_start + r * 16, 16), 16)
                total = sum(term[here, :].astype(jnp.float32) for term in terms[which]) + bias
                goal = t_ref[there, :].astype(jnp.float32)
                r_ref[there, :] = total.astype(r_ref.dtype)
                diff = total - goal
                diff, goal = diff * diff, goal * goal
                return sums[0] + diff[:8] + diff[8:], sums[1] + goal[:8] + goal[8:]

            return run

        zero = jnp.zeros((8, width), jnp.float32)
        sums = (zero, zero)
        for which, start, target_start, count in spans:
            sums = lax.fori_loop(0, count // 16, block(which, start, target_start), sums)
        row = lax.broadcasted_iota(jnp.int32, (8, 128), 0)
        value = jnp.where(row == layer_ref[0], jnp.sum(sums[0]), 0.0)
        s_ref[...] = jnp.where(row == layer_ref[0] + 2, jnp.sum(sums[1]), value)

    vmem = pl.BlockSpec(memory_space=pltpu.VMEM)
    return pl.pallas_call(
        body,
        in_specs=[pl.BlockSpec(memory_space=pltpu.SMEM)] + [vmem] * (2 + n + m),
        out_specs=[vmem] * 2,
        out_shape=[
            jax.ShapeDtypeStruct((rows, width), jnp.bfloat16),
            jax.ShapeDtypeStruct((8, 128), jnp.float32),
        ],
        compiler_params=pltpu.CompilerParams(vmem_limit_bytes=VMEM_LIMIT),
        cost_estimate=COST,
        name="finale",
    )(layer.astype(jnp.int32).reshape(1), bias, target, *outer_terms, *inner_terms)


def mean_ratio(terms):
    n = len(terms)

    def body(*refs):
        total = sum(ref[...] for ref in refs[:n])
        ratio = total[0:2] / total[2:4]
        refs[n][...] = (ratio[0:1, 0:1] + ratio[1:2, 0:1]) / 2.0

    vmem = pl.BlockSpec(memory_space=pltpu.VMEM)
    return pl.pallas_call(
        body,
        in_specs=[vmem] * n,
        out_specs=vmem,
        out_shape=jax.ShapeDtypeStruct((1, 1), jnp.float32),
        cost_estimate=COST,
        name="mean_ratio",
    )(*terms).reshape(1)


def shifted(value, axis, distance):
    n = lax.axis_size(axis)
    return lax.ppermute(value, axis, [(i, (i + distance) % n) for i in range(n)])


def swapped(value, axis, bit):
    n = lax.axis_size(axis)
    return lax.ppermute(value, axis, [(i, i ^ bit) for i in range(n)])


def sum_over(value, axis):
    total = value
    for distance in range(1, lax.axis_size(axis)):
        total = total + shifted(value, axis, distance)
    return total


def in_hbm(value):
    return pltpu.with_memory_space_constraint(value, pltpu.HBM)


def wide(value):
    return value.astype(jnp.float32)


def local(inputs, targets, enc_weight, encoder_layer_bias, dec_self, dec_cross, dec_bias):
    layer = lax.axis_index("layer")
    lat = lax.axis_index("latent")
    n_lat = lax.axis_size("latent")
    n_tok = lax.axis_size("token")
    x_own = in_hbm(inputs[0])
    rows, model = x_own.shape
    enc_w = in_hbm(enc_weight[0])
    own_w = in_hbm(dec_self[0])
    cross_w = in_hbm(dec_cross)
    lat_dev = enc_w.shape[1]
    width = dec_bias.shape[1]
    side = lat % 2

    edge = rows * 7 // 24 // 16 * 16
    square, x_held, outer = square_sum(x_own, side.astype(jnp.int32), edge)
    square = sum_over(square, "token")
    scale = jnp.sqrt(square / (rows * n_tok * model) + 1e-06)
    inv = 1.0 / scale
    bias = lax.dynamic_slice_in_dim(
        encoder_layer_bias, lax.axis_index("token") * lat_dev, lat_dev, axis=1
    )

    group = n_lat // 4
    other, mine_bit = 1 - lat % 2, lat % 2
    far, near = 1 - (lat // 2) % 2, (lat // 2) % 2

    def info(low, highs):
        blocks = [4 * i + 2 * high + low for high in highs for i in range(group)]
        return jnp.stack([layer] + blocks).astype(jnp.int32)

    middle = rows * 13 // 24 // 16 * 16
    first = (rows - middle) // 2 // 16 * 16
    last = first + middle
    narrow = jnp.bfloat16

    def earlier_of(codes):
        return [lax.ppermute(part, "layer", [(0, 1)]) for part in codes]

    def places(*rows):
        return jnp.stack([jnp.int32(row) for row in rows])

    def products(codes, earlier, info, outs, also):
        return decode(codes, earlier, own_w, cross_w, info, outs, width, also)

    def finish(total):
        bit = 4
        while bit < n_lat:
            here = (lat // bit) % 2
            pairs = total.reshape(total.shape[0] // 2, 2, *total.shape[1:])
            away = lax.dynamic_index_in_dim(pairs, 1 - here, 1, keepdims=False)
            arrived = swapped(away.astype(narrow), "latent", bit)
            total = lax.dynamic_index_in_dim(pairs, here, 1, keepdims=False) + wide(arrived)
            bit *= 2
        return total[0]

    codes = activate(encode([(x_held, 0, rows)], places(0), None, enc_w, bias, 2, []), inv, bias)
    inner = cut(x_held, edge, codes[0])
    foreign = []
    for distance in range(1, n_tok):
        mine = shifted(outer, "token", distance)
        theirs = swapped(mine, "latent", 1)
        foreign.append((n_tok - distance, mine, theirs, shifted(inner, "token", distance)))
    earlier = earlier_of(codes)
    inside = ((first, middle),)
    outside = ((0, first), (last, rows - last))
    spans = [(0, group, inside), (group, group, inside), (0, group, outside), (group, group, outside)]
    far_sent, near_sent, far_out_sent, near_out_sent = products(
        codes, earlier, info(other, (far, near)),
        [span + (dtype,) for span, dtype in zip(spans, (narrow, narrow, jnp.float32, jnp.float32))], [])
    far_in = swapped(far_sent, "latent", 1)
    near_in = swapped(near_sent, "latent", 1)
    far_kept, near_kept, far_out_kept, near_out_kept = products(
        codes, earlier, info(mine_bit, (far, near)), [span + (jnp.float32,) for span in spans], [far_sent])
    across_in = (far_kept + wide(far_in)).astype(narrow)
    total_in = near_kept + wide(near_in) + wide(swapped(across_in, "latent", 2))

    after = across_in
    returned = []
    far_out_back, near_out_back, near_out_kept_back = [], [], []

    def joined(own, back):
        return own + sum(wide(part) for part in back)

    for back, mine, theirs, inner_rows in foreign:
        codes = encode(
            [(mine, 0, edge), (theirs, 0, edge), (inner_rows, 0, rows - 2 * edge)],
            places(side * (rows - edge), (1 - side) * (rows - edge), edge),
            inv, enc_w, bias, 1, [after])
        earlier = earlier_of(codes)

        def quarter_of(low, high, spans, dtype, also):
            *insides, outer = products(
                codes, earlier, info(low, (high,)),
                [(0, group, span, dtype) for span in spans] + [(0, group, outside, narrow)], also)
            return insides, shifted(outer, "token", back)

        (far_sent,), far_back = quarter_of(other, far, [inside], narrow, [])
        far_in = swapped(far_sent, "latent", 1)
        (far_kept,), far_kept_back = quarter_of(mine_bit, far, [inside], jnp.float32, [far_sent, total_in])
        far_out_back.append(far_back)
        ready = [(far_kept + wide(far_in)).astype(narrow)]
        across = swapped(ready[0], "latent", 2)
        if len(far_out_back) == n_tok - 1:
            ready.append(joined(far_out_sent, far_out_back).astype(narrow))
            far_out = swapped(ready[1], "latent", 1)
        cut_at = (middle // 2 + 15) // 16 * 16
        halves = [((first, cut_at),), ((first + cut_at, middle - cut_at),)]
        near_sent, near_back = quarter_of(other, near, halves, narrow, ready)
        near_in = jnp.concatenate([swapped(rows_in, "latent", 1) for rows_in in near_sent], axis=1)
        far_out_kept = far_out_kept + wide(far_kept_back)
        pins = list(near_sent)
        if len(far_out_back) == n_tok - 1:
            far_out_kept = (far_out_kept + wide(far_out)).astype(narrow)
            pins.append(far_out_kept)
        (near_kept,), near_kept_back = quarter_of(mine_bit, near, [inside], jnp.float32, pins)
        part = finish(near_kept + wide(near_in) + wide(across))
        returned.append(shifted(part.astype(narrow), "token", back))
        near_out_back.append(near_back)
        near_out_kept_back.append(near_kept_back)
        after = near_kept

    near_out = swapped(joined(near_out_sent, near_out_back).astype(narrow), "latent", 1)
    across_out = swapped(far_out_kept, "latent", 2)
    if group == 1:
        outer_terms = [near_out_kept, *near_out_kept_back, near_out, across_out]
        outer_terms = [term[0] for term in outer_terms]
    else:
        outer_terms = [finish(joined(near_out_kept, near_out_kept_back) + wide(near_out) + wide(across_out))]
    recon, sums = finale(outer_terms, [finish(total_in), *returned], first, dec_bias, targets[0], layer)

    sums = sum_over(sums, ("token", "layer"))
    loss = mean_ratio([sums] + [shifted(sums, "latent", d) for d in range(1, n_lat)])
    return (recon[None], loss)


def solution(mesh):
    return jax.shard_map(
        local,
        mesh=mesh,
        in_specs=(
            P("layer", ("groups", "token"), None),
            P("layer", ("groups", "token"), "latent"),
            P("layer", None, ("latent", "token")),
            P("layer", "latent"),
            P("layer", ("latent", "token"), None),
            P(("latent", "token"), None),
            P("layer", "latent"),
        ),
        out_specs=(P("layer", ("groups", "token"), "latent"), P("groups")),
        check_vma=False,
    )
```

```python
import jax
import jax.numpy as jnp
from jax import lax
from jax.experimental import pallas as pl
from jax.experimental.pallas import tpu as pltpu
from jax.sharding import PartitionSpec as P

VMEM_LIMIT = 28 * 1024 * 1024
ENCODE_TILE, ENCODE_SLOTS = 512, 3
DECODE_TILE, DECODE_SLOTS = 256, 6
COST = pl.CostEstimate(flops=0, bytes_accessed=0, transcendentals=0)


def tile_of(size, most):
    tile = min(size, most)
    while size % tile:
        tile //= 2
    return tile


def square_sum(x):
    rows, width = x.shape
    lanes = tile_of(width, 1024)
    loads = 4
    piece = rows // loads

    def body(x_ref, o_ref, held, sem):
        def load(i):
            place = pl.ds(i * piece, piece)
            return pltpu.make_async_copy(x_ref.at[place], held.at[place], sem.at[i])

        for i in range(loads):
            load(i).start()
        total = jnp.zeros((8, lanes), jnp.float32)
        for i in range(loads):
            load(i).wait()
            for c in range(width // lanes):
                def add(r, acc):
                    here = pl.ds(pl.multiple_of(i * piece + r * 16, 16), 16)
                    value = held[here, c * lanes:(c + 1) * lanes].astype(jnp.float32)
                    value = value * value
                    return acc + value[:8] + value[8:]

                total = lax.fori_loop(0, piece // 16, add, total, unroll=2)
        o_ref[0] = jnp.sum(total)

    return pl.pallas_call(
        body,
        in_specs=[pl.BlockSpec(memory_space=pl.ANY)],
        out_specs=[pl.BlockSpec(memory_space=pltpu.SMEM), pl.BlockSpec(memory_space=pltpu.VMEM)],
        out_shape=[jax.ShapeDtypeStruct((1,), jnp.float32), pltpu.VMEM((rows, width), x.dtype)],
        scratch_shapes=[pltpu.SemaphoreType.DMA((loads,))],
        compiler_params=pltpu.CompilerParams(vmem_limit_bytes=VMEM_LIMIT),
        cost_estimate=COST,
        name="square_sum",
    )(x)


def cut(x, first, count, after):
    width = x.shape[1]

    def body(first_ref, x_ref, after_ref, o_ref, sem):
        place = pl.ds(pl.multiple_of(first_ref[0], 16), count)
        copy = pltpu.make_async_copy(x_ref.at[place], o_ref, sem)
        copy.start()
        copy.wait()

    return pl.pallas_call(
        body,
        in_specs=[
            pl.BlockSpec(memory_space=pltpu.SMEM),
            pl.BlockSpec(memory_space=pltpu.VMEM),
            pl.BlockSpec(memory_space=pl.ANY),
        ],
        out_specs=pl.BlockSpec(memory_space=pl.ANY),
        out_shape=pltpu.HBM((count, width), x.dtype),
        scratch_shapes=[pltpu.SemaphoreType.DMA],
        compiler_params=pltpu.CompilerParams(vmem_limit_bytes=VMEM_LIMIT),
        cost_estimate=COST,
        name="cut",
    )(first.reshape(1), pltpu.with_memory_space_constraint(x, pltpu.VMEM), after)


def ring_loop(count, slots, start, step):
    for t in range(min(slots, count)):
        start(t, t)

    def turn(t, carry):
        slot = lax.rem(t, slots)
        step(t, slot)

        @pl.when(t + slots < count)
        def _():
            start(t + slots, slot)

        return carry

    lax.fori_loop(0, count, turn, 0)


def encode(pieces, places, inv, weight, bias, parts, also):
    rows, width = sum(piece[2] for piece in pieces), pieces[0][0].shape[1]
    latents = weight.shape[1]
    part = latents // parts
    tile = tile_of(part, ENCODE_TILE)
    n, m = len(pieces), len(also)

    def body(places_ref, inv_ref, b_ref, *refs):
        x_refs, w_ref = refs[:n], refs[n]
        o_refs = refs[n + 1 + m:n + 1 + m + parts]
        lhs, ring, lhs_sem, ring_sem = refs[n + 1 + m + parts:]

        def lhs_copy(i):
            _, first, count = pieces[i]
            place = pl.ds(pl.multiple_of(places_ref[i], 16), count)
            return pltpu.make_async_copy(
                x_refs[i].at[pl.ds(first, count)], lhs.at[place], lhs_sem.at[i])

        def columns(t):
            return pl.ds(pl.multiple_of(t * tile, tile), tile)

        def tile_copy(t, slot):
            return pltpu.make_async_copy(w_ref.at[:, columns(t)], ring.at[slot], ring_sem.at[slot])

        for i in range(n):
            lhs_copy(i).start()

        def step(t, slot):
            @pl.when(t == 0)
            def _():
                for i in range(n):
                    lhs_copy(i).wait()

            tile_copy(t, slot).wait()
            value = jnp.dot(lhs[...], ring[slot], preferred_element_type=jnp.float32)
            value = value * inv_ref[0] + b_ref[:, columns(t)].astype(jnp.float32)
            value = jnp.maximum(value, 0.0).astype(jnp.bfloat16)
            per = part // tile
            for i, o_ref in enumerate(o_refs):
                @pl.when(lax.div(t, per) == i)
                def _():
                    o_ref[:, columns(lax.rem(t, per))] = value

        ring_loop(latents // tile, ENCODE_SLOTS, lambda t, slot: tile_copy(t, slot).start(), step)

    return pl.pallas_call(
        body,
        in_specs=[
            pl.BlockSpec(memory_space=pltpu.SMEM),
            pl.BlockSpec(memory_space=pltpu.SMEM),
            pl.BlockSpec(memory_space=pltpu.VMEM),
        ] + [pl.BlockSpec(memory_space=pl.ANY)] * (n + 1 + m),
        out_specs=[pl.BlockSpec(memory_space=pltpu.VMEM)] * parts,
        out_shape=[jax.ShapeDtypeStruct((rows, part), jnp.bfloat16)] * parts,
        scratch_shapes=[
            pltpu.VMEM((rows, width), jnp.bfloat16),
            pltpu.VMEM((ENCODE_SLOTS, width, tile), jnp.bfloat16),
            pltpu.SemaphoreType.DMA((n,)),
            pltpu.SemaphoreType.DMA((ENCODE_SLOTS,)),
        ],
        compiler_params=pltpu.CompilerParams(vmem_limit_bytes=VMEM_LIMIT),
        cost_estimate=COST,
        name="encode",
    )(places, inv, bias, *[piece[0] for piece in pieces], weight, *also)


def decode(codes, earlier, own_w, cross_w, info, outs, width, also):
    parts = len(codes)
    rows, part = codes[0].shape
    latents = parts * part
    tile = tile_of(width, DECODE_TILE)
    per = width // tile
    blocks = info.shape[0] - 1
    m = len(also)

    def body(info_ref, *refs):
        code_refs, (s_ref, x_ref), refs = refs[:2 * parts], refs[2 * parts:2 * parts + 2], refs[2 * parts + 2:]
        o_refs = refs[m:m + len(outs)]
        lhs, ring, lhs_sem, ring_sem = refs[m + len(outs):]
        later = info_ref[0] != 0

        def lhs_copy(i):
            return pltpu.make_async_copy(
                code_refs[i], lhs.at[:, pl.ds(i * part, part)], lhs_sem.at[i])

        def tile_copy(source, i, t, slot):
            column = info_ref[1 + lax.div(t, per)] * width + lax.rem(t, per) * tile
            across = pl.ds(pl.multiple_of(column, tile), tile)
            return pltpu.make_async_copy(
                source.at[:, across], ring.at[slot, pl.ds(i * latents, latents)], ring_sem.at[slot, i])

        def start(t, slot):
            t = jnp.int32(t)
            tile_copy(s_ref, 0, t, slot).start()

            @pl.when(later)
            def _():
                tile_copy(x_ref, 1, t, slot).start()

        for i in range(parts):
            lhs_copy(i).start()

        @pl.when(later)
        def _():
            for i in range(parts, 2 * parts):
                lhs_copy(i).start()

        def put(t, value):
            b = lax.div(t, per)
            across = pl.ds(pl.multiple_of(lax.rem(t, per) * tile, tile), tile)
            for (block, many, spans, dtype), o_ref in zip(outs, o_refs):
                @pl.when((b >= block) & (b < block + many))
                def _():
                    here = jnp.clip(b - block, 0, many - 1)
                    at = 0
                    for row, height in spans:
                        o_ref[here, at:at + height, across] = value[row:row + height].astype(dtype)
                        at += height

        def step(t, slot):
            @pl.when(t == 0)
            def _():
                for i in range(parts):
                    lhs_copy(i).wait()

            tile_copy(s_ref, 0, t, slot).wait()

            @pl.when(later)
            def _():
                @pl.when(t == 0)
                def _():
                    for i in range(parts, 2 * parts):
                        lhs_copy(i).wait()

                tile_copy(x_ref, 1, t, slot).wait()
                put(t, jnp.dot(lhs[...], ring[slot], preferred_element_type=jnp.float32))

            @pl.when(jnp.logical_not(later))
            def _():
                put(t, jnp.dot(
                    lhs[:, :latents], ring[slot, :latents], preferred_element_type=jnp.float32))

        ring_loop(blocks * per, DECODE_SLOTS, start, step)

    return pl.pallas_call(
        body,
        in_specs=[pl.BlockSpec(memory_space=pltpu.SMEM)]
        + [pl.BlockSpec(memory_space=pl.ANY)] * (2 * parts + 2 + m),
        out_specs=[pl.BlockSpec(memory_space=pltpu.VMEM)] * len(outs),
        out_shape=[
            jax.ShapeDtypeStruct((many, sum(height for _, height in spans), width), dtype)
            for _, many, spans, dtype in outs
        ],
        scratch_shapes=[
            pltpu.VMEM((rows, 2 * latents), jnp.bfloat16),
            pltpu.VMEM((DECODE_SLOTS, 2 * latents, tile), jnp.bfloat16),
            pltpu.SemaphoreType.DMA((2 * parts,)),
            pltpu.SemaphoreType.DMA((DECODE_SLOTS, 2)),
        ],
        compiler_params=pltpu.CompilerParams(vmem_limit_bytes=VMEM_LIMIT),
        cost_estimate=COST,
        name="decode",
    )(info, *codes, *earlier, own_w, cross_w, *also)


def finale(outer_terms, inner_terms, first, bias, target, layer):
    rows, width = target.shape
    middle = inner_terms[0].shape[0]
    last = first + middle
    n, m = len(outer_terms), len(inner_terms)

    def body(layer_ref, b_ref, t_ref, *refs):
        terms = {0: refs[:n], 1: refs[n:n + m]}
        r_ref, s_ref = refs[n + m:]
        bias = b_ref[...].astype(jnp.float32)
        spans = [(0, 0, 0, first), (1, 0, first, middle), (0, first, last, rows - last)]

        def block(which, start, target_start):
            def run(r, sums):
                here = pl.ds(pl.multiple_of(start + r * 16, 16), 16)
                there = pl.ds(pl.multiple_of(target_start + r * 16, 16), 16)
                total = sum(term[here, :].astype(jnp.float32) for term in terms[which]) + bias
                goal = t_ref[there, :].astype(jnp.float32)
                r_ref[there, :] = total.astype(r_ref.dtype)
                diff = total - goal
                diff, goal = diff * diff, goal * goal
                return sums[0] + diff[:8] + diff[8:], sums[1] + goal[:8] + goal[8:]

            return run

        zero = jnp.zeros((8, width), jnp.float32)
        sums = (zero, zero)
        for which, start, target_start, count in spans:
            sums = lax.fori_loop(0, count // 16, block(which, start, target_start), sums)
        row = lax.broadcasted_iota(jnp.int32, (8, 128), 0)
        value = jnp.where(row == layer_ref[0], jnp.sum(sums[0]), 0.0)
        s_ref[...] = jnp.where(row == layer_ref[0] + 2, jnp.sum(sums[1]), value)

    vmem = pl.BlockSpec(memory_space=pltpu.VMEM)
    return pl.pallas_call(
        body,
        in_specs=[pl.BlockSpec(memory_space=pltpu.SMEM)] + [vmem] * (2 + n + m),
        out_specs=[vmem] * 2,
        out_shape=[
            jax.ShapeDtypeStruct((rows, width), jnp.bfloat16),
            jax.ShapeDtypeStruct((8, 128), jnp.float32),
        ],
        compiler_params=pltpu.CompilerParams(vmem_limit_bytes=VMEM_LIMIT),
        cost_estimate=COST,
        name="finale",
    )(layer.astype(jnp.int32).reshape(1), bias, target, *outer_terms, *inner_terms)


def mean_ratio(terms):
    n = len(terms)

    def body(*refs):
        total = sum(ref[...] for ref in refs[:n])
        ratio = total[0:2] / total[2:4]
        refs[n][...] = (ratio[0:1, 0:1] + ratio[1:2, 0:1]) / 2.0

    vmem = pl.BlockSpec(memory_space=pltpu.VMEM)
    return pl.pallas_call(
        body,
        in_specs=[vmem] * n,
        out_specs=vmem,
        out_shape=jax.ShapeDtypeStruct((1, 1), jnp.float32),
        cost_estimate=COST,
        name="mean_ratio",
    )(*terms).reshape(1)


def shifted(value, axis, distance):
    n = lax.axis_size(axis)
    return lax.ppermute(value, axis, [(i, (i + distance) % n) for i in range(n)])


def swapped(value, axis, bit):
    n = lax.axis_size(axis)
    return lax.ppermute(value, axis, [(i, i ^ bit) for i in range(n)])


def sum_over(value, axis):
    total = value
    for distance in range(1, lax.axis_size(axis)):
        total = total + shifted(value, axis, distance)
    return total


def in_hbm(value):
    return pltpu.with_memory_space_constraint(value, pltpu.HBM)


def wide(value):
    return value.astype(jnp.float32)


def local(inputs, targets, enc_weight, encoder_layer_bias, dec_self, dec_cross, dec_bias):
    layer = lax.axis_index("layer")
    lat = lax.axis_index("latent")
    n_lat = lax.axis_size("latent")
    n_tok = lax.axis_size("token")
    x_own = in_hbm(inputs[0])
    rows, model = x_own.shape
    enc_w = in_hbm(enc_weight[0])
    own_w = in_hbm(dec_self[0])
    cross_w = in_hbm(dec_cross)
    lat_dev = enc_w.shape[1]
    width = dec_bias.shape[1]
    side = lat % 2

    edge = rows // 4 // 16 * 16
    square, x_held = square_sum(x_own)
    square = sum_over(square, "token")
    scale = jnp.sqrt(square / (rows * n_tok * model) + 1e-06)
    inv = 1.0 / scale
    outer = cut(x_held, (side * (rows - edge)).astype(jnp.int32), edge, square)
    bias = lax.dynamic_slice_in_dim(
        encoder_layer_bias, lax.axis_index("token") * lat_dev, lat_dev, axis=1
    )

    group = n_lat // 4
    other, mine_bit = 1 - lat % 2, lat % 2
    far, near = 1 - (lat // 2) % 2, (lat // 2) % 2

    def info(low, highs):
        blocks = [4 * i + 2 * high + low for high in highs for i in range(group)]
        return jnp.stack([layer] + blocks).astype(jnp.int32)

    middle = rows * 13 // 24 // 16 * 16
    first = (rows - middle) // 2 // 16 * 16
    last = first + middle
    narrow = jnp.bfloat16

    def earlier_of(codes):
        return [lax.ppermute(part, "layer", [(0, 1)]) for part in codes]

    def places(*rows):
        return jnp.stack([jnp.int32(row) for row in rows])

    def products(codes, earlier, info, outs, also):
        return decode(codes, earlier, own_w, cross_w, info, outs, width, also)

    def finish(total):
        bit = 4
        while bit < n_lat:
            here = (lat // bit) % 2
            pairs = total.reshape(total.shape[0] // 2, 2, *total.shape[1:])
            away = lax.dynamic_index_in_dim(pairs, 1 - here, 1, keepdims=False)
            arrived = swapped(away.astype(narrow), "latent", bit)
            total = lax.dynamic_index_in_dim(pairs, here, 1, keepdims=False) + wide(arrived)
            bit *= 2
        return total[0]

    codes = encode([(x_held, 0, rows)], places(0), inv, enc_w, bias, 2, [])
    inner = cut(x_held, jnp.int32(edge), rows - 2 * edge, codes[0])
    foreign = []
    for distance in range(1, n_tok):
        mine = shifted(outer, "token", distance)
        theirs = swapped(mine, "latent", 1)
        foreign.append((n_tok - distance, mine, theirs, shifted(inner, "token", distance)))
    earlier = earlier_of(codes)
    inside = ((first, middle),)
    outside = ((0, first), (last, rows - last))
    spans = [(0, group, inside), (group, group, inside), (0, group, outside), (group, group, outside)]
    far_sent, near_sent, far_out_sent, near_out_sent = products(
        codes, earlier, info(other, (far, near)),
        [span + (dtype,) for span, dtype in zip(spans, (narrow, narrow, jnp.float32, jnp.float32))], [])
    far_in = swapped(far_sent, "latent", 1)
    near_in = swapped(near_sent, "latent", 1)
    far_kept, near_kept, far_out_kept, near_out_kept = products(
        codes, earlier, info(mine_bit, (far, near)), [span + (jnp.float32,) for span in spans], [far_sent])
    across_in = (far_kept + wide(far_in)).astype(narrow)
    total_in = near_kept + wide(near_in) + wide(swapped(across_in, "latent", 2))

    after = across_in
    returned = []
    far_out_back, near_out_back, near_out_kept_back = [], [], []

    def joined(own, back):
        return own + sum(wide(part) for part in back)

    for back, mine, theirs, inner_rows in foreign:
        codes = encode(
            [(mine, 0, edge), (theirs, 0, edge), (inner_rows, 0, rows - 2 * edge)],
            places(side * (rows - edge), (1 - side) * (rows - edge), edge),
            inv, enc_w, bias, 1, [after])
        earlier = earlier_of(codes)

        def quarter_of(low, high, spans, dtype, also):
            *insides, outer = products(
                codes, earlier, info(low, (high,)),
                [(0, group, span, dtype) for span in spans] + [(0, group, outside, narrow)], also)
            return insides, shifted(outer, "token", back)

        (far_sent,), far_back = quarter_of(other, far, [inside], narrow, [])
        far_in = swapped(far_sent, "latent", 1)
        (far_kept,), far_kept_back = quarter_of(mine_bit, far, [inside], jnp.float32, [far_sent, total_in])
        far_out_back.append(far_back)
        ready = [(far_kept + wide(far_in)).astype(narrow)]
        across = swapped(ready[0], "latent", 2)
        if len(far_out_back) == n_tok - 1:
            ready.append(joined(far_out_sent, far_out_back).astype(narrow))
            far_out = swapped(ready[1], "latent", 1)
        cut_at = (middle // 2 + 15) // 16 * 16
        halves = [((first, cut_at),), ((first + cut_at, middle - cut_at),)]
        near_sent, near_back = quarter_of(other, near, halves, narrow, ready)
        near_in = jnp.concatenate([swapped(rows_in, "latent", 1) for rows_in in near_sent], axis=1)
        far_out_kept = far_out_kept + wide(far_kept_back)
        pins = list(near_sent)
        if len(far_out_back) == n_tok - 1:
            far_out_kept = (far_out_kept + wide(far_out)).astype(narrow)
            pins.append(far_out_kept)
        (near_kept,), near_kept_back = quarter_of(mine_bit, near, [inside], jnp.float32, pins)
        part = finish(near_kept + wide(near_in) + wide(across))
        returned.append(shifted(part.astype(narrow), "token", back))
        near_out_back.append(near_back)
        near_out_kept_back.append(near_kept_back)
        after = near_kept

    near_out = swapped(joined(near_out_sent, near_out_back).astype(narrow), "latent", 1)
    across_out = swapped(far_out_kept, "latent", 2)
    if group == 1:
        outer_terms = [near_out_kept, *near_out_kept_back, near_out, across_out]
        outer_terms = [term[0] for term in outer_terms]
    else:
        outer_terms = [finish(joined(near_out_kept, near_out_kept_back) + wide(near_out) + wide(across_out))]
    recon, sums = finale(outer_terms, [finish(total_in), *returned], first, dec_bias, targets[0], layer)

    sums = sum_over(sums, ("token", "layer"))
    loss = mean_ratio([sums] + [shifted(sums, "latent", d) for d in range(1, n_lat)])
    return (recon[None], loss)


def solution(mesh):
    return jax.shard_map(
        local,
        mesh=mesh,
        in_specs=(
            P("layer", ("groups", "token"), None),
            P("layer", ("groups", "token"), "latent"),
            P("layer", None, ("latent", "token")),
            P("layer", "latent"),
            P("layer", ("latent", "token"), None),
            P(("latent", "token"), None),
            P("layer", "latent"),
        ),
        out_specs=(P("layer", ("groups", "token"), "latent"), P("groups")),
        check_vma=False,
    )
```

```python
import jax
import jax.numpy as jnp
from jax import lax
from jax.experimental import pallas as pl
from jax.experimental.pallas import tpu as pltpu
from jax.sharding import PartitionSpec as P

VMEM_LIMIT = 28 * 1024 * 1024
ENCODE_TILE, ENCODE_SLOTS = 512, 3
DECODE_TILE, DECODE_SLOTS = 256, 6
COST = pl.CostEstimate(flops=0, bytes_accessed=0, transcendentals=0)


def tile_of(size, most):
    tile = min(size, most)
    while size % tile:
        tile //= 2
    return tile


def square_sum(x):
    rows, width = x.shape
    lanes = tile_of(width, 1024)
    loads = 4
    piece = rows // loads

    def body(x_ref, o_ref, held, sem):
        def load(i):
            place = pl.ds(i * piece, piece)
            return pltpu.make_async_copy(x_ref.at[place], held.at[place], sem.at[i])

        for i in range(loads):
            load(i).start()
        total = jnp.zeros((8, lanes), jnp.float32)
        for i in range(loads):
            load(i).wait()
            for c in range(width // lanes):
                def add(r, acc):
                    here = pl.ds(pl.multiple_of(i * piece + r * 16, 16), 16)
                    value = held[here, c * lanes:(c + 1) * lanes].astype(jnp.float32)
                    value = value * value
                    return acc + value[:8] + value[8:]

                total = lax.fori_loop(0, piece // 16, add, total, unroll=2)
        o_ref[0] = jnp.sum(total)

    return pl.pallas_call(
        body,
        in_specs=[pl.BlockSpec(memory_space=pl.ANY)],
        out_specs=[pl.BlockSpec(memory_space=pltpu.SMEM), pl.BlockSpec(memory_space=pltpu.VMEM)],
        out_shape=[jax.ShapeDtypeStruct((1,), jnp.float32), pltpu.VMEM((rows, width), x.dtype)],
        scratch_shapes=[pltpu.SemaphoreType.DMA((loads,))],
        compiler_params=pltpu.CompilerParams(vmem_limit_bytes=VMEM_LIMIT),
        cost_estimate=COST,
        name="square_sum",
    )(x)


def cut(x, first, count, after):
    width = x.shape[1]

    def body(first_ref, x_ref, after_ref, o_ref, sem):
        place = pl.ds(pl.multiple_of(first_ref[0], 16), count)
        copy = pltpu.make_async_copy(x_ref.at[place], o_ref, sem)
        copy.start()
        copy.wait()

    return pl.pallas_call(
        body,
        in_specs=[
            pl.BlockSpec(memory_space=pltpu.SMEM),
            pl.BlockSpec(memory_space=pltpu.VMEM),
            pl.BlockSpec(memory_space=pl.ANY),
        ],
        out_specs=pl.BlockSpec(memory_space=pl.ANY),
        out_shape=pltpu.HBM((count, width), x.dtype),
        scratch_shapes=[pltpu.SemaphoreType.DMA],
        compiler_params=pltpu.CompilerParams(vmem_limit_bytes=VMEM_LIMIT),
        cost_estimate=COST,
        name="cut",
    )(first.reshape(1), pltpu.with_memory_space_constraint(x, pltpu.VMEM), after)


def ring_loop(count, slots, start, step):
    for t in range(min(slots, count)):
        start(t, t)

    def turn(t, carry):
        slot = lax.rem(t, slots)
        step(t, slot)

        @pl.when(t + slots < count)
        def _():
            start(t + slots, slot)

        return carry

    lax.fori_loop(0, count, turn, 0)


def encode(pieces, places, inv, weight, bias, parts, also):
    rows, width = sum(piece[2] for piece in pieces), pieces[0][0].shape[1]
    latents = weight.shape[1]
    part = latents // parts
    tile = tile_of(part, ENCODE_TILE)
    n, m = len(pieces), len(also)

    def body(places_ref, inv_ref, b_ref, *refs):
        x_refs, w_ref = refs[:n], refs[n]
        o_refs = refs[n + 1 + m:n + 1 + m + parts]
        lhs, ring, lhs_sem, ring_sem = refs[n + 1 + m + parts:]

        def lhs_copy(i):
            _, first, count = pieces[i]
            place = pl.ds(pl.multiple_of(places_ref[i], 16), count)
            return pltpu.make_async_copy(
                x_refs[i].at[pl.ds(first, count)], lhs.at[place], lhs_sem.at[i])

        def columns(t):
            return pl.ds(pl.multiple_of(t * tile, tile), tile)

        def tile_copy(t, slot):
            return pltpu.make_async_copy(w_ref.at[:, columns(t)], ring.at[slot], ring_sem.at[slot])

        for i in range(n):
            lhs_copy(i).start()

        def step(t, slot):
            @pl.when(t == 0)
            def _():
                for i in range(n):
                    lhs_copy(i).wait()

            tile_copy(t, slot).wait()
            value = jnp.dot(lhs[...], ring[slot], preferred_element_type=jnp.float32)
            value = value * inv_ref[0] + b_ref[:, columns(t)].astype(jnp.float32)
            value = jnp.maximum(value, 0.0).astype(jnp.bfloat16)
            per = part // tile
            for i, o_ref in enumerate(o_refs):
                @pl.when(lax.div(t, per) == i)
                def _():
                    o_ref[:, columns(lax.rem(t, per))] = value

        ring_loop(latents // tile, ENCODE_SLOTS, lambda t, slot: tile_copy(t, slot).start(), step)

    return pl.pallas_call(
        body,
        in_specs=[
            pl.BlockSpec(memory_space=pltpu.SMEM),
            pl.BlockSpec(memory_space=pltpu.SMEM),
            pl.BlockSpec(memory_space=pltpu.VMEM),
        ] + [pl.BlockSpec(memory_space=pl.ANY)] * (n + 1 + m),
        out_specs=[pl.BlockSpec(memory_space=pltpu.VMEM)] * parts,
        out_shape=[jax.ShapeDtypeStruct((rows, part), jnp.bfloat16)] * parts,
        scratch_shapes=[
            pltpu.VMEM((rows, width), jnp.bfloat16),
            pltpu.VMEM((ENCODE_SLOTS, width, tile), jnp.bfloat16),
            pltpu.SemaphoreType.DMA((n,)),
            pltpu.SemaphoreType.DMA((ENCODE_SLOTS,)),
        ],
        compiler_params=pltpu.CompilerParams(vmem_limit_bytes=VMEM_LIMIT),
        cost_estimate=COST,
        name="encode",
    )(places, inv, bias, *[piece[0] for piece in pieces], weight, *also)


def decode(codes, earlier, own_w, cross_w, info, outs, width, also):
    parts = len(codes)
    rows, part = codes[0].shape
    latents = parts * part
    tile = tile_of(width, DECODE_TILE)
    per = width // tile
    blocks = info.shape[0] - 1
    m = len(also)

    def body(info_ref, *refs):
        code_refs, (s_ref, x_ref), refs = refs[:2 * parts], refs[2 * parts:2 * parts + 2], refs[2 * parts + 2:]
        o_refs = refs[m:m + len(outs)]
        lhs, ring, lhs_sem, ring_sem = refs[m + len(outs):]
        later = info_ref[0] != 0

        def lhs_copy(i):
            return pltpu.make_async_copy(
                code_refs[i], lhs.at[:, pl.ds(i * part, part)], lhs_sem.at[i])

        def tile_copy(source, i, t, slot):
            column = info_ref[1 + lax.div(t, per)] * width + lax.rem(t, per) * tile
            across = pl.ds(pl.multiple_of(column, tile), tile)
            return pltpu.make_async_copy(
                source.at[:, across], ring.at[slot, pl.ds(i * latents, latents)], ring_sem.at[slot, i])

        def start(t, slot):
            t = jnp.int32(t)
            tile_copy(s_ref, 0, t, slot).start()

            @pl.when(later)
            def _():
                tile_copy(x_ref, 1, t, slot).start()

        for i in range(parts):
            lhs_copy(i).start()

        @pl.when(later)
        def _():
            for i in range(parts, 2 * parts):
                lhs_copy(i).start()

        def put(t, value):
            b = lax.div(t, per)
            across = pl.ds(pl.multiple_of(lax.rem(t, per) * tile, tile), tile)
            for (block, many, spans, dtype), o_ref in zip(outs, o_refs):
                @pl.when((b >= block) & (b < block + many))
                def _():
                    here = jnp.clip(b - block, 0, many - 1)
                    at = 0
                    for row, height in spans:
                        o_ref[here, at:at + height, across] = value[row:row + height].astype(dtype)
                        at += height

        def step(t, slot):
            @pl.when(t == 0)
            def _():
                for i in range(parts):
                    lhs_copy(i).wait()

            tile_copy(s_ref, 0, t, slot).wait()

            @pl.when(later)
            def _():
                @pl.when(t == 0)
                def _():
                    for i in range(parts, 2 * parts):
                        lhs_copy(i).wait()

                tile_copy(x_ref, 1, t, slot).wait()
                put(t, jnp.dot(lhs[...], ring[slot], preferred_element_type=jnp.float32))

            @pl.when(jnp.logical_not(later))
            def _():
                put(t, jnp.dot(
                    lhs[:, :latents], ring[slot, :latents], preferred_element_type=jnp.float32))

        ring_loop(blocks * per, DECODE_SLOTS, start, step)

    return pl.pallas_call(
        body,
        in_specs=[pl.BlockSpec(memory_space=pltpu.SMEM)]
        + [pl.BlockSpec(memory_space=pl.ANY)] * (2 * parts + 2 + m),
        out_specs=[pl.BlockSpec(memory_space=pltpu.VMEM)] * len(outs),
        out_shape=[
            jax.ShapeDtypeStruct((many, sum(height for _, height in spans), width), dtype)
            for _, many, spans, dtype in outs
        ],
        scratch_shapes=[
            pltpu.VMEM((rows, 2 * latents), jnp.bfloat16),
            pltpu.VMEM((DECODE_SLOTS, 2 * latents, tile), jnp.bfloat16),
            pltpu.SemaphoreType.DMA((2 * parts,)),
            pltpu.SemaphoreType.DMA((DECODE_SLOTS, 2)),
        ],
        compiler_params=pltpu.CompilerParams(vmem_limit_bytes=VMEM_LIMIT),
        cost_estimate=COST,
        name="decode",
    )(info, *codes, *earlier, own_w, cross_w, *also)


def finale(outer_terms, inner_terms, first, bias, target, layer):
    rows, width = target.shape
    middle = inner_terms[0].shape[0]
    last = first + middle
    n, m = len(outer_terms), len(inner_terms)

    def body(layer_ref, b_ref, t_ref, *refs):
        terms = {0: refs[:n], 1: refs[n:n + m]}
        r_ref, s_ref = refs[n + m:]
        bias = b_ref[...].astype(jnp.float32)
        spans = [(0, 0, 0, first), (1, 0, first, middle), (0, first, last, rows - last)]

        def block(which, start, target_start):
            def run(r, sums):
                here = pl.ds(pl.multiple_of(start + r * 16, 16), 16)
                there = pl.ds(pl.multiple_of(target_start + r * 16, 16), 16)
                total = sum(term[here, :].astype(jnp.float32) for term in terms[which]) + bias
                goal = t_ref[there, :].astype(jnp.float32)
                r_ref[there, :] = total.astype(r_ref.dtype)
                diff = total - goal
                diff, goal = diff * diff, goal * goal
                return sums[0] + diff[:8] + diff[8:], sums[1] + goal[:8] + goal[8:]

            return run

        zero = jnp.zeros((8, width), jnp.float32)
        sums = (zero, zero)
        for which, start, target_start, count in spans:
            sums = lax.fori_loop(0, count // 16, block(which, start, target_start), sums)
        row = lax.broadcasted_iota(jnp.int32, (8, 128), 0)
        value = jnp.where(row == layer_ref[0], jnp.sum(sums[0]), 0.0)
        s_ref[...] = jnp.where(row == layer_ref[0] + 2, jnp.sum(sums[1]), value)

    vmem = pl.BlockSpec(memory_space=pltpu.VMEM)
    return pl.pallas_call(
        body,
        in_specs=[pl.BlockSpec(memory_space=pltpu.SMEM)] + [vmem] * (2 + n + m),
        out_specs=[vmem] * 2,
        out_shape=[
            jax.ShapeDtypeStruct((rows, width), jnp.bfloat16),
            jax.ShapeDtypeStruct((8, 128), jnp.float32),
        ],
        compiler_params=pltpu.CompilerParams(vmem_limit_bytes=VMEM_LIMIT),
        cost_estimate=COST,
        name="finale",
    )(layer.astype(jnp.int32).reshape(1), bias, target, *outer_terms, *inner_terms)


def summed(terms, also):
    n = len(terms)
    shape = terms[0].shape

    def body(*refs):
        o_ref = refs[-1]

        def block(r, carry):
            here = pl.ds(pl.multiple_of(r * 16, 16), 16)
            for g in range(shape[0]):
                o_ref[g, here, :] = sum(ref[g, here, :].astype(jnp.float32) for ref in refs[:n])
            return carry

        lax.fori_loop(0, shape[1] // 16, block, 0)

    vmem = pl.BlockSpec(memory_space=pltpu.VMEM)
    return pl.pallas_call(
        body,
        in_specs=[vmem] * n + [pl.BlockSpec(memory_space=pl.ANY)] * len(also),
        out_specs=vmem,
        out_shape=jax.ShapeDtypeStruct(shape, jnp.float32),
        compiler_params=pltpu.CompilerParams(vmem_limit_bytes=VMEM_LIMIT),
        cost_estimate=COST,
        name="summed",
    )(*terms, *also)


def mean_ratio(terms):
    n = len(terms)

    def body(*refs):
        total = sum(ref[...] for ref in refs[:n])
        ratio = total[0:2] / total[2:4]
        refs[n][...] = (ratio[0:1, 0:1] + ratio[1:2, 0:1]) / 2.0

    vmem = pl.BlockSpec(memory_space=pltpu.VMEM)
    return pl.pallas_call(
        body,
        in_specs=[vmem] * n,
        out_specs=vmem,
        out_shape=jax.ShapeDtypeStruct((1, 1), jnp.float32),
        cost_estimate=COST,
        name="mean_ratio",
    )(*terms).reshape(1)


def shifted(value, axis, distance):
    n = lax.axis_size(axis)
    return lax.ppermute(value, axis, [(i, (i + distance) % n) for i in range(n)])


def swapped(value, axis, bit):
    n = lax.axis_size(axis)
    return lax.ppermute(value, axis, [(i, i ^ bit) for i in range(n)])


def sum_over(value, axis):
    total = value
    for distance in range(1, lax.axis_size(axis)):
        total = total + shifted(value, axis, distance)
    return total


def in_hbm(value):
    return pltpu.with_memory_space_constraint(value, pltpu.HBM)


def wide(value):
    return value.astype(jnp.float32)


def local(inputs, targets, enc_weight, encoder_layer_bias, dec_self, dec_cross, dec_bias):
    layer = lax.axis_index("layer")
    lat = lax.axis_index("latent")
    n_lat = lax.axis_size("latent")
    n_tok = lax.axis_size("token")
    x_own = in_hbm(inputs[0])
    rows, model = x_own.shape
    enc_w = in_hbm(enc_weight[0])
    own_w = in_hbm(dec_self[0])
    cross_w = in_hbm(dec_cross)
    lat_dev = enc_w.shape[1]
    width = dec_bias.shape[1]
    side = lat % 2

    edge = rows // 4 // 16 * 16
    square, x_held = square_sum(x_own)
    square = sum_over(square, "token")
    scale = jnp.sqrt(square / (rows * n_tok * model) + 1e-06)
    inv = 1.0 / scale
    outer = cut(x_held, (side * (rows - edge)).astype(jnp.int32), edge, square)
    bias = lax.dynamic_slice_in_dim(
        encoder_layer_bias, lax.axis_index("token") * lat_dev, lat_dev, axis=1
    )

    group = n_lat // 4
    other, mine_bit = 1 - lat % 2, lat % 2
    far, near = 1 - (lat // 2) % 2, (lat // 2) % 2

    def info(low, highs):
        blocks = [4 * i + 2 * high + low for high in highs for i in range(group)]
        return jnp.stack([layer] + blocks).astype(jnp.int32)

    middle = rows * 13 // 24 // 16 * 16
    first = (rows - middle) // 2 // 16 * 16
    last = first + middle
    narrow = jnp.bfloat16

    def earlier_of(codes):
        return [lax.ppermute(part, "layer", [(0, 1)]) for part in codes]

    def places(*rows):
        return jnp.stack([jnp.int32(row) for row in rows])

    def products(codes, earlier, info, outs, also):
        return decode(codes, earlier, own_w, cross_w, info, outs, width, also)

    def finish(total):
        bit = 4
        while bit < n_lat:
            here = (lat // bit) % 2
            pairs = total.reshape(total.shape[0] // 2, 2, *total.shape[1:])
            away = lax.dynamic_index_in_dim(pairs, 1 - here, 1, keepdims=False)
            arrived = swapped(away.astype(narrow), "latent", bit)
            total = lax.dynamic_index_in_dim(pairs, here, 1, keepdims=False) + wide(arrived)
            bit *= 2
        return total[0]

    codes = encode([(x_held, 0, rows)], places(0), inv, enc_w, bias, 2, [])
    inner = cut(x_held, jnp.int32(edge), rows - 2 * edge, codes[0])
    foreign = []
    for distance in range(1, n_tok):
        mine = shifted(outer, "token", distance)
        theirs = swapped(mine, "latent", 1)
        foreign.append((n_tok - distance, mine, theirs, shifted(inner, "token", distance)))
    earlier = earlier_of(codes)
    inside = ((first, middle),)
    outside = ((0, first), (last, rows - last))
    spans = [(0, group, inside), (group, group, inside), (0, group, outside), (group, group, outside)]
    far_sent, near_sent, far_out_sent, near_out_sent = products(
        codes, earlier, info(other, (far, near)),
        [span + (dtype,) for span, dtype in zip(spans, (narrow, narrow, jnp.float32, jnp.float32))], [])
    far_in = swapped(far_sent, "latent", 1)
    near_in = swapped(near_sent, "latent", 1)
    far_kept, near_kept, far_out_kept, near_out_kept = products(
        codes, earlier, info(mine_bit, (far, near)), [span + (jnp.float32,) for span in spans], [far_sent])
    across_in = (far_kept + wide(far_in)).astype(narrow)
    across_there = swapped(across_in, "latent", 2)
    total_in = near_kept + wide(near_in)

    after = across_in
    returned = []
    far_out_back, near_out_back, near_out_kept_back = [], [], []

    def joined(own, back):
        return own + sum(wide(part) for part in back)

    for back, mine, theirs, inner_rows in foreign:
        codes = encode(
            [(mine, 0, edge), (theirs, 0, edge), (inner_rows, 0, rows - 2 * edge)],
            places(side * (rows - edge), (1 - side) * (rows - edge), edge),
            inv, enc_w, bias, 1, [after])
        earlier = earlier_of(codes)

        def quarter_of(low, high, spans, dtype, also):
            *insides, outer = products(
                codes, earlier, info(low, (high,)),
                [(0, group, span, dtype) for span in spans] + [(0, group, outside, narrow)], also)
            return insides, shifted(outer, "token", back)

        (far_sent,), far_back = quarter_of(other, far, [inside], narrow, [])
        far_in = swapped(far_sent, "latent", 1)
        halves = [inside]
        near_sent, near_back = quarter_of(other, near, halves, narrow, [far_sent])
        near_in = [swapped(rows_in, "latent", 1) for rows_in in near_sent]
        near_in = jnp.concatenate(near_in, axis=1) if len(near_in) > 1 else near_in[0]
        far_out_back.append(far_back)
        pins = list(near_sent)
        if not returned:
            total_in = summed([total_in, across_there], near_sent)
            pins.append(total_in)
        if len(far_out_back) == n_tok - 1:
            pins.append(joined(far_out_sent, far_out_back).astype(narrow))
            far_out = swapped(pins[-1], "latent", 1)
        (far_kept,), far_kept_back = quarter_of(mine_bit, far, [inside], jnp.float32, pins)
        pins = [(far_kept + wide(far_in)).astype(narrow)]
        across = swapped(pins[0], "latent", 2)
        far_out_kept = far_out_kept + wide(far_kept_back)
        if len(far_out_back) == n_tok - 1:
            far_out_kept = (far_out_kept + wide(far_out)).astype(narrow)

        (near_kept,), near_kept_back = quarter_of(mine_bit, near, [inside], jnp.float32, pins)
        part = finish(near_kept + wide(near_in) + wide(across))
        returned.append(shifted(part.astype(narrow), "token", back))
        near_out_back.append(near_back)
        near_out_kept_back.append(near_kept_back)
        after = near_kept

    near_out = swapped(joined(near_out_sent, near_out_back).astype(narrow), "latent", 1)
    across_out = swapped(far_out_kept, "latent", 2)
    if group == 1:
        outer_terms = [near_out_kept, *near_out_kept_back, near_out, across_out]
        outer_terms = [term[0] for term in outer_terms]
    else:
        outer_terms = [finish(joined(near_out_kept, near_out_kept_back) + wide(near_out) + wide(across_out))]
    recon, sums = finale(outer_terms, [finish(total_in), *returned], first, dec_bias, targets[0], layer)

    sums = sum_over(sums, ("token", "layer"))
    loss = mean_ratio([sums] + [shifted(sums, "latent", d) for d in range(1, n_lat)])
    return (recon[None], loss)


def solution(mesh):
    return jax.shard_map(
        local,
        mesh=mesh,
        in_specs=(
            P("layer", ("groups", "token"), None),
            P("layer", ("groups", "token"), "latent"),
            P("layer", None, ("latent", "token")),
            P("layer", "latent"),
            P("layer", ("latent", "token"), None),
            P(("latent", "token"), None),
            P("layer", "latent"),
        ),
        out_specs=(P("layer", ("groups", "token"), "latent"), P("groups")),
        check_vma=False,
    )
```

```python
import jax
import jax.numpy as jnp
from jax import lax
from jax.experimental import pallas as pl
from jax.experimental.pallas import tpu as pltpu
from jax.sharding import PartitionSpec as P

VMEM_LIMIT = 28 * 1024 * 1024
ENCODE_TILE, ENCODE_SLOTS = 512, 3
DECODE_TILE, DECODE_SLOTS = 256, 6
COST = pl.CostEstimate(flops=0, bytes_accessed=0, transcendentals=0)


def tile_of(size, most):
    tile = min(size, most)
    while size % tile:
        tile //= 2
    return tile


def square_sum(x):
    rows, width = x.shape
    lanes = tile_of(width, 1024)
    loads = 4
    piece = rows // loads

    def body(x_ref, o_ref, held, sem):
        def load(i):
            place = pl.ds(i * piece, piece)
            return pltpu.make_async_copy(x_ref.at[place], held.at[place], sem.at[i])

        for i in range(loads):
            load(i).start()
        total = jnp.zeros((8, lanes), jnp.float32)
        for i in range(loads):
            load(i).wait()
            for c in range(width // lanes):
                def add(r, acc):
                    here = pl.ds(pl.multiple_of(i * piece + r * 16, 16), 16)
                    value = held[here, c * lanes:(c + 1) * lanes].astype(jnp.float32)
                    value = value * value
                    return acc + value[:8] + value[8:]

                total = lax.fori_loop(0, piece // 16, add, total, unroll=2)
        o_ref[0] = jnp.sum(total)

    return pl.pallas_call(
        body,
        in_specs=[pl.BlockSpec(memory_space=pl.ANY)],
        out_specs=[pl.BlockSpec(memory_space=pltpu.SMEM), pl.BlockSpec(memory_space=pltpu.VMEM)],
        out_shape=[jax.ShapeDtypeStruct((1,), jnp.float32), pltpu.VMEM((rows, width), x.dtype)],
        scratch_shapes=[pltpu.SemaphoreType.DMA((loads,))],
        compiler_params=pltpu.CompilerParams(vmem_limit_bytes=VMEM_LIMIT),
        cost_estimate=COST,
        name="square_sum",
    )(x)


def cut(x, first, count, after):
    width = x.shape[1]

    def body(first_ref, x_ref, after_ref, o_ref, sem):
        place = pl.ds(pl.multiple_of(first_ref[0], 16), count)
        copy = pltpu.make_async_copy(x_ref.at[place], o_ref, sem)
        copy.start()
        copy.wait()

    return pl.pallas_call(
        body,
        in_specs=[
            pl.BlockSpec(memory_space=pltpu.SMEM),
            pl.BlockSpec(memory_space=pltpu.VMEM),
            pl.BlockSpec(memory_space=pl.ANY),
        ],
        out_specs=pl.BlockSpec(memory_space=pl.ANY),
        out_shape=pltpu.HBM((count, width), x.dtype),
        scratch_shapes=[pltpu.SemaphoreType.DMA],
        compiler_params=pltpu.CompilerParams(vmem_limit_bytes=VMEM_LIMIT),
        cost_estimate=COST,
        name="cut",
    )(first.reshape(1), pltpu.with_memory_space_constraint(x, pltpu.VMEM), after)


def ring_loop(count, slots, start, step):
    for t in range(min(slots, count)):
        start(t, t)

    def turn(t, carry):
        slot = lax.rem(t, slots)
        step(t, slot)

        @pl.when(t + slots < count)
        def _():
            start(t + slots, slot)

        return carry

    lax.fori_loop(0, count, turn, 0)


def encode(pieces, places, inv, weight, bias, parts, also):
    rows, width = sum(piece[2] for piece in pieces), pieces[0][0].shape[1]
    latents = weight.shape[1]
    part = latents // parts
    tile = tile_of(part, ENCODE_TILE)
    n, m = len(pieces), len(also)

    def body(places_ref, inv_ref, b_ref, *refs):
        x_refs, w_ref = refs[:n], refs[n]
        o_refs = refs[n + 1 + m:n + 1 + m + parts]
        lhs, ring, lhs_sem, ring_sem = refs[n + 1 + m + parts:]

        def lhs_copy(i):
            _, first, count = pieces[i]
            place = pl.ds(pl.multiple_of(places_ref[i], 16), count)
            return pltpu.make_async_copy(
                x_refs[i].at[pl.ds(first, count)], lhs.at[place], lhs_sem.at[i])

        def columns(t):
            return pl.ds(pl.multiple_of(t * tile, tile), tile)

        def tile_copy(t, slot):
            return pltpu.make_async_copy(w_ref.at[:, columns(t)], ring.at[slot], ring_sem.at[slot])

        for i in range(n):
            lhs_copy(i).start()

        def step(t, slot):
            @pl.when(t == 0)
            def _():
                for i in range(n):
                    lhs_copy(i).wait()

            tile_copy(t, slot).wait()
            value = jnp.dot(lhs[...], ring[slot], preferred_element_type=jnp.float32)
            value = value * inv_ref[0] + b_ref[:, columns(t)].astype(jnp.float32)
            value = jnp.maximum(value, 0.0).astype(jnp.bfloat16)
            per = part // tile
            for i, o_ref in enumerate(o_refs):
                @pl.when(lax.div(t, per) == i)
                def _():
                    o_ref[:, columns(lax.rem(t, per))] = value

        ring_loop(latents // tile, ENCODE_SLOTS, lambda t, slot: tile_copy(t, slot).start(), step)

    return pl.pallas_call(
        body,
        in_specs=[
            pl.BlockSpec(memory_space=pltpu.SMEM),
            pl.BlockSpec(memory_space=pltpu.SMEM),
            pl.BlockSpec(memory_space=pltpu.VMEM),
        ] + [pl.BlockSpec(memory_space=pl.ANY)] * (n + 1 + m),
        out_specs=[pl.BlockSpec(memory_space=pltpu.VMEM)] * parts,
        out_shape=[jax.ShapeDtypeStruct((rows, part), jnp.bfloat16)] * parts,
        scratch_shapes=[
            pltpu.VMEM((rows, width), jnp.bfloat16),
            pltpu.VMEM((ENCODE_SLOTS, width, tile), jnp.bfloat16),
            pltpu.SemaphoreType.DMA((n,)),
            pltpu.SemaphoreType.DMA((ENCODE_SLOTS,)),
        ],
        compiler_params=pltpu.CompilerParams(vmem_limit_bytes=VMEM_LIMIT),
        cost_estimate=COST,
        name="encode",
    )(places, inv, bias, *[piece[0] for piece in pieces], weight, *also)


def decode(codes, earlier, own_w, cross_w, info, outs, width, also):
    parts = len(codes)
    rows, part = codes[0].shape
    latents = parts * part
    tile = tile_of(width, DECODE_TILE)
    per = width // tile
    blocks = info.shape[0] - 1
    m = len(also)

    def body(info_ref, *refs):
        code_refs, (s_ref, x_ref), refs = refs[:2 * parts], refs[2 * parts:2 * parts + 2], refs[2 * parts + 2:]
        o_refs = refs[m:m + len(outs)]
        lhs, ring, lhs_sem, ring_sem = refs[m + len(outs):]
        later = info_ref[0] != 0

        def lhs_copy(i):
            return pltpu.make_async_copy(
                code_refs[i], lhs.at[:, pl.ds(i * part, part)], lhs_sem.at[i])

        def tile_copy(source, i, t, slot):
            column = info_ref[1 + lax.div(t, per)] * width + lax.rem(t, per) * tile
            across = pl.ds(pl.multiple_of(column, tile), tile)
            return pltpu.make_async_copy(
                source.at[:, across], ring.at[slot, pl.ds(i * latents, latents)], ring_sem.at[slot, i])

        def start(t, slot):
            t = jnp.int32(t)
            tile_copy(s_ref, 0, t, slot).start()

            @pl.when(later)
            def _():
                tile_copy(x_ref, 1, t, slot).start()

        for i in range(parts):
            lhs_copy(i).start()

        @pl.when(later)
        def _():
            for i in range(parts, 2 * parts):
                lhs_copy(i).start()

        def put(t, value):
            b = lax.div(t, per)
            across = pl.ds(pl.multiple_of(lax.rem(t, per) * tile, tile), tile)
            for (block, many, spans, dtype), o_ref in zip(outs, o_refs):
                @pl.when((b >= block) & (b < block + many))
                def _():
                    here = jnp.clip(b - block, 0, many - 1)
                    at = 0
                    for row, height in spans:
                        o_ref[here, at:at + height, across] = value[row:row + height].astype(dtype)
                        at += height

        def step(t, slot):
            @pl.when(t == 0)
            def _():
                for i in range(parts):
                    lhs_copy(i).wait()

            tile_copy(s_ref, 0, t, slot).wait()

            @pl.when(later)
            def _():
                @pl.when(t == 0)
                def _():
                    for i in range(parts, 2 * parts):
                        lhs_copy(i).wait()

                tile_copy(x_ref, 1, t, slot).wait()
                put(t, jnp.dot(lhs[...], ring[slot], preferred_element_type=jnp.float32))

            @pl.when(jnp.logical_not(later))
            def _():
                put(t, jnp.dot(
                    lhs[:, :latents], ring[slot, :latents], preferred_element_type=jnp.float32))

        ring_loop(blocks * per, DECODE_SLOTS, start, step)

    return pl.pallas_call(
        body,
        in_specs=[pl.BlockSpec(memory_space=pltpu.SMEM)]
        + [pl.BlockSpec(memory_space=pl.ANY)] * (2 * parts + 2 + m),
        out_specs=[pl.BlockSpec(memory_space=pltpu.VMEM)] * len(outs),
        out_shape=[
            jax.ShapeDtypeStruct((many, sum(height for _, height in spans), width), dtype)
            for _, many, spans, dtype in outs
        ],
        scratch_shapes=[
            pltpu.VMEM((rows, 2 * latents), jnp.bfloat16),
            pltpu.VMEM((DECODE_SLOTS, 2 * latents, tile), jnp.bfloat16),
            pltpu.SemaphoreType.DMA((2 * parts,)),
            pltpu.SemaphoreType.DMA((DECODE_SLOTS, 2)),
        ],
        compiler_params=pltpu.CompilerParams(vmem_limit_bytes=VMEM_LIMIT),
        cost_estimate=COST,
        name="decode",
    )(info, *codes, *earlier, own_w, cross_w, *also)


def finale(outer_terms, inner_terms, first, bias, target, layer):
    rows, width = target.shape
    middle = inner_terms[0].shape[0]
    last = first + middle
    n, m = len(outer_terms), len(inner_terms)

    def body(layer_ref, b_ref, t_ref, *refs):
        terms = {0: refs[:n], 1: refs[n:n + m]}
        r_ref, s_ref = refs[n + m:]
        bias = b_ref[...].astype(jnp.float32)
        spans = [(0, 0, 0, first), (1, 0, first, middle), (0, first, last, rows - last)]

        def block(which, start, target_start):
            def run(r, sums):
                here = pl.ds(pl.multiple_of(start + r * 16, 16), 16)
                there = pl.ds(pl.multiple_of(target_start + r * 16, 16), 16)
                total = sum(term[here, :].astype(jnp.float32) for term in terms[which]) + bias
                goal = t_ref[there, :].astype(jnp.float32)
                r_ref[there, :] = total.astype(r_ref.dtype)
                diff = total - goal
                diff, goal = diff * diff, goal * goal
                return sums[0] + diff[:8] + diff[8:], sums[1] + goal[:8] + goal[8:]

            return run

        zero = jnp.zeros((8, width), jnp.float32)
        sums = (zero, zero)
        for which, start, target_start, count in spans:
            sums = lax.fori_loop(0, count // 16, block(which, start, target_start), sums)
        row = lax.broadcasted_iota(jnp.int32, (8, 128), 0)
        value = jnp.where(row == layer_ref[0], jnp.sum(sums[0]), 0.0)
        s_ref[...] = jnp.where(row == layer_ref[0] + 2, jnp.sum(sums[1]), value)

    vmem = pl.BlockSpec(memory_space=pltpu.VMEM)
    return pl.pallas_call(
        body,
        in_specs=[pl.BlockSpec(memory_space=pltpu.SMEM)] + [vmem] * (2 + n + m),
        out_specs=[vmem] * 2,
        out_shape=[
            jax.ShapeDtypeStruct((rows, width), jnp.bfloat16),
            jax.ShapeDtypeStruct((8, 128), jnp.float32),
        ],
        compiler_params=pltpu.CompilerParams(vmem_limit_bytes=VMEM_LIMIT),
        cost_estimate=COST,
        name="finale",
    )(layer.astype(jnp.int32).reshape(1), bias, target, *outer_terms, *inner_terms)


def summed(terms, also):
    n = len(terms)
    shape = terms[0].shape

    def body(*refs):
        o_ref = refs[-1]

        def block(r, carry):
            here = pl.ds(pl.multiple_of(r * 16, 16), 16)
            for g in range(shape[0]):
                o_ref[g, here, :] = sum(ref[g, here, :].astype(jnp.float32) for ref in refs[:n])
            return carry

        lax.fori_loop(0, shape[1] // 16, block, 0)

    vmem = pl.BlockSpec(memory_space=pltpu.VMEM)
    return pl.pallas_call(
        body,
        in_specs=[vmem] * n + [pl.BlockSpec(memory_space=pl.ANY)] * len(also),
        out_specs=vmem,
        out_shape=jax.ShapeDtypeStruct(shape, jnp.float32),
        compiler_params=pltpu.CompilerParams(vmem_limit_bytes=VMEM_LIMIT),
        cost_estimate=COST,
        name="summed",
    )(*terms, *also)


def mean_ratio(terms):
    n = len(terms)

    def body(*refs):
        total = sum(ref[...] for ref in refs[:n])
        ratio = total[0:2] / total[2:4]
        refs[n][...] = (ratio[0:1, 0:1] + ratio[1:2, 0:1]) / 2.0

    vmem = pl.BlockSpec(memory_space=pltpu.VMEM)
    return pl.pallas_call(
        body,
        in_specs=[vmem] * n,
        out_specs=vmem,
        out_shape=jax.ShapeDtypeStruct((1, 1), jnp.float32),
        cost_estimate=COST,
        name="mean_ratio",
    )(*terms).reshape(1)


def shifted(value, axis, distance):
    n = lax.axis_size(axis)
    return lax.ppermute(value, axis, [(i, (i + distance) % n) for i in range(n)])


def swapped(value, axis, bit):
    n = lax.axis_size(axis)
    return lax.ppermute(value, axis, [(i, i ^ bit) for i in range(n)])


def sum_over(value, axis):
    total = value
    for distance in range(1, lax.axis_size(axis)):
        total = total + shifted(value, axis, distance)
    return total


def in_hbm(value):
    return pltpu.with_memory_space_constraint(value, pltpu.HBM)


def wide(value):
    return value.astype(jnp.float32)


def local(inputs, targets, enc_weight, encoder_layer_bias, dec_self, dec_cross, dec_bias):
    layer = lax.axis_index("layer")
    lat = lax.axis_index("latent")
    n_lat = lax.axis_size("latent")
    n_tok = lax.axis_size("token")
    x_own = in_hbm(inputs[0])
    rows, model = x_own.shape
    enc_w = in_hbm(enc_weight[0])
    own_w = in_hbm(dec_self[0])
    cross_w = in_hbm(dec_cross)
    lat_dev = enc_w.shape[1]
    width = dec_bias.shape[1]
    side = lat % 2

    edge = rows // 4 // 16 * 16
    square, x_held = square_sum(x_own)
    square = sum_over(square, "token")
    scale = jnp.sqrt(square / (rows * n_tok * model) + 1e-06)
    inv = 1.0 / scale
    outer = cut(x_held, (side * (rows - edge)).astype(jnp.int32), edge, square)
    bias = lax.dynamic_slice_in_dim(
        encoder_layer_bias, lax.axis_index("token") * lat_dev, lat_dev, axis=1
    )

    group = n_lat // 4
    other, mine_bit = 1 - lat % 2, lat % 2
    far, near = 1 - (lat // 2) % 2, (lat // 2) % 2

    def info(low, highs):
        blocks = [4 * i + 2 * high + low for high in highs for i in range(group)]
        return jnp.stack([layer] + blocks).astype(jnp.int32)

    middle = rows * 13 // 24 // 16 * 16
    first = (rows - middle) // 2 // 16 * 16
    last = first + middle
    narrow = jnp.bfloat16

    def earlier_of(codes):
        return [lax.ppermute(part, "layer", [(0, 1)]) for part in codes]

    def places(*rows):
        return jnp.stack([jnp.int32(row) for row in rows])

    def products(codes, earlier, info, outs, also):
        return decode(codes, earlier, own_w, cross_w, info, outs, width, also)

    def finish(total):
        bit = 4
        while bit < n_lat:
            here = (lat // bit) % 2
            pairs = total.reshape(total.shape[0] // 2, 2, *total.shape[1:])
            away = lax.dynamic_index_in_dim(pairs, 1 - here, 1, keepdims=False)
            arrived = swapped(away.astype(narrow), "latent", bit)
            total = lax.dynamic_index_in_dim(pairs, here, 1, keepdims=False) + wide(arrived)
            bit *= 2
        return total[0]

    codes = encode([(x_held, 0, rows)], places(0), inv, enc_w, bias, 2, [])
    inner = cut(x_held, jnp.int32(edge), rows - 2 * edge, codes[0])
    foreign = []
    for distance in range(1, n_tok):
        mine = shifted(outer, "token", distance)
        theirs = swapped(mine, "latent", 1)
        foreign.append((n_tok - distance, mine, theirs, shifted(inner, "token", distance)))
    earlier = earlier_of(codes)
    inside = ((first, middle),)
    outside = ((0, first), (last, rows - last))
    spans = [(0, group, inside), (group, group, inside), (0, group, outside), (group, group, outside)]
    far_sent, near_sent, far_out_sent, near_out_sent = products(
        codes, earlier, info(other, (far, near)),
        [span + (dtype,) for span, dtype in zip(spans, (narrow, narrow, jnp.float32, jnp.float32))], [])
    far_in = swapped(far_sent, "latent", 1)
    near_in = swapped(near_sent, "latent", 1)
    far_kept, near_kept, far_out_kept, near_out_kept = products(
        codes, earlier, info(mine_bit, (far, near)), [span + (jnp.float32,) for span in spans], [far_sent])
    across_in = (far_kept + wide(far_in)).astype(narrow)
    across_there = swapped(across_in, "latent", 2)
    own_terms = [near_kept, near_in, across_there]

    after = across_in
    returned = []
    far_out_back, near_out_back, near_out_kept_back = [], [], []

    def joined(own, back):
        return own + sum(wide(part) for part in back)

    for back, mine, theirs, inner_rows in foreign:
        codes = encode(
            [(mine, 0, edge), (theirs, 0, edge), (inner_rows, 0, rows - 2 * edge)],
            places(side * (rows - edge), (1 - side) * (rows - edge), edge),
            inv, enc_w, bias, 1, [after])
        earlier = earlier_of(codes)

        def quarter_of(low, high, spans, dtype, also):
            *insides, outer = products(
                codes, earlier, info(low, (high,)),
                [(0, group, span, dtype) for span in spans] + [(0, group, outside, narrow)], also)
            return insides, shifted(outer, "token", back)

        (far_sent,), far_back = quarter_of(other, far, [inside], narrow, [])
        far_in = swapped(far_sent, "latent", 1)
        halves = [inside]
        near_sent, near_back = quarter_of(other, near, halves, narrow, [far_sent])
        near_in = [swapped(rows_in, "latent", 1) for rows_in in near_sent]
        near_in = jnp.concatenate(near_in, axis=1) if len(near_in) > 1 else near_in[0]
        far_out_back.append(far_back)
        pins = list(near_sent)
        if not returned:
            total_in = summed(own_terms, near_sent)
            pins.append(total_in)
        if len(far_out_back) == n_tok - 1:
            pins.append(joined(far_out_sent, far_out_back).astype(narrow))
            far_out = swapped(pins[-1], "latent", 1)
        (far_kept,), far_kept_back = quarter_of(mine_bit, far, [inside], jnp.float32, pins)
        pins = [(far_kept + wide(far_in)).astype(narrow)]
        across = swapped(pins[0], "latent", 2)
        far_out_kept = far_out_kept + wide(far_kept_back)
        if len(far_out_back) == n_tok - 1:
            far_out_kept = (far_out_kept + wide(far_out)).astype(narrow)

        (near_kept,), near_kept_back = quarter_of(mine_bit, near, [inside], jnp.float32, pins)
        part = finish(near_kept + wide(near_in) + wide(across))
        returned.append(shifted(part.astype(narrow), "token", back))
        near_out_back.append(near_back)
        near_out_kept_back.append(near_kept_back)
        after = near_kept

    near_out = swapped(joined(near_out_sent, near_out_back).astype(narrow), "latent", 1)
    across_out = swapped(far_out_kept, "latent", 2)
    if group == 1:
        outer_terms = [near_out_kept, *near_out_kept_back, near_out, across_out]
        outer_terms = [term[0] for term in outer_terms]
    else:
        outer_terms = [finish(joined(near_out_kept, near_out_kept_back) + wide(near_out) + wide(across_out))]
    recon, sums = finale(outer_terms, [finish(total_in), *returned], first, dec_bias, targets[0], layer)

    sums = sum_over(sums, ("token", "layer"))
    loss = mean_ratio([sums] + [shifted(sums, "latent", d) for d in range(1, n_lat)])
    return (recon[None], loss)


def solution(mesh):
    return jax.shard_map(
        local,
        mesh=mesh,
        in_specs=(
            P("layer", ("groups", "token"), None),
            P("layer", ("groups", "token"), "latent"),
            P("layer", None, ("latent", "token")),
            P("layer", "latent"),
            P("layer", ("latent", "token"), None),
            P(("latent", "token"), None),
            P("layer", "latent"),
        ),
        out_specs=(P("layer", ("groups", "token"), "latent"), P("groups")),
        check_vma=False,
    )
```

```python
import jax
import jax.numpy as jnp
from jax import lax
from jax.experimental import pallas as pl
from jax.experimental.pallas import tpu as pltpu
from jax.sharding import PartitionSpec as P

VMEM_LIMIT = 28 * 1024 * 1024
ENCODE_TILE, ENCODE_SLOTS = 512, 3
DECODE_TILE, DECODE_SLOTS = 256, 6
COST = pl.CostEstimate(flops=0, bytes_accessed=0, transcendentals=0)


def tile_of(size, most):
    tile = min(size, most)
    while size % tile:
        tile //= 2
    return tile


def square_sum(x):
    rows, width = x.shape
    lanes = tile_of(width, 1024)
    loads = 4
    piece = rows // loads

    def body(x_ref, o_ref, held, sem):
        def load(i):
            place = pl.ds(i * piece, piece)
            return pltpu.make_async_copy(x_ref.at[place], held.at[place], sem.at[i])

        for i in range(loads):
            load(i).start()
        total = jnp.zeros((8, lanes), jnp.float32)
        for i in range(loads):
            load(i).wait()
            for c in range(width // lanes):
                def add(r, acc):
                    here = pl.ds(pl.multiple_of(i * piece + r * 16, 16), 16)
                    value = held[here, c * lanes:(c + 1) * lanes].astype(jnp.float32)
                    value = value * value
                    return acc + value[:8] + value[8:]

                total = lax.fori_loop(0, piece // 16, add, total, unroll=2)
        o_ref[0] = jnp.sum(total)

    return pl.pallas_call(
        body,
        in_specs=[pl.BlockSpec(memory_space=pl.ANY)],
        out_specs=[pl.BlockSpec(memory_space=pltpu.SMEM), pl.BlockSpec(memory_space=pltpu.VMEM)],
        out_shape=[jax.ShapeDtypeStruct((1,), jnp.float32), pltpu.VMEM((rows, width), x.dtype)],
        scratch_shapes=[pltpu.SemaphoreType.DMA((loads,))],
        compiler_params=pltpu.CompilerParams(vmem_limit_bytes=VMEM_LIMIT),
        cost_estimate=COST,
        name="square_sum",
    )(x)


def cut(x, first, count, after):
    width = x.shape[1]

    def body(first_ref, x_ref, after_ref, o_ref, sem):
        place = pl.ds(pl.multiple_of(first_ref[0], 16), count)
        copy = pltpu.make_async_copy(x_ref.at[place], o_ref, sem)
        copy.start()
        copy.wait()

    return pl.pallas_call(
        body,
        in_specs=[
            pl.BlockSpec(memory_space=pltpu.SMEM),
            pl.BlockSpec(memory_space=pltpu.VMEM),
            pl.BlockSpec(memory_space=pl.ANY),
        ],
        out_specs=pl.BlockSpec(memory_space=pl.ANY),
        out_shape=pltpu.HBM((count, width), x.dtype),
        scratch_shapes=[pltpu.SemaphoreType.DMA],
        compiler_params=pltpu.CompilerParams(vmem_limit_bytes=VMEM_LIMIT),
        cost_estimate=COST,
        name="cut",
    )(first.reshape(1), pltpu.with_memory_space_constraint(x, pltpu.VMEM), after)


def ring_loop(count, slots, start, step):
    for t in range(min(slots, count)):
        start(t, t)

    def turn(t, carry):
        slot = lax.rem(t, slots)
        step(t, slot)

        @pl.when(t + slots < count)
        def _():
            start(t + slots, slot)

        return carry

    lax.fori_loop(0, count, turn, 0)


def encode(pieces, places, inv, weight, bias, parts, also):
    rows, width = sum(piece[2] for piece in pieces), pieces[0][0].shape[1]
    latents = weight.shape[1]
    part = latents // parts
    tile = tile_of(part, ENCODE_TILE)
    n, m = len(pieces), len(also)

    def body(places_ref, inv_ref, b_ref, *refs):
        x_refs, w_ref = refs[:n], refs[n]
        o_refs = refs[n + 1 + m:n + 1 + m + parts]
        lhs, ring, lhs_sem, ring_sem = refs[n + 1 + m + parts:]

        def lhs_copy(i):
            _, first, count = pieces[i]
            place = pl.ds(pl.multiple_of(places_ref[i], 16), count)
            return pltpu.make_async_copy(
                x_refs[i].at[pl.ds(first, count)], lhs.at[place], lhs_sem.at[i])

        def columns(t):
            return pl.ds(pl.multiple_of(t * tile, tile), tile)

        def tile_copy(t, slot):
            return pltpu.make_async_copy(w_ref.at[:, columns(t)], ring.at[slot], ring_sem.at[slot])

        for i in range(n):
            lhs_copy(i).start()

        def step(t, slot):
            @pl.when(t == 0)
            def _():
                for i in range(n):
                    lhs_copy(i).wait()

            tile_copy(t, slot).wait()
            value = jnp.dot(lhs[...], ring[slot], preferred_element_type=jnp.float32)
            value = value * inv_ref[0] + b_ref[:, columns(t)].astype(jnp.float32)
            value = jnp.maximum(value, 0.0).astype(jnp.bfloat16)
            per = part // tile
            for i, o_ref in enumerate(o_refs):
                @pl.when(lax.div(t, per) == i)
                def _():
                    o_ref[:, columns(lax.rem(t, per))] = value

        ring_loop(latents // tile, ENCODE_SLOTS, lambda t, slot: tile_copy(t, slot).start(), step)

    return pl.pallas_call(
        body,
        in_specs=[
            pl.BlockSpec(memory_space=pltpu.SMEM),
            pl.BlockSpec(memory_space=pltpu.SMEM),
            pl.BlockSpec(memory_space=pltpu.VMEM),
        ] + [pl.BlockSpec(memory_space=pl.ANY)] * (n + 1 + m),
        out_specs=[pl.BlockSpec(memory_space=pltpu.VMEM)] * parts,
        out_shape=[jax.ShapeDtypeStruct((rows, part), jnp.bfloat16)] * parts,
        scratch_shapes=[
            pltpu.VMEM((rows, width), jnp.bfloat16),
            pltpu.VMEM((ENCODE_SLOTS, width, tile), jnp.bfloat16),
            pltpu.SemaphoreType.DMA((n,)),
            pltpu.SemaphoreType.DMA((ENCODE_SLOTS,)),
        ],
        compiler_params=pltpu.CompilerParams(vmem_limit_bytes=VMEM_LIMIT),
        cost_estimate=COST,
        name="encode",
    )(places, inv, bias, *[piece[0] for piece in pieces], weight, *also)


def decode(codes, earlier, own_w, cross_w, info, outs, width, also):
    parts = len(codes)
    rows, part = codes[0].shape
    latents = parts * part
    tile = tile_of(width, DECODE_TILE)
    per = width // tile
    blocks = info.shape[0] - 1
    m = len(also)

    def body(info_ref, *refs):
        code_refs, (s_ref, x_ref), refs = refs[:2 * parts], refs[2 * parts:2 * parts + 2], refs[2 * parts + 2:]
        o_refs = refs[m:m + len(outs)]
        lhs, ring, lhs_sem, ring_sem = refs[m + len(outs):]
        later = info_ref[0] != 0

        def lhs_copy(i):
            return pltpu.make_async_copy(
                code_refs[i], lhs.at[:, pl.ds(i * part, part)], lhs_sem.at[i])

        def tile_copy(source, i, t, slot):
            column = info_ref[1 + lax.div(t, per)] * width + lax.rem(t, per) * tile
            across = pl.ds(pl.multiple_of(column, tile), tile)
            return pltpu.make_async_copy(
                source.at[:, across], ring.at[slot, pl.ds(i * latents, latents)], ring_sem.at[slot, i])

        def start(t, slot):
            t = jnp.int32(t)
            tile_copy(s_ref, 0, t, slot).start()

            @pl.when(later)
            def _():
                tile_copy(x_ref, 1, t, slot).start()

        for i in range(parts):
            lhs_copy(i).start()

        @pl.when(later)
        def _():
            for i in range(parts, 2 * parts):
                lhs_copy(i).start()

        def put(t, value):
            b = lax.div(t, per)
            across = pl.ds(pl.multiple_of(lax.rem(t, per) * tile, tile), tile)
            for (block, many, spans, dtype), o_ref in zip(outs, o_refs):
                @pl.when((b >= block) & (b < block + many))
                def _():
                    here = jnp.clip(b - block, 0, many - 1)
                    at = 0
                    for row, height in spans:
                        o_ref[here, at:at + height, across] = value[row:row + height].astype(dtype)
                        at += height

        def step(t, slot):
            @pl.when(t == 0)
            def _():
                for i in range(parts):
                    lhs_copy(i).wait()

            tile_copy(s_ref, 0, t, slot).wait()

            @pl.when(later)
            def _():
                @pl.when(t == 0)
                def _():
                    for i in range(parts, 2 * parts):
                        lhs_copy(i).wait()

                tile_copy(x_ref, 1, t, slot).wait()
                put(t, jnp.dot(lhs[...], ring[slot], preferred_element_type=jnp.float32))

            @pl.when(jnp.logical_not(later))
            def _():
                put(t, jnp.dot(
                    lhs[:, :latents], ring[slot, :latents], preferred_element_type=jnp.float32))

        ring_loop(blocks * per, DECODE_SLOTS, start, step)

    return pl.pallas_call(
        body,
        in_specs=[pl.BlockSpec(memory_space=pltpu.SMEM)]
        + [pl.BlockSpec(memory_space=pl.ANY)] * (2 * parts + 2 + m),
        out_specs=[pl.BlockSpec(memory_space=pltpu.VMEM)] * len(outs),
        out_shape=[
            jax.ShapeDtypeStruct((many, sum(height for _, height in spans), width), dtype)
            for _, many, spans, dtype in outs
        ],
        scratch_shapes=[
            pltpu.VMEM((rows, 2 * latents), jnp.bfloat16),
            pltpu.VMEM((DECODE_SLOTS, 2 * latents, tile), jnp.bfloat16),
            pltpu.SemaphoreType.DMA((2 * parts,)),
            pltpu.SemaphoreType.DMA((DECODE_SLOTS, 2)),
        ],
        compiler_params=pltpu.CompilerParams(vmem_limit_bytes=VMEM_LIMIT),
        cost_estimate=COST,
        name="decode",
    )(info, *codes, *earlier, own_w, cross_w, *also)


def finale(outer_terms, inner_terms, first, bias, target, layer):
    rows, width = target.shape
    middle = inner_terms[0].shape[0]
    last = first + middle
    n, m = len(outer_terms), len(inner_terms)

    def body(layer_ref, b_ref, t_ref, *refs):
        terms = {0: refs[:n], 1: refs[n:n + m]}
        r_ref, s_ref = refs[n + m:]
        bias = b_ref[...].astype(jnp.float32)
        spans = [(0, 0, 0, first), (1, 0, first, middle), (0, first, last, rows - last)]

        def block(which, start, target_start):
            def run(r, sums):
                here = pl.ds(pl.multiple_of(start + r * 16, 16), 16)
                there = pl.ds(pl.multiple_of(target_start + r * 16, 16), 16)
                total = sum(term[here, :].astype(jnp.float32) for term in terms[which]) + bias
                goal = t_ref[there, :].astype(jnp.float32)
                r_ref[there, :] = total.astype(r_ref.dtype)
                diff = total - goal
                diff, goal = diff * diff, goal * goal
                return sums[0] + diff[:8] + diff[8:], sums[1] + goal[:8] + goal[8:]

            return run

        zero = jnp.zeros((8, width), jnp.float32)
        sums = (zero, zero)
        for which, start, target_start, count in spans:
            sums = lax.fori_loop(0, count // 16, block(which, start, target_start), sums)
        row = lax.broadcasted_iota(jnp.int32, (8, 128), 0)
        value = jnp.where(row == layer_ref[0], jnp.sum(sums[0]), 0.0)
        s_ref[...] = jnp.where(row == layer_ref[0] + 2, jnp.sum(sums[1]), value)

    vmem = pl.BlockSpec(memory_space=pltpu.VMEM)
    return pl.pallas_call(
        body,
        in_specs=[pl.BlockSpec(memory_space=pltpu.SMEM)] + [vmem] * (2 + n + m),
        out_specs=[vmem] * 2,
        out_shape=[
            jax.ShapeDtypeStruct((rows, width), jnp.bfloat16),
            jax.ShapeDtypeStruct((8, 128), jnp.float32),
        ],
        compiler_params=pltpu.CompilerParams(vmem_limit_bytes=VMEM_LIMIT),
        cost_estimate=COST,
        name="finale",
    )(layer.astype(jnp.int32).reshape(1), bias, target, *outer_terms, *inner_terms)


def summed(terms, also):
    n = len(terms)
    shape = terms[0].shape

    def body(*refs):
        o_ref = refs[-1]

        def block(r, carry):
            here = pl.ds(pl.multiple_of(r * 16, 16), 16)
            for g in range(shape[0]):
                o_ref[g, here, :] = sum(ref[g, here, :].astype(jnp.float32) for ref in refs[:n])
            return carry

        lax.fori_loop(0, shape[1] // 16, block, 0)

    vmem = pl.BlockSpec(memory_space=pltpu.VMEM)
    return pl.pallas_call(
        body,
        in_specs=[vmem] * n + [pl.BlockSpec(memory_space=pl.ANY)] * len(also),
        out_specs=vmem,
        out_shape=jax.ShapeDtypeStruct(shape, jnp.float32),
        compiler_params=pltpu.CompilerParams(vmem_limit_bytes=VMEM_LIMIT),
        cost_estimate=COST,
        name="summed",
    )(*terms, *also)


def mean_ratio(terms):
    n = len(terms)

    def body(*refs):
        total = sum(ref[...] for ref in refs[:n])
        ratio = total[0:2] / total[2:4]
        refs[n][...] = (ratio[0:1, 0:1] + ratio[1:2, 0:1]) / 2.0

    vmem = pl.BlockSpec(memory_space=pltpu.VMEM)
    return pl.pallas_call(
        body,
        in_specs=[vmem] * n,
        out_specs=vmem,
        out_shape=jax.ShapeDtypeStruct((1, 1), jnp.float32),
        cost_estimate=COST,
        name="mean_ratio",
    )(*terms).reshape(1)


def shifted(value, axis, distance):
    n = lax.axis_size(axis)
    return lax.ppermute(value, axis, [(i, (i + distance) % n) for i in range(n)])


def swapped(value, axis, bit):
    n = lax.axis_size(axis)
    return lax.ppermute(value, axis, [(i, i ^ bit) for i in range(n)])


def sum_over(value, axis):
    total = value
    for distance in range(1, lax.axis_size(axis)):
        total = total + shifted(value, axis, distance)
    return total


def in_hbm(value):
    return pltpu.with_memory_space_constraint(value, pltpu.HBM)


def wide(value):
    return value.astype(jnp.float32)


def local(inputs, targets, enc_weight, encoder_layer_bias, dec_self, dec_cross, dec_bias):
    layer = lax.axis_index("layer")
    lat = lax.axis_index("latent")
    n_lat = lax.axis_size("latent")
    n_tok = lax.axis_size("token")
    x_own = in_hbm(inputs[0])
    rows, model = x_own.shape
    enc_w = in_hbm(enc_weight[0])
    own_w = in_hbm(dec_self[0])
    cross_w = in_hbm(dec_cross)
    lat_dev = enc_w.shape[1]
    width = dec_bias.shape[1]
    side = lat % 2

    edge = rows // 4 // 16 * 16
    square, x_held = square_sum(x_own)
    square = sum_over(square, "token")
    scale = jnp.sqrt(square / (rows * n_tok * model) + 1e-06)
    inv = 1.0 / scale
    outer = cut(x_held, (side * (rows - edge)).astype(jnp.int32), edge, square)
    bias = lax.dynamic_slice_in_dim(
        encoder_layer_bias, lax.axis_index("token") * lat_dev, lat_dev, axis=1
    )

    group = n_lat // 4
    other, mine_bit = 1 - lat % 2, lat % 2
    far, near = 1 - (lat // 2) % 2, (lat // 2) % 2

    def info(low, highs):
        blocks = [4 * i + 2 * high + low for high in highs for i in range(group)]
        return jnp.stack([layer] + blocks).astype(jnp.int32)

    middle = rows * 11 // 24 // 16 * 16
    first = (rows - middle) // 2 // 16 * 16
    last = first + middle
    narrow = jnp.bfloat16

    def earlier_of(codes):
        return [lax.ppermute(part, "layer", [(0, 1)]) for part in codes]

    def places(*rows):
        return jnp.stack([jnp.int32(row) for row in rows])

    def products(codes, earlier, info, outs, also):
        return decode(codes, earlier, own_w, cross_w, info, outs, width, also)

    def finish(total):
        bit = 4
        while bit < n_lat:
            here = (lat // bit) % 2
            pairs = total.reshape(total.shape[0] // 2, 2, *total.shape[1:])
            away = lax.dynamic_index_in_dim(pairs, 1 - here, 1, keepdims=False)
            arrived = swapped(away.astype(narrow), "latent", bit)
            total = lax.dynamic_index_in_dim(pairs, here, 1, keepdims=False) + wide(arrived)
            bit *= 2
        return total[0]

    codes = encode([(x_held, 0, rows)], places(0), inv, enc_w, bias, 2, [])
    inner = cut(x_held, jnp.int32(edge), rows - 2 * edge, codes[0])
    foreign = []
    for distance in range(1, n_tok):
        mine = shifted(outer, "token", distance)
        theirs = swapped(mine, "latent", 1)
        foreign.append((n_tok - distance, mine, theirs, shifted(inner, "token", distance)))
    earlier = earlier_of(codes)
    inside = ((first, middle),)
    outside = ((0, first), (last, rows - last))
    spans = [(0, group, inside), (group, group, inside), (0, group, outside), (group, group, outside)]
    far_sent, near_sent, far_out_sent, near_out_sent = products(
        codes, earlier, info(other, (far, near)),
        [span + (dtype,) for span, dtype in zip(spans, (narrow, narrow, jnp.float32, jnp.float32))], [])
    far_in = swapped(far_sent, "latent", 1)
    near_in = swapped(near_sent, "latent", 1)
    far_kept, near_kept, far_out_kept, near_out_kept = products(
        codes, earlier, info(mine_bit, (far, near)), [span + (jnp.float32,) for span in spans], [far_sent])
    across_in = (far_kept + wide(far_in)).astype(narrow)
    across_there = swapped(across_in, "latent", 2)
    own_terms = [near_kept, near_in, across_there]

    after = across_in
    returned = []
    far_out_back, near_out_back, near_out_kept_back = [], [], []

    def joined(own, back):
        return own + sum(wide(part) for part in back)

    for back, mine, theirs, inner_rows in foreign:
        codes = encode(
            [(mine, 0, edge), (theirs, 0, edge), (inner_rows, 0, rows - 2 * edge)],
            places(side * (rows - edge), (1 - side) * (rows - edge), edge),
            inv, enc_w, bias, 1, [after])
        earlier = earlier_of(codes)

        def quarter_of(low, high, spans, dtype, also):
            *insides, outer = products(
                codes, earlier, info(low, (high,)),
                [(0, group, span, dtype) for span in spans] + [(0, group, outside, narrow)], also)
            return insides, shifted(outer, "token", back)

        (far_sent,), far_back = quarter_of(other, far, [inside], narrow, [])
        far_in = swapped(far_sent, "latent", 1)
        halves = [inside]
        near_sent, near_back = quarter_of(other, near, halves, narrow, [far_sent])
        near_in = [swapped(rows_in, "latent", 1) for rows_in in near_sent]
        near_in = jnp.concatenate(near_in, axis=1) if len(near_in) > 1 else near_in[0]
        far_out_back.append(far_back)
        pins = list(near_sent)
        if not returned:
            total_in = summed(own_terms, near_sent)
            pins.append(total_in)
        if len(far_out_back) == n_tok - 1:
            pins.append(joined(far_out_sent, far_out_back).astype(narrow))
            far_out = swapped(pins[-1], "latent", 1)
        (far_kept,), far_kept_back = quarter_of(mine_bit, far, [inside], jnp.float32, pins)
        pins = [(far_kept + wide(far_in)).astype(narrow)]
        across = swapped(pins[0], "latent", 2)
        far_out_kept = far_out_kept + wide(far_kept_back)
        if len(far_out_back) == n_tok - 1:
            far_out_kept = (far_out_kept + wide(far_out)).astype(narrow)

        (near_kept,), near_kept_back = quarter_of(mine_bit, near, [inside], jnp.float32, pins)
        part = finish(near_kept + wide(near_in) + wide(across))
        returned.append(shifted(part.astype(narrow), "token", back))
        near_out_back.append(near_back)
        near_out_kept_back.append(near_kept_back)
        after = near_kept

    near_out = swapped(joined(near_out_sent, near_out_back).astype(narrow), "latent", 1)
    across_out = swapped(far_out_kept, "latent", 2)
    if group == 1:
        outer_terms = [near_out_kept, *near_out_kept_back, near_out, across_out]
        outer_terms = [term[0] for term in outer_terms]
    else:
        outer_terms = [finish(joined(near_out_kept, near_out_kept_back) + wide(near_out) + wide(across_out))]
    recon, sums = finale(outer_terms, [finish(total_in), *returned], first, dec_bias, targets[0], layer)

    sums = sum_over(sums, ("token", "layer"))
    loss = mean_ratio([sums] + [shifted(sums, "latent", d) for d in range(1, n_lat)])
    return (recon[None], loss)


def solution(mesh):
    return jax.shard_map(
        local,
        mesh=mesh,
        in_specs=(
            P("layer", ("groups", "token"), None),
            P("layer", ("groups", "token"), "latent"),
            P("layer", None, ("latent", "token")),
            P("layer", "latent"),
            P("layer", ("latent", "token"), None),
            P(("latent", "token"), None),
            P("layer", "latent"),
        ),
        out_specs=(P("layer", ("groups", "token"), "latent"), P("groups")),
        check_vma=False,
    )
```
